256 devices in a mesh: axial: 16 (over z, core), azim: 16 (over y, x).
Axes of the slice: x: 4, y: 4, z: 8, core: 2. Of those that a mesh axis runs over, the one named last changes fastest.
Arguments:
- stored: bfloat16 [4, 16, 16, 16, 2, 8, 2048], P(None, 'axial', 'azim'), may hold values from -4 to 4, as said below
- holder: int32 [4, 16, 16], replicated, may hold values from 0 to 31, as said below
- seed_temp: float32 [64, 1024, 128], P('axial', 'azim'), may hold values from -6 to 6
- seed_disloc: float32 [64, 1024, 128], P('axial', 'azim'), may hold values from -6 to 6
- decay_length: float32 [1024, 128], P('azim'), may hold values from 12 to 256
- face_radius: int32 [64, 1024], P('axial', 'azim'), may hold values from 64 to 127
- kernel: float32 [17], replicated, may hold values from 0.1 to 1
Outputs:
- adj_temp: float32 [64, 1024, 128], P('axial', 'azim')
- adj_disloc: float32 [64, 1024, 128], P('axial', 'azim')
- heater_grad: float32 [64, 1024], P('axial', 'azim')
The draws below stay inside these ranges and needn't reach their ends.
Inputs may be any that keep to these rules, and one draw needn't show every extreme that they name: holder[k, o, j] = 2 p + c says that piece j of the checkpoint of axial index o for step k is in slot c of axial peer p; every slot holds at most one piece; per owner and step, about a quarter of the peers hold 2 pieces and some hold none. `stored`: slots that hold no piece are zero.
All inputs are finite; a program needn't handle non-finite values.
Results may differ from the reference program's by a relative error of at most 0.0003.
Values may be sent and summed in bfloat16 or wider, within the bound.
No kernel may reach another device: no remote copies, remote signals or barrier semaphores. Data moves between devices by JAX's collectives and lax.ppermute only.
A program may use at most 64 MiB of HBM per device.

```python
import math
import jax
import jax.numpy as jnp
import numpy as np
from jax import lax

AXC = 4
AZC = 64
RAD = 128
STEPS = 4
CAP = 2
BAND = 8
PEERS = 16
SECTORS = 16
NZ = 64
NAZ = 1024
PIECE = 2048


def plan(key):
    heavy = max(1, PEERS // 4)
    loads = [2] * heavy + [1] * (PEERS - 2 * heavy) + [0] * heavy
    ranks = np.repeat(np.arange(PEERS), loads).astype(np.int32)
    slots = np.concatenate([np.arange(count) for count in loads]).astype(np.int32)
    keys = jax.random.split(jax.random.fold_in(key, 11), STEPS * PEERS)

    def single(subkey):
        first, second = jax.random.split(subkey)
        peers = jax.random.permutation(first, PEERS).astype(jnp.int32)
        pieces = jax.random.permutation(second, PEERS).astype(jnp.int32)
        place = peers[ranks] * CAP + slots
        holding = jnp.zeros((PEERS,), jnp.int32).at[pieces].set(place)
        filled = jnp.zeros((PEERS, CAP), jnp.float32).at[peers[ranks], slots].set(1.0)
        return (holding, filled)
    holding, filled = jax.vmap(single)(keys)
    holding = holding.reshape(STEPS, PEERS, PEERS)
    filled = jnp.transpose(filled.reshape(STEPS, PEERS, PEERS, CAP), (0, 2, 1, 3))
    return (holding, filled)


def draw_holder(key, part):
    holding, filled = plan(key)
    return holding


def draw_stored(key, part):
    holding, filled = plan(key)
    key = jax.random.fold_in(key, 5)
    shape = (STEPS, PEERS, SECTORS, PEERS, CAP, 8, PIECE)
    values = jnp.clip(jax.random.normal(key, shape, jnp.float32), -4.0, 4.0)
    values = values * filled[:, :, None, :, :, None, None]
    return values.astype(jnp.bfloat16)


def with_ends(array, rng, low, top_value):
    dims = array.shape
    index_at = [jax.random.randint(jax.random.fold_in(rng, axis), (), 0, dims[axis]) for axis in range(len(dims))]
    array = array.at[tuple(index_at)].set(low)
    longest = dims.index(max(dims))
    index_at[longest] = (index_at[longest] + 1) % dims[longest]
    return array.at[tuple(index_at)].set(top_value)


def shard_levels(stream_key, extent, cuts, least, top_value):
    def one(dim, shards_of):
        draws = jax.random.uniform(jax.random.fold_in(jax.random.fold_in(stream_key, 6), dim), (shards_of,), jnp.float32, least / len(cuts), top_value / len(cuts))
        return jnp.repeat(jnp.exp(draws), extent[dim] // shards_of).reshape((-1,) + (1,) * (len(extent) - dim - 1))

    factor_of = one(*cuts[0])
    for cut in cuts[1:]:
        factor_of = factor_of * one(*cut)
    return factor_of


def centred(stream_key, extent, scale, reach, cuts=(), kind=jnp.bfloat16):
    gain = shard_levels(stream_key, extent, cuts, -0.22, 0.18) if cuts else 1.0
    array = jax.random.normal(stream_key, extent, jnp.float32) * scale * gain
    return jnp.minimum(jnp.maximum(array, -reach), reach).astype(kind)


def setup_inputs(seed: int = 0) -> dict:
    streams_of = jax.random.split(jax.random.key(seed), 8)
    stored = draw_stored(jax.random.fold_in(streams_of[7], 71), 0)
    holder = draw_holder(jax.random.fold_in(streams_of[7], 71), 0)
    seed_temp = centred(streams_of[2], (NZ, NAZ, RAD), 1.0, 6.0, ((0, 16), (1, 16)), jnp.float32)
    seed_disloc = centred(streams_of[3], (NZ, NAZ, RAD), 1.0, 6.0, ((0, 16), (1, 16)), jnp.float32)
    decay_length = jnp.clip(jnp.exp(math.log(256.0) - 3.0602708 * jax.random.uniform(streams_of[4], (NAZ, RAD), jnp.float32) ** shard_levels(streams_of[4], (NAZ, RAD), ((0, 16),), -0.2, 0.2)), 12.0, 256.0)
    face_radius = with_ends(jax.random.randint(streams_of[5], (NZ, NAZ), RAD // 2, RAD), jax.random.fold_in(streams_of[5], 1), RAD // 2, RAD - 1).astype(jnp.int32)
    kernel = jnp.clip(jax.random.uniform(streams_of[6], (2 * BAND + 1,), jnp.float32, 0.1, 1.0), 0.1, 1.0)
    return {"stored": stored, "holder": holder, "seed_temp": seed_temp, "seed_disloc": seed_disloc, "decay_length": decay_length, "face_radius": face_radius, "kernel": kernel}


def assemble(stored_step, holder_step):
    peer_index = holder_step // CAP
    slot_index = holder_step % CAP
    owner_index = jnp.arange(PEERS, dtype=jnp.int32)[:, None]
    pieces = stored_step[peer_index, :, owner_index, slot_index]
    pieces = jnp.transpose(pieces, (3, 0, 2, 1, 4))
    cells = pieces.reshape(8, PEERS, SECTORS, AXC, AZC, RAD)
    cells = jnp.transpose(cells, (0, 1, 3, 2, 4, 5)).reshape(8, NZ, NAZ, RAD)
    return cells.astype(jnp.float32)

def laplace(field):
    axial_pad = jnp.pad(field, ((1, 1), (0, 0), (0, 0)))
    radial_pad = jnp.pad(field, ((0, 0), (0, 0), (1, 1)))
    total = axial_pad[2:] + axial_pad[:-2]
    total = total + jnp.roll(field, 1, axis=1) + jnp.roll(field, -1, axis=1)
    total = total + radial_pad[:, :, 2:] + radial_pad[:, :, :-2]
    return total - 6.0 * field

def reference(stored, holder, seed_temp, seed_disloc, decay_length, face_radius, kernel):
    decay = jnp.exp(-1.0 / decay_length)
    radial = lax.broadcasted_iota(jnp.int32, (NZ, NAZ, RAD), 2)
    face_mask = (radial == face_radius[:, :, None]).astype(jnp.float32)
    adj_temp, adj_disloc = (seed_temp, seed_disloc)
    flux = jnp.zeros((NZ, NAZ), jnp.float32)

    def glide(carry, layer):
        return (decay * carry + (1.0 - decay) * layer, carry)
    for step in reversed(range(STEPS)):
        state = assemble(stored[step], holder[step])
        theta, rho = (state[0], state[7])
        flux = flux + lax.optimization_barrier(jnp.sum(adj_temp * face_mask, axis=2))
        stress = jnp.sqrt(1.0 + lax.optimization_barrier(jnp.sum(state[1:7] * state[1:7], axis=0)) / 6.0)
        slope = jnp.tanh(theta)
        rate = stress * jnp.exp(0.5 * slope)
        _, chain = lax.scan(glide, jnp.zeros((NAZ, RAD), jnp.float32), adj_disloc, reverse=True)
        new_temp = adj_temp + 0.15 * laplace(adj_temp) + 0.2 * rho * rate * 0.5 * (1.0 - slope * slope) * adj_disloc
        new_disloc = -0.3 * adj_temp + (1.0 + 0.2 * rate) * adj_disloc + chain
        adj_temp, adj_disloc = (new_temp, new_disloc)
    heater_grad = jnp.zeros((NZ, NAZ), jnp.float32)
    for offset in range(-BAND, BAND + 1):
        heater_grad = heater_grad + kernel[offset + BAND] * jnp.roll(flux, -offset, axis=1)
    return (adj_temp, adj_disloc, heater_grad)
```

```python
import functools

import jax
import jax.numpy as jnp
from jax import lax
from jax.experimental import pallas as pl
from jax.experimental.pallas import tpu as pltpu
from jax.sharding import PartitionSpec as P

ROWS = 16
LANES = 128
RATE_MID = 3.7
RATE_SCALE = 10500.0
COEF_SCALE = 1374.0
COEF_BASE = 23.0
VMEM_LIMIT = 48 * 1024 * 1024


def encode_body(stored_ref, out_ref, mixed):
    slots = stored_ref.shape[1]
    cap = out_ref.shape[2]
    for slot in range(slots):
        for row in range(ROWS):
            mixed[slot, 8 * row : 8 * row + 8, :] = stored_ref[
                0, slot, :, LANES * row : LANES * (row + 1)
            ].astype(jnp.float32)
    for slot in range(slots):

        def part(index):
            return mixed[slot, pl.ds(index, ROWS, stride=8), :]

        squares = part(1) * part(1)
        for index in range(2, 7):
            squares = squares + part(index) * part(index)
        slope = jnp.tanh(part(0))
        rate = jnp.sqrt(1.0 + squares / 6.0) * jnp.exp(0.5 * slope)
        coef = 0.1 * part(7) * rate * (1.0 - slope * slope)
        size = jnp.log2(jnp.maximum(jnp.abs(coef), 2.0 ** -(COEF_BASE + 1.0)))
        size = jnp.maximum(jnp.round((size + COEF_BASE) * COEF_SCALE), 0.0)
        coef_code = jnp.where(coef < 0.0, -size, size)
        rate_code = jnp.round((rate - RATE_MID) * RATE_SCALE)
        out_ref[slot // cap, 0, slot % cap, 0] = rate_code.astype(jnp.int32).astype(jnp.int16)
        out_ref[slot // cap, 0, slot % cap, 1] = coef_code.astype(jnp.int32).astype(jnp.int16)


def encode(stored, first, count):
    steps, _, _, owners, cap, comps, cells = stored.shape
    flat = stored.reshape(steps, owners * cap, comps, cells)
    chunk = 4
    return pl.pallas_call(
        encode_body,
        grid=(count, owners // chunk),
        in_specs=[
            pl.BlockSpec((1, chunk * cap, comps, cells), lambda k, c: (first - k, c, 0, 0))
        ],
        out_specs=pl.BlockSpec(
            (chunk, 1, cap, 2, ROWS, LANES), lambda k, c: (c, k, 0, 0, 0, 0)
        ),
        out_shape=jax.ShapeDtypeStruct((owners, count, cap, 2, ROWS, LANES), jnp.int16),
        scratch_shapes=[pltpu.VMEM((chunk * cap, 8 * ROWS, LANES), jnp.float32)],
        compiler_params=pltpu.CompilerParams(vmem_limit_bytes=VMEM_LIMIT),
    )(flat)


def decoded(info_ref, rec_ref, step, place, layer, field):
    pieces = []
    for quarter in range(4):
        held = info_ref[16 * step + 4 * layer + quarter]
        code = rec_ref[held // 2, place, held % 2, field].astype(jnp.int32).astype(jnp.float32)
        if field == 0:
            pieces.append(code * (1.0 / RATE_SCALE) + RATE_MID)
        else:
            size = jnp.exp2(jnp.abs(code) * (1.0 / COEF_SCALE) - COEF_BASE)
            pieces.append(jnp.where(code > 0.0, size, jnp.where(code < 0.0, -size, 0.0)))
    return jnp.concatenate(pieces, axis=0)


def laplace(field, low, high, left, right):
    layers = len(field)
    azimuths, radials = field[0].shape
    row = lax.broadcasted_iota(jnp.int32, (azimuths, radials), 0)
    lane = lax.broadcasted_iota(jnp.int32, (azimuths, radials), 1)
    out = []
    for layer in range(layers):
        x = field[layer]
        below = low if layer == 0 else field[layer - 1]
        above = high if layer == layers - 1 else field[layer + 1]
        before = jnp.where(row == 0, left[layer : layer + 1, :], pltpu.roll(x, 1, axis=0))
        after = jnp.where(
            row == azimuths - 1, right[layer : layer + 1, :], pltpu.roll(x, azimuths - 1, axis=0)
        )
        inner = jnp.where(lane == 0, 0.0, pltpu.roll(x, 1, axis=1))
        outer = jnp.where(lane == radials - 1, 0.0, pltpu.roll(x, radials - 1, axis=1))
        out.append(((below + above) + (before + after)) + (inner + outer) - 6.0 * x)
    return out


def chain(field, decay, carry):
    layers = len(field)
    out = [None] * layers
    for layer in reversed(range(layers)):
        out[layer] = carry
        carry = decay * carry + (1.0 - decay) * field[layer]
    return out, carry


def put_edges(field, low_ref, high_ref, left_ref, right_ref):
    layers = len(field)
    azimuths = field[0].shape[0]
    low_ref[...] = field[0]
    high_ref[...] = field[-1]
    for layer in range(layers):
        left_ref[layer : layer + 1, :] = field[layer][0:1, :]
        right_ref[layer : layer + 1, :] = field[layer][azimuths - 1 : azimuths, :]


def summary_body(lr_ref, length_ref, out_ref):
    decay = jnp.exp(-1.0 / length_ref[...])
    field = [lr_ref[layer] for layer in range(lr_ref.shape[0])]
    _, out_ref[...] = chain(field, decay, jnp.zeros_like(decay))


def first_body(
    info_ref, rec_ref, lt_ref, lr_ref, low_ref, high_ref, left_ref, right_ref, length_ref,
    sums_ref, new_lt_ref, new_lr_ref, out_ref, low_out, high_out, left_out, right_out,
):
    layers = lt_ref.shape[0]
    me = info_ref[64]
    peers = sums_ref.shape[0]
    decay = jnp.exp(-1.0 / length_ref[...])
    power = decay * decay
    power = power * power
    carry = lax.fori_loop(
        0,
        peers - 1 - me,
        lambda k, value: power * value + sums_ref[peers - 1 - k],
        jnp.zeros_like(decay),
    )
    lt = [lt_ref[layer] for layer in range(layers)]
    lr = [lr_ref[layer] for layer in range(layers)]
    spread = laplace(lt, low_ref[...], high_ref[...], left_ref[...], right_ref[...])
    new_lt = [
        lt[l] + 0.15 * spread[l] + decoded(info_ref, rec_ref, 3, 0, l, 1) * lr[l]
        for l in range(layers)
    ]
    put_edges(new_lt, low_out, high_out, left_out, right_out)
    climbs, _ = chain(lr, decay, carry)
    new_lr = [
        -0.3 * lt[l] + (1.0 + 0.2 * decoded(info_ref, rec_ref, 3, 0, l, 0)) * lr[l] + climbs[l]
        for l in range(layers)
    ]
    climbs, total = chain(new_lr, decay, jnp.zeros_like(decay))
    out_ref[0] = total
    later = [
        -0.3 * new_lt[l]
        + (1.0 + 0.2 * decoded(info_ref, rec_ref, 2, 1, l, 0)) * new_lr[l]
        + climbs[l]
        for l in range(layers)
    ]
    _, out_ref[1] = chain(later, decay, jnp.zeros_like(decay))
    for l in range(layers):
        new_lt_ref[l] = new_lt[l]
        new_lr_ref[l] = new_lr[l]


def second_body(
    info_ref, rec_ref, next_ref, lt_ref, lr_ref, low_ref, high_ref, left_ref, right_ref,
    length_ref, sums_ref, new_lt_ref, mid_lr_ref, new_lr_ref, out_ref, low_out, high_out,
    left_out, right_out,
):
    layers = lt_ref.shape[0]
    me = info_ref[64]
    peers = sums_ref.shape[0]
    decay = jnp.exp(-1.0 / length_ref[...])
    power = decay * decay
    cross = 4.0 * (1.0 - decay) * power * decay
    power = power * power

    def climb(k, values):
        one, two = values
        at = peers - 1 - k
        return (
            power * one + sums_ref[at, 0],
            power * two + (sums_ref[at, 1] + cross * one),
        )

    zero = jnp.zeros_like(decay)
    one, two = lax.fori_loop(0, peers - 1 - me, climb, (zero, zero))
    lt = [lt_ref[layer] for layer in range(layers)]
    lr = [lr_ref[layer] for layer in range(layers)]
    spread = laplace(lt, low_ref[...], high_ref[...], left_ref[...], right_ref[...])
    new_lt = [
        lt[l] + 0.15 * spread[l] + decoded(info_ref, rec_ref, 2, 1, l, 1) * lr[l]
        for l in range(layers)
    ]
    put_edges(new_lt, low_out, high_out, left_out, right_out)
    climbs, _ = chain(lr, decay, one)
    mid_lr = [
        -0.3 * lt[l] + (1.0 + 0.2 * decoded(info_ref, rec_ref, 2, 1, l, 0)) * lr[l] + climbs[l]
        for l in range(layers)
    ]
    climbs, _ = chain(mid_lr, decay, two)
    new_lr = [
        -0.3 * new_lt[l]
        + (1.0 + 0.2 * decoded(info_ref, next_ref, 1, 0, l, 0)) * mid_lr[l]
        + climbs[l]
        for l in range(layers)
    ]
    _, total = chain(new_lr, decay, zero)
    for peer in range(peers):
        out_ref[peer] = total
    for l in range(layers):
        new_lt_ref[l] = new_lt[l]
        mid_lr_ref[l] = mid_lr[l]
        new_lr_ref[l] = new_lr[l]


def third_body(
    info_ref, next_ref, lt_ref, lr_ref, low_ref, high_ref, left_ref, right_ref, old_ref,
    older_ref, face_ref, new_lt_ref, flux_ref, low_out, high_out, left_out, right_out,
):
    layers = lt_ref.shape[0]
    lt = [lt_ref[layer] for layer in range(layers)]
    spread = laplace(lt, low_ref[...], high_ref[...], left_ref[...], right_ref[...])
    new_lt = [
        lt[l] + 0.15 * spread[l] + decoded(info_ref, next_ref, 1, 0, l, 1) * lr_ref[l]
        for l in range(layers)
    ]
    put_edges(new_lt, low_out, high_out, left_out, right_out)
    for l in range(layers):
        new_lt_ref[l] = new_lt[l]
    lane = lax.broadcasted_iota(jnp.int32, lt[0].shape, 1)
    for l in range(layers):
        total = (older_ref[l] + old_ref[l]) + (lt[l] + new_lt[l])
        kept = jnp.where(lane == face_ref[l], total, 0.0)
        flux_ref[l] = jnp.sum(kept, axis=1, keepdims=True)


def last_body(
    info_ref, next_ref, lt_ref, lr_ref, low_ref, high_ref, left_ref, right_ref, length_ref,
    sums_ref, new_lt_ref, new_lr_ref,
):
    layers = lt_ref.shape[0]
    me = info_ref[64]
    peers = sums_ref.shape[0]
    decay = jnp.exp(-1.0 / length_ref[...])
    power = decay * decay
    power = power * power
    carry = lax.fori_loop(
        0,
        peers - 1 - me,
        lambda k, value: power * value + sums_ref[peers - 1 - k],
        jnp.zeros_like(decay),
    )
    lt = [lt_ref[layer] for layer in range(layers)]
    lr = [lr_ref[layer] for layer in range(layers)]
    spread = laplace(lt, low_ref[...], high_ref[...], left_ref[...], right_ref[...])
    climbs, _ = chain(lr, decay, carry)
    for l in range(layers):
        new_lt_ref[l] = (
            lt[l] + 0.15 * spread[l] + decoded(info_ref, next_ref, 0, 1, l, 1) * lr[l]
        )
        new_lr_ref[l] = (
            -0.3 * lt[l]
            + (1.0 + 0.2 * decoded(info_ref, next_ref, 0, 1, l, 0)) * lr[l]
            + climbs[l]
        )


def run(body, info, args, shapes):
    smem = pl.BlockSpec(memory_space=pltpu.SMEM)
    vmem = pl.BlockSpec(memory_space=pltpu.VMEM)
    return pl.pallas_call(
        body,
        in_specs=([smem] if info is not None else []) + [vmem] * len(args),
        out_specs=[vmem] * len(shapes),
        out_shape=[jax.ShapeDtypeStruct(shape, jnp.float32) for shape in shapes],
        compiler_params=pltpu.CompilerParams(vmem_limit_bytes=VMEM_LIMIT),
    )(*(() if info is None else (info,)), *args)


def exchanged(low, high, left, right):
    axial, azim = lax.axis_size("axial"), lax.axis_size("azim")
    up = [(i, i + 1) for i in range(axial - 1)]
    down = [(i + 1, i) for i in range(axial - 1)]
    ahead = [(i, (i + 1) % azim) for i in range(azim)]
    back = [((i + 1) % azim, i) for i in range(azim)]
    return (
        lax.ppermute(high, "axial", up),
        lax.ppermute(low, "axial", down),
        lax.ppermute(right, "azim", ahead),
        lax.ppermute(left, "azim", back),
    )


def local(stored, holder, seed_temp, seed_disloc, decay_length, face_radius, kernel):
    layers, azimuths, radials = seed_temp.shape
    peers = stored.shape[3]
    me = lax.axis_index("axial")
    wanted = lax.dynamic_index_in_dim(holder, me, 1, keepdims=False).reshape(-1)
    info = jnp.concatenate([wanted, jnp.full((16,), me, jnp.int32)])
    plane = (azimuths, radials)
    side = (layers, radials)
    block = (layers, azimuths, radials)
    edges = [plane, plane, side, side]

    early = encode(stored, 3, 2)
    early = lax.all_to_all(early, "axial", 0, 0, tiled=True)
    late = encode(stored, 1, 2)

    (total,) = run(summary_body, None, (seed_disloc, decay_length), [plane])
    sums = lax.all_gather(total, "axial")
    halo = exchanged(
        seed_temp[0], seed_temp[layers - 1], seed_temp[:, 0], seed_temp[:, azimuths - 1]
    )
    lt1, lr1, pair, *rim = run(
        first_body,
        info,
        (early, seed_temp, seed_disloc, *halo, decay_length, sums),
        [block, block, (2, *plane), *edges],
    )
    late, pair, rim = lax.optimization_barrier((late, pair, rim))
    late = lax.all_to_all(late, "axial", 0, 0, tiled=True)
    halo = exchanged(*rim)
    sums = lax.all_gather(pair, "axial")
    lt2, lr2, lr3, spread, *rim = run(
        second_body,
        info,
        (early, late, lt1, lr1, *halo, decay_length, sums),
        [block, block, block, (peers, *plane), *edges],
    )
    halo = exchanged(*rim)
    sums = lax.all_to_all(spread, "axial", 0, 0, tiled=True)
    lt3, flux, *rim = run(
        third_body,
        info,
        (late, lt2, lr2, *halo, lt1, seed_temp, face_radius[:, :, None]),
        [block, (layers, azimuths, 1), *edges],
    )
    halo = exchanged(*rim)
    flux = flux[:, :, 0]
    band = (kernel.shape[0] - 1) // 2
    azim = lax.axis_size("azim")
    before = lax.ppermute(
        flux[:, azimuths - band :], "azim", [(i, (i + 1) % azim) for i in range(azim)]
    )
    after = lax.ppermute(
        flux[:, :band], "azim", [((i + 1) % azim, i) for i in range(azim)]
    )
    adj_temp, adj_disloc = run(
        last_body, info, (late, lt3, lr3, *halo, decay_length, sums), [block, block]
    )
    padded = jnp.concatenate([before, flux, after], axis=1)
    heater_grad = jnp.zeros_like(flux)
    for offset in range(2 * band + 1):
        heater_grad = heater_grad + kernel[offset] * padded[:, offset : offset + azimuths]
    return (adj_temp, adj_disloc, heater_grad)


def solution(mesh):
    in_specs = (
        P(None, "axial", "azim", None, None, None, None),
        P(),
        P("axial", "azim", None),
        P("axial", "azim", None),
        P("azim", None),
        P("axial", "azim"),
        P(),
    )
    out_specs = (P("axial", "azim", None), P("axial", "azim", None), P("axial", "azim"))
    return jax.shard_map(local, mesh=mesh, in_specs=in_specs, out_specs=out_specs, check_vma=False)
```

```python
import jax
import jax.numpy as jnp
from jax import lax
from jax.experimental import pallas as pl
from jax.experimental.pallas import tpu as pltpu
from jax.sharding import PartitionSpec as P

ROWS = 16
LANES = 128
RATE_MID = 3.7
RATE_SCALE = 10500.0
COEF_SCALE = 1374.0
COEF_BASE = 23.0
ENCODE_VMEM = 60 * 1024 * 1024
STEP_VMEM = 16 * 1024 * 1024


def encode_body(stored_ref, out_ref):
    slots = stored_ref.shape[1]
    cap = out_ref.shape[2]
    rows = 8 * ROWS
    row = lax.broadcasted_iota(jnp.int32, (rows, rows), 0)
    column = lax.broadcasted_iota(jnp.int32, (rows, rows), 1)
    picked = (row % ROWS) * 8 + row // ROWS == column
    order = jnp.where(picked, 1.0, 0.0).astype(jnp.bfloat16)
    for slot in range(slots):
        mixed = stored_ref[0, slot].astype(jnp.float32)
        mixed = jnp.concatenate(
            [mixed[:, LANES * r : LANES * (r + 1)] for r in range(ROWS)], axis=0
        ).astype(jnp.bfloat16)
        parts = jnp.dot(order, mixed, preferred_element_type=jnp.float32)

        def part(index):
            return parts[ROWS * index : ROWS * (index + 1), :]

        squares = part(1) * part(1)
        for index in range(2, 7):
            squares = squares + part(index) * part(index)
        slope = jnp.tanh(part(0))
        rate = jnp.sqrt(1.0 + squares * (1.0 / 6.0)) * jnp.exp(0.5 * slope)
        coef = 0.1 * part(7) * rate * (1.0 - slope * slope)
        size = jnp.log2(jnp.maximum(jnp.abs(coef), 2.0 ** -(COEF_BASE + 1.0)))
        size = jnp.maximum(jnp.round((size + COEF_BASE) * COEF_SCALE), 0.0)
        coef_code = jnp.where(coef < 0.0, -size, size)
        rate_code = jnp.round((rate - RATE_MID) * RATE_SCALE)
        out_ref[slot // cap, 0, slot % cap, 0] = rate_code.astype(jnp.int32).astype(jnp.int16)
        out_ref[slot // cap, 0, slot % cap, 1] = coef_code.astype(jnp.int32).astype(jnp.int16)


def encode(stored):
    steps, _, _, owners, cap, comps, cells = stored.shape
    flat = stored.reshape(steps, owners * cap, comps, cells)
    chunk = 8
    return pl.pallas_call(
        encode_body,
        grid=(steps, owners // chunk),
        in_specs=[pl.BlockSpec((1, chunk * cap, comps, cells), lambda k, c: (k, c, 0, 0))],
        out_specs=pl.BlockSpec(
            (chunk, 1, cap, 2, ROWS, LANES), lambda k, c: (c, k, 0, 0, 0, 0)
        ),
        out_shape=jax.ShapeDtypeStruct((owners, steps, cap, 2, ROWS, LANES), jnp.int16),
        compiler_params=pltpu.CompilerParams(vmem_limit_bytes=ENCODE_VMEM),
    )(flat)


def decoded(info_ref, rec_ref, step, layer, field):
    pieces = []
    for quarter in range(4):
        held = info_ref[16 * step + 4 * layer + quarter]
        code = rec_ref[held // 2, step, held % 2, field].astype(jnp.int32).astype(jnp.float32)
        if field == 0:
            pieces.append(code * (1.0 / RATE_SCALE) + RATE_MID)
        else:
            size = jnp.exp2(jnp.abs(code) * (1.0 / COEF_SCALE) - COEF_BASE)
            pieces.append(jnp.where(code > 0.0, size, jnp.where(code < 0.0, -size, 0.0)))
    return jnp.concatenate(pieces, axis=0)


def laplace(info_ref, field, low_ref, high_ref, left_ref, right_ref):
    layers = len(field)
    low = jnp.where(info_ref[64] == 0, 0.0, low_ref[...])
    high = jnp.where(info_ref[64] == info_ref[65] - 1, 0.0, high_ref[...])
    left, right = left_ref[...], right_ref[...]
    azimuths, radials = field[0].shape
    row = lax.broadcasted_iota(jnp.int32, (azimuths, radials), 0)
    lane = lax.broadcasted_iota(jnp.int32, (azimuths, radials), 1)
    out = []
    for layer in range(layers):
        x = field[layer]
        below = low if layer == 0 else field[layer - 1]
        above = high if layer == layers - 1 else field[layer + 1]
        before = jnp.where(row == 0, left[layer : layer + 1, :], pltpu.roll(x, 1, axis=0))
        after = jnp.where(
            row == azimuths - 1, right[layer : layer + 1, :], pltpu.roll(x, azimuths - 1, axis=0)
        )
        inner = jnp.where(lane == 0, 0.0, pltpu.roll(x, 1, axis=1))
        outer = jnp.where(lane == radials - 1, 0.0, pltpu.roll(x, radials - 1, axis=1))
        out.append(((below + above) + (before + after)) + (inner + outer) - 6.0 * x)
    return out


def chain(field, decay, carry):
    layers = len(field)
    out = [None] * layers
    for layer in reversed(range(layers)):
        out[layer] = carry
        carry = decay * carry + (1.0 - decay) * field[layer]
    return out, carry


def put_edges(field, low_ref, high_ref, left_ref, right_ref):
    layers = len(field)
    azimuths = field[0].shape[0]
    low_ref[...] = field[0]
    high_ref[...] = field[-1]
    for layer in range(layers):
        left_ref[layer : layer + 1, :] = field[layer][0:1, :]
        right_ref[layer : layer + 1, :] = field[layer][azimuths - 1 : azimuths, :]


def powers(length):
    decay = jnp.exp(-1.0 / length)
    cube = decay * decay * decay
    return decay, decay * cube, 4.0 * (1.0 - decay) * cube


def applied(carry, here, fall, cross):
    out = [sums + fall * value for value, sums in zip(carry, here)]
    if len(carry) > 1:
        out[1] = out[1] + cross * carry[0]
        out[2] = out[2] + cross * carry[1] + here[3] * carry[0]
    return tuple(out)


def halves(info_ref, values, scratch, keep_ref, give_ref):
    mine = info_ref[64] % 2
    half = scratch.shape[1] // 2
    for index, value in enumerate(values):
        scratch[index] = value
    for index in range(len(values)):
        keep_ref[index] = scratch[index, pl.ds(half * mine, half), :]
        give_ref[index] = scratch[index, pl.ds(half * (1 - mine), half), :]


def restored(info_ref, mine_ref, got_ref, scratch):
    mine = info_ref[64] % 2
    half = scratch.shape[1] // 2
    count = scratch.shape[0]
    for index in range(count):
        scratch[index, pl.ds(half * mine, half), :] = mine_ref[index]
        scratch[index, pl.ds(half * (1 - mine), half), :] = got_ref[index]
    return [scratch[index] for index in range(count)]


def half_powers(info_ref, length_ref):
    half = length_ref.shape[0] // 2
    return powers(length_ref[pl.ds(half * (info_ref[64] % 2), half), :])


def cores(info_ref, keep_ref, got_ref):
    upper_here = info_ref[64] % 2 == 1
    own = [keep_ref[index] for index in range(keep_ref.shape[0])]
    other = [got_ref[index] for index in range(got_ref.shape[0])]
    upper = [jnp.where(upper_here, a, b) for a, b in zip(own, other)]
    lower = [jnp.where(upper_here, b, a) for a, b in zip(own, other)]
    return upper, lower


def chip_body(info_ref, keep_ref, got_ref, length_ref, out_ref):
    _, fall, cross = half_powers(info_ref, length_ref)
    upper, lower = cores(info_ref, keep_ref, got_ref)
    count = 3 if len(upper) > 1 else 1
    total = list(applied(upper[:count], lower, fall, cross))
    if count > 1:
        total.append(fall * (lower[3] + upper[3]) + cross * cross)
    for chip in range(out_ref.shape[0]):
        for index, value in enumerate(total):
            out_ref[chip, index] = value


def carry_body(info_ref, keep_ref, got_ref, sums_ref, length_ref, mine_ref, other_ref):
    _, fall, cross = half_powers(info_ref, length_ref)
    chips, fields = sums_ref.shape[:2]
    count = mine_ref.shape[0]

    def climb(k, total):
        at = chips - 1 - k
        here = [sums_ref[at, index] for index in range(fields)]
        return applied(total, here, fall * fall, 2.0 * fall * cross)

    zero = jnp.zeros_like(fall)
    total = lax.fori_loop(0, chips - 1 - info_ref[64] // 2, climb, (zero,) * count)
    upper, _ = cores(info_ref, keep_ref, got_ref)
    below = applied(total, upper, fall, cross)
    upper_here = info_ref[64] % 2 == 1
    for index in range(count):
        mine_ref[index] = jnp.where(upper_here, total[index], below[index])
        other_ref[index] = jnp.where(upper_here, below[index], total[index])


def first_body(
    info_ref, rec_ref, lt_ref, lr_ref, low_ref, high_ref, left_ref, right_ref, length_ref,
    new_lt_ref, keep_ref, give_ref, low_out, high_out, left_out, right_out, scratch,
):
    layers = lt_ref.shape[0]
    decay, _, _ = powers(length_ref[...])
    nothing = jnp.zeros_like(decay)
    lt = [lt_ref[layer] for layer in range(layers)]
    lr = [lr_ref[layer] for layer in range(layers)]
    climbs, now = chain(lr, decay, nothing)
    new_lr = [
        -0.3 * lt[l] + (1.0 + 0.2 * decoded(info_ref, rec_ref, 3, l, 0)) * lr[l] + climbs[l]
        for l in range(layers)
    ]
    spread = laplace(info_ref, lt, low_ref, high_ref, left_ref, right_ref)
    new_lt = [
        lt[l] + 0.15 * spread[l] + decoded(info_ref, rec_ref, 3, l, 1) * lr[l]
        for l in range(layers)
    ]
    put_edges(new_lt, low_out, high_out, left_out, right_out)
    gain = [1.0 + 0.2 * decoded(info_ref, rec_ref, 2, l, 0) for l in range(layers)]
    climbs, soon = chain(new_lr, decay, nothing)
    after = [-0.3 * new_lt[l] + gain[l] * new_lr[l] + climbs[l] for l in range(layers)]
    _, later = chain(after, decay, nothing)
    shares = [None] * layers
    power = jnp.ones_like(decay)
    for layer in reversed(range(layers)):
        shares[layer] = power
        power = decay * power
    climbs, _ = chain(shares, decay, nothing)
    after = [gain[l] * shares[l] + climbs[l] for l in range(layers)]
    _, weight = chain(after, decay, nothing)
    halves(info_ref, (now, soon, later, weight), scratch, keep_ref, give_ref)
    for l in range(layers):
        new_lt_ref[l] = new_lt[l]


def second_body(
    info_ref, rec_ref, seed_ref, lr_ref, lt_ref, low_ref, high_ref, left_ref, right_ref,
    length_ref, mine_ref, got_ref, new_lt_ref, mid_lr_ref, new_lr_ref, keep_ref, give_ref,
    low_out, high_out, left_out, right_out, carried, scratch,
):
    layers = lt_ref.shape[0]
    decay, _, _ = powers(length_ref[...])
    zero, one, two = restored(info_ref, mine_ref, got_ref, carried)
    lt = [lt_ref[layer] for layer in range(layers)]
    lr = [lr_ref[layer] for layer in range(layers)]
    climbs, _ = chain(lr, decay, zero)
    lr = [
        -0.3 * seed_ref[l]
        + (1.0 + 0.2 * decoded(info_ref, rec_ref, 3, l, 0)) * lr[l]
        + climbs[l]
        for l in range(layers)
    ]
    spread = laplace(info_ref, lt, low_ref, high_ref, left_ref, right_ref)
    new_lt = [
        lt[l] + 0.15 * spread[l] + decoded(info_ref, rec_ref, 2, l, 1) * lr[l]
        for l in range(layers)
    ]
    put_edges(new_lt, low_out, high_out, left_out, right_out)
    climbs, _ = chain(lr, decay, one)
    lr = [
        -0.3 * lt[l] + (1.0 + 0.2 * decoded(info_ref, rec_ref, 2, l, 0)) * lr[l] + climbs[l]
        for l in range(layers)
    ]
    climbs, _ = chain(lr, decay, two)
    new_lr = [
        -0.3 * new_lt[l]
        + (1.0 + 0.2 * decoded(info_ref, rec_ref, 1, l, 0)) * lr[l]
        + climbs[l]
        for l in range(layers)
    ]
    _, total = chain(new_lr, decay, jnp.zeros_like(decay))
    halves(info_ref, (total,), scratch, keep_ref, give_ref)
    for l in range(layers):
        new_lt_ref[l] = new_lt[l]
        mid_lr_ref[l] = lr[l]
        new_lr_ref[l] = new_lr[l]


def third_body(
    info_ref, rec_ref, seed_ref, one_ref, lt_ref, lr_ref, low_ref, high_ref, left_ref,
    right_ref, face_ref, new_lt_ref, flux_ref, low_out, high_out, left_out, right_out,
):
    layers, azimuths, radials = lt_ref.shape
    lt = [lt_ref[layer] for layer in range(layers)]
    spread = laplace(info_ref, lt, low_ref, high_ref, left_ref, right_ref)
    new_lt = [
        lt[l] + 0.15 * spread[l] + decoded(info_ref, rec_ref, 1, l, 1) * lr_ref[l]
        for l in range(layers)
    ]
    put_edges(new_lt, low_out, high_out, left_out, right_out)
    for l in range(layers):
        new_lt_ref[l] = new_lt[l]
    lane = lax.broadcasted_iota(jnp.int32, (azimuths, radials), 1)
    ones = jnp.ones((8, radials), jnp.float32)
    for l in range(layers):
        kept = jnp.where(
            lane == face_ref[l], (seed_ref[l] + one_ref[l]) + (lt[l] + new_lt[l]), 0.0
        )
        row = lax.dot_general(
            ones,
            kept,
            (((1,), (1,)), ((), ())),
            precision=lax.Precision.HIGHEST,
            preferred_element_type=jnp.float32,
        )[0:1, :]
        twice = jnp.concatenate([row, row], axis=1)
        flux_ref[l : l + 1, :] = twice
        left_out[layers + l : layers + l + 1, :] = twice
        right_out[layers + l : layers + l + 1, :] = twice


def last_body(
    info_ref, weight_ref, rec_ref, lt_ref, lr_ref, low_ref, high_ref, left_ref, right_ref,
    length_ref, mine_ref, got_ref, flux_ref, new_lt_ref, new_lr_ref, heat_ref, scratch,
):
    layers, azimuths, radials = lt_ref.shape
    band = weight_ref.shape[0] // 2
    decay, _, _ = powers(length_ref[...])
    (three,) = restored(info_ref, mine_ref, got_ref, scratch)
    lt = [lt_ref[layer] for layer in range(layers)]
    lr = [lr_ref[layer] for layer in range(layers)]
    spread = laplace(info_ref, lt, low_ref, high_ref, left_ref, right_ref)
    climbs, _ = chain(lr, decay, three)
    for l in range(layers):
        new_lt_ref[l] = lt[l] + 0.15 * spread[l] + decoded(info_ref, rec_ref, 0, l, 1) * lr[l]
        new_lr_ref[l] = (
            -0.3 * lt[l]
            + (1.0 + 0.2 * decoded(info_ref, rec_ref, 0, l, 0)) * lr[l]
            + climbs[l]
        )
    lane = lax.broadcasted_iota(jnp.int32, (layers, radials), 1)
    ring = jnp.where(
        lane < azimuths,
        flux_ref[...],
        jnp.where(
            lane < azimuths + band,
            right_ref[layers : 2 * layers, :],
            left_ref[layers : 2 * layers, :],
        ),
    )
    heat = jnp.zeros_like(ring)
    for offset in range(-band, band + 1):
        heat = heat + weight_ref[offset + band] * pltpu.roll(ring, (-offset) % radials, axis=1)
    heat_ref[...] = heat[:, :azimuths]


def run(body, scalars, args, shapes, scratch=()):
    smem = pl.BlockSpec(memory_space=pltpu.SMEM)
    vmem = pl.BlockSpec(memory_space=pltpu.VMEM)
    return pl.pallas_call(
        body,
        in_specs=[smem] * len(scalars) + [vmem] * len(args),
        out_specs=[vmem] * len(shapes),
        out_shape=[jax.ShapeDtypeStruct(shape, jnp.float32) for shape in shapes],
        scratch_shapes=[pltpu.VMEM(shape, jnp.float32) for shape in scratch],
        compiler_params=pltpu.CompilerParams(vmem_limit_bytes=STEP_VMEM),
    )(*scalars, *args)


def turned(value, axis, shift):
    count = lax.axis_size(axis)
    return lax.ppermute(value, axis, [(i, (i + shift) % count) for i in range(count)])


def exchanged(low, high, left, right):
    return (
        turned(high, "axial", 1),
        turned(low, "axial", -1),
        turned(right, "azim", 1),
        turned(left, "azim", -1),
    )


def swapped(value):
    return lax.ppermute(value, "axial", [(i, i ^ 1) for i in range(lax.axis_size("axial"))])


def carries(info, keep, give, length, count, rim):
    got = swapped(give)
    axial = lax.axis_size("axial")
    (total,) = run(chip_body, (info,), (keep, got, length), [(axial // 2, *keep.shape)])
    groups = [list(range(core, axial, 2)) for core in range(2)]
    sums = lax.all_to_all(total, "axial", 0, 0, tiled=True, axis_index_groups=groups)
    halo = exchanged(*rim)
    sums, halo = lax.optimization_barrier((sums, halo))
    shape = (count, *keep.shape[1:])
    mine, other = run(carry_body, (info,), (keep, got, sums, length), [shape, shape])
    return (mine, swapped(other)), halo


def local(stored, holder, seed_temp, seed_disloc, decay_length, face_radius, kernel):
    layers, azimuths, radials = seed_temp.shape
    axial, me = lax.axis_size("axial"), lax.axis_index("axial")
    wanted = lax.dynamic_index_in_dim(holder, me, 1, keepdims=False).reshape(-1)
    info = jnp.concatenate([wanted, jnp.stack([me, axial]).astype(jnp.int32)])
    plane = (azimuths, radials)
    side = (layers, radials)
    wide = (2 * layers, radials)
    block = (layers, azimuths, radials)
    first = (4, azimuths // 2, radials)
    single = (1, azimuths // 2, radials)
    edges = [plane, plane, side, side]

    pieces = lax.all_to_all(encode(stored), "axial", 0, 0, tiled=True)
    halo = exchanged(
        seed_temp[0], seed_temp[layers - 1], seed_temp[:, 0], seed_temp[:, azimuths - 1]
    )
    lt1, keep, give, *rim = run(
        first_body,
        (info,),
        (pieces, seed_temp, seed_disloc, *halo, decay_length),
        [block, first, first, *edges],
        [(4, *plane)],
    )
    carry, halo = carries(info, keep, give, decay_length, 3, rim)
    lt2, lr2, lr3, keep, give, *rim = run(
        second_body,
        (info,),
        (pieces, seed_temp, seed_disloc, lt1, *halo, decay_length, *carry),
        [block, block, block, single, single, *edges],
        [(3, *plane), (1, *plane)],
    )
    carry, halo = carries(info, keep, give, decay_length, 1, rim)
    lt3, flux, *rim = run(
        third_body,
        (info,),
        (pieces, seed_temp, lt1, lt2, lr2, *halo, face_radius[:, :, None]),
        [block, side, plane, plane, wide, wide],
    )
    halo = exchanged(*rim)
    return tuple(
        run(
            last_body,
            (info, kernel),
            (pieces, lt3, lr3, *halo, decay_length, *carry, flux),
            [block, block, (layers, azimuths)],
            [(1, *plane)],
        )
    )


def solution(mesh):
    in_specs = (
        P(None, "axial", "azim", None, None, None, None),
        P(),
        P("axial", "azim", None),
        P("axial", "azim", None),
        P("azim", None),
        P("axial", "azim"),
        P(),
    )
    out_specs = (P("axial", "azim", None), P("axial", "azim", None), P("axial", "azim"))
    return jax.shard_map(local, mesh=mesh, in_specs=in_specs, out_specs=out_specs, check_vma=False)
```

```python
import jax
import jax.numpy as jnp
from jax import lax
from jax.experimental import pallas as pl
from jax.experimental.pallas import tpu as pltpu
from jax.sharding import PartitionSpec as P

ROWS = 16
LANES = 128
RATE_MID = 3.7
RATE_SCALE = 10500.0
COEF_SCALE = 1374.0
COEF_BASE = 23.0
SEED_SCALE = 1023.0
SEED_BASE = 31.0
ENCODE_VMEM = 60 * 1024 * 1024
STEP_VMEM = 16 * 1024 * 1024


def squeezed(value, base, scale):
    size = jnp.log2(jnp.maximum(jnp.abs(value), 2.0**-base))
    size = size * scale + (base * scale + 0.5)
    return jnp.where(value < 0.0, -size, size).astype(jnp.int32).astype(jnp.int16)


def spread_out(code, base, scale):
    code = code.astype(jnp.int32).astype(jnp.float32)
    size = jnp.exp2(jnp.abs(code) * (1.0 / scale) - base)
    return jnp.where(code > 0.0, size, jnp.where(code < 0.0, -size, 0.0))


def encode_body(
    stored_ref, seed_ref, length_ref, out_ref, pieces, seed, length, codes, in_sems, more_sems,
    out_sems,
):
    steps, slots = stored_ref.shape[:2]
    owners = out_ref.shape[0]
    cap = slots // owners
    rows = 8 * ROWS
    first = [
        pltpu.make_async_copy(seed_ref, seed, more_sems.at[0]),
        pltpu.make_async_copy(length_ref, length, more_sems.at[1]),
    ]
    arrivals = [
        pltpu.make_async_copy(stored_ref.at[step], pieces.at[step], in_sems.at[step])
        for step in range(steps)
    ]
    for copy in first + arrivals:
        copy.start()
    row = lax.broadcasted_iota(jnp.int32, (rows, rows), 0)
    column = lax.broadcasted_iota(jnp.int32, (rows, rows), 1)
    picked = (row % ROWS) * 8 + row // ROWS == column
    order = jnp.where(picked, 1.0, 0.0).astype(jnp.bfloat16)
    for copy in first:
        copy.wait()
    decay, _, _ = powers(length[...])
    field = [seed[layer] for layer in range(seed.shape[0])]
    _, total = chain(field, decay, jnp.zeros_like(decay))
    total = squeezed(total, SEED_BASE, SEED_SCALE)
    per = 2 * cap
    half = total.shape[0] // 2
    for owner in range(owners):
        for block in range(half // ROWS):
            top = half * (owner % 2) + ROWS * block
            codes[owner, steps * per + block] = total[top : top + ROWS, :]

    def mixed(step, slot):
        cells = pieces[step, slot].astype(jnp.float32)
        return jnp.concatenate(
            [cells[:, LANES * r : LANES * (r + 1)] for r in range(ROWS)], axis=0
        ).astype(jnp.bfloat16)

    departures = []

    def depart(start, count):
        copy = pltpu.make_async_copy(
            codes.at[:, pl.ds(start, count)],
            out_ref.at[:, pl.ds(start, count)],
            out_sems.at[len(departures)],
        )
        copy.start()
        departures.append(copy)

    depart(steps * per, half // ROWS)
    for step in range(steps):
        arrivals[step].wait()
        for slot in range(0, slots, cap):
            both = jnp.concatenate([mixed(step, slot + c) for c in range(cap)], axis=1)
            parts = jnp.dot(order, both, preferred_element_type=jnp.float32)

            def part(index):
                return parts[ROWS * index : ROWS * (index + 1), :]

            squares = part(1) * part(1)
            for index in range(2, 7):
                squares = squares + part(index) * part(index)
            slope = jnp.tanh(part(0))
            total = 1.0 + squares * (1.0 / 6.0)
            rate = total * lax.rsqrt(total) * jnp.exp(0.5 * slope)
            coef = (0.1 * part(7)) * rate * (1.0 - slope * slope)
            coef_code = squeezed(coef, COEF_BASE, COEF_SCALE)
            rate_code = jnp.round((rate - RATE_MID) * RATE_SCALE)
            rate_code = rate_code.astype(jnp.int32).astype(jnp.int16)
            for c in range(cap):
                lanes = slice(LANES * c, LANES * (c + 1))
                codes[slot // cap, per * step + 2 * c] = rate_code[:, lanes]
                codes[slot // cap, per * step + 2 * c + 1] = coef_code[:, lanes]
        depart(per * step, per)
    for copy in departures:
        copy.wait()


def encode(stored, seed, length):
    steps, _, _, owners, cap, comps, cells = stored.shape
    flat = stored.reshape(steps, owners * cap, comps, cells)
    shape = (owners, steps * cap * 2 + seed.shape[1] // (2 * ROWS), ROWS, LANES)
    return pl.pallas_call(
        encode_body,
        in_specs=[pl.BlockSpec(memory_space=pl.ANY)] * 3,
        out_specs=pl.BlockSpec(memory_space=pl.ANY),
        out_shape=jax.ShapeDtypeStruct(shape, jnp.int16),
        scratch_shapes=[
            pltpu.VMEM(flat.shape, jnp.bfloat16),
            pltpu.VMEM(seed.shape, jnp.float32),
            pltpu.VMEM(length.shape, jnp.float32),
            pltpu.VMEM(shape, jnp.int16),
            pltpu.SemaphoreType.DMA((steps,)),
            pltpu.SemaphoreType.DMA((2,)),
            pltpu.SemaphoreType.DMA((steps + 1,)),
        ],
        compiler_params=pltpu.CompilerParams(vmem_limit_bytes=ENCODE_VMEM),
    )(flat, seed, length)


def decoded(info_ref, rec_ref, step, layer, field):
    pieces = []
    for quarter in range(4):
        held = info_ref[16 * step + 4 * layer + quarter]
        code = rec_ref[held // 2, 4 * step + 2 * (held % 2) + field]
        if field == 0:
            code = code.astype(jnp.int32).astype(jnp.float32)
            pieces.append(code * (1.0 / RATE_SCALE) + RATE_MID)
        else:
            pieces.append(spread_out(code, COEF_BASE, COEF_SCALE))
    return jnp.concatenate(pieces, axis=0)


def halos(info_ref, low_ref, high_ref, left_ref, right_ref):
    low = jnp.where(info_ref[64] == 0, 0.0, low_ref[...])
    high = jnp.where(info_ref[64] == info_ref[65] - 1, 0.0, high_ref[...])
    return low, high, left_ref[...], right_ref[...]


def radial(x):
    lane = lax.broadcasted_iota(jnp.int32, x.shape, 1)
    inner = jnp.where(lane == 0, 0.0, pltpu.roll(x, 1, axis=1))
    outer = jnp.where(lane == x.shape[1] - 1, 0.0, pltpu.roll(x, x.shape[1] - 1, axis=1))
    return inner + outer


def laplace(field, low, high, left=None, right=None):
    layers = len(field)
    azimuths = field[0].shape[0]
    row = lax.broadcasted_iota(jnp.int32, field[0].shape, 0)
    out = []
    for layer in range(layers):
        x = field[layer]
        below = low if layer == 0 else field[layer - 1]
        above = high if layer == layers - 1 else field[layer + 1]
        first = 0.0 if left is None else left[layer : layer + 1, :]
        last = 0.0 if right is None else right[layer : layer + 1, :]
        before = jnp.where(row == 0, first, pltpu.roll(x, 1, axis=0))
        after = jnp.where(row == azimuths - 1, last, pltpu.roll(x, azimuths - 1, axis=0))
        out.append(((below + above) + (before + after)) + radial(x) - 6.0 * x)
    return out


def chain(field, decay, carry):
    layers = len(field)
    out = [None] * layers
    for layer in reversed(range(layers)):
        out[layer] = carry
        carry = decay * carry + (1.0 - decay) * field[layer]
    return out, carry


def put_edges(field, low_ref, high_ref, left_ref, right_ref):
    layers = len(field)
    azimuths = field[0].shape[0]
    low_ref[...] = field[0]
    high_ref[...] = field[-1]
    for layer in range(layers):
        left_ref[layer : layer + 1, :] = field[layer][0:1, :]
        right_ref[layer : layer + 1, :] = field[layer][azimuths - 1 : azimuths, :]


def powers(length):
    decay = jnp.exp(-1.0 / length)
    cube = decay * decay * decay
    return decay, decay * cube, 4.0 * (1.0 - decay) * cube


def half_powers(info_ref, length_ref):
    half = length_ref.shape[0] // 2
    return powers(length_ref[pl.ds(half * (info_ref[64] % 2), half), :])


def halves(info_ref, values, scratch, keep_ref, give_ref):
    mine = info_ref[64] % 2
    half = scratch.shape[1] // 2
    for index, value in enumerate(values):
        scratch[index] = value
    for index in range(len(values)):
        keep_ref[index] = scratch[index, pl.ds(half * mine, half), :]
        give_ref[index] = scratch[index, pl.ds(half * (1 - mine), half), :]


def restored(info_ref, mine_ref, got_ref, scratch):
    mine = info_ref[64] % 2
    half = scratch.shape[1] // 2
    count = scratch.shape[0]
    for index in range(count):
        scratch[index, pl.ds(half * mine, half), :] = mine_ref[index]
        scratch[index, pl.ds(half * (1 - mine), half), :] = got_ref[index]
    return [scratch[index] for index in range(count)]


def cores(info_ref, keep_ref, got_ref):
    upper_here = info_ref[64] % 2 == 1
    own = [keep_ref[index] for index in range(keep_ref.shape[0])]
    other = [got_ref[index] for index in range(got_ref.shape[0])]
    upper = [jnp.where(upper_here, a, b) for a, b in zip(own, other)]
    lower = [jnp.where(upper_here, b, a) for a, b in zip(own, other)]
    return upper, lower


def share_out(info_ref, upper, lower, mine_ref, other_ref):
    upper_here = info_ref[64] % 2 == 1
    for index, (a, b) in enumerate(zip(upper, lower)):
        mine_ref[index] = jnp.where(upper_here, a, b)
        other_ref[index] = jnp.where(upper_here, b, a)


def applied(carry, here, fall, cross):
    out = [sums + fall * value for value, sums in zip(carry, here)]
    if len(carry) > 1:
        out[1] = out[1] + cross * carry[0]
    return tuple(out)


def climbed(info_ref, sums_ref, fall, cross):
    chips, count = sums_ref.shape[:2]

    def climb(k, total):
        here = [sums_ref[chips - 1 - k, index] for index in range(count)]
        return applied(total, here, fall * fall, 2.0 * fall * cross)

    zero = jnp.zeros_like(fall)
    return lax.fori_loop(0, chips - 1 - info_ref[64] // 2, climb, (zero,) * count)


def answered(gain, share, decay):
    climbs, _ = chain(share, decay, jnp.zeros_like(decay))
    return [g * s + c for g, s, c in zip(gain, share, climbs)]


def seed_carry_body(info_ref, rec_ref, length_ref, mine_ref, other_ref):
    _, fall, _ = half_powers(info_ref, length_ref)
    peers, blocks = rec_ref.shape[:2]
    count = fall.shape[0] // ROWS

    def total_of(peer):
        code = [rec_ref[peer, blocks - count + block] for block in range(count)]
        return jnp.concatenate(
            [spread_out(part, SEED_BASE, SEED_SCALE) for part in code], axis=0
        )

    upper = info_ref[64] // 2 * 2 + 1
    above = lax.fori_loop(
        0,
        peers - 1 - upper,
        lambda k, value: fall * value + total_of(peers - 1 - k),
        jnp.zeros_like(fall),
    )
    below = fall * above + total_of(upper)
    share_out(info_ref, (above,), (below,), mine_ref, other_ref)


def first_body(
    info_ref, rec_ref, lt_ref, lr_ref, low_ref, high_ref, left_ref, right_ref, length_ref,
    mine_ref, got_ref, new_lt_ref, new_lr_ref, source_ref, up_ref, down_ref, keep_ref, give_ref,
    carried, scratch,
):
    layers = lt_ref.shape[0]
    decay, _, _ = powers(length_ref[...])
    (zero,) = restored(info_ref, mine_ref, got_ref, carried)
    lt = [lt_ref[layer] for layer in range(layers)]
    lr = [lr_ref[layer] for layer in range(layers)]
    spread = laplace(lt, *halos(info_ref, low_ref, high_ref, left_ref, right_ref))
    new_lt = [
        lt[l] + 0.15 * spread[l] + decoded(info_ref, rec_ref, 3, l, 1) * lr[l]
        for l in range(layers)
    ]
    climbs, _ = chain(lr, decay, zero)
    lr = [
        -0.3 * lt[l] + (1.0 + 0.2 * decoded(info_ref, rec_ref, 3, l, 0)) * lr[l] + climbs[l]
        for l in range(layers)
    ]
    source = [decoded(info_ref, rec_ref, 2, l, 1) * lr[l] for l in range(layers)]
    up_ref[0], up_ref[1], up_ref[2] = new_lt[-2], new_lt[-1], source[-1]
    down_ref[0], down_ref[1], down_ref[2] = new_lt[0], new_lt[1], source[0]
    nothing = jnp.zeros_like(decay)
    _, now = chain(lr, decay, nothing)
    gain = [1.0 + 0.2 * decoded(info_ref, rec_ref, 2, l, 0) for l in range(layers)]
    after = [a - 0.3 * new_lt[l] for l, a in enumerate(answered(gain, lr, decay))]
    _, later = chain(after, decay, nothing)
    halves(info_ref, (now, later), scratch, keep_ref, give_ref)
    for l in range(layers):
        new_lt_ref[l] = new_lt[l]
        new_lr_ref[l] = lr[l]
        source_ref[l] = source[l]


def pair_chip_body(info_ref, keep_ref, got_ref, length_ref, out_ref):
    _, fall, cross = half_powers(info_ref, length_ref)
    upper, lower = cores(info_ref, keep_ref, got_ref)
    total = applied(upper, lower, fall, cross)
    for chip in range(out_ref.shape[0]):
        for index, value in enumerate(total):
            out_ref[chip, index] = value


def reach_body(
    info_ref, lt_ref, source_ref, low_ref, high_ref, new_lt_ref, left_out, right_out,
):
    layers, azimuths, _ = lt_ref.shape
    bottom = info_ref[64] == 0
    top = info_ref[64] == info_ref[65] - 1
    low = [jnp.where(bottom, 0.0, low_ref[index]) for index in range(3)]
    high = [jnp.where(top, 0.0, high_ref[index]) for index in range(3)]
    lt = [low[1], *[lt_ref[l] for l in range(layers)], high[0]]
    source = [low[2], *[source_ref[l] for l in range(layers)], high[2]]
    spread = laplace(lt, low[0], high[1])
    new_lt = [lt[l] + 0.15 * spread[l] + source[l] for l in range(layers + 2)]
    new_lt[0] = jnp.where(bottom, 0.0, new_lt[0])
    new_lt[-1] = jnp.where(top, 0.0, new_lt[-1])
    sides = ((left_out, 0, 1), (right_out, azimuths - 1, azimuths - 2))
    for out, edge, inside in sides:
        for l in range(layers + 2):
            out[l : l + 1, :] = lt[l][edge : edge + 1, :]
        out[layers + 2 : layers + 4, :] = jnp.zeros_like(out[layers + 2 : layers + 4, :])
        for l in range(layers):
            out[8 + l : 9 + l, :] = lt[l + 1][inside : inside + 1, :]
            out[12 + l : 13 + l, :] = source[l + 1][edge : edge + 1, :]
    for l in range(layers + 2):
        new_lt_ref[l] = new_lt[l]


def beyond(there, here):
    middle = there[1:5]
    total = (there[0:4] + there[2:6]) + (there[8:12] + here[1:5]) + radial(middle)
    return middle + 0.15 * (total - 6.0 * middle) + there[12:16]


def second_body(
    info_ref, rec_ref, old_lt_ref, lr_ref, lt_ref, own_left_ref, own_right_ref, left_ref,
    right_ref, length_ref, new_lt_ref, sides_ref, keep_ref, give_ref, scratch,
):
    layers, azimuths, radials = lr_ref.shape
    decay, _, _ = powers(length_ref[...])
    nothing = jnp.zeros_like(decay)
    left, right = left_ref[...], right_ref[...]
    sides_ref[0:layers, :] = beyond(left, own_left_ref[...])
    sides_ref[layers : 2 * layers, :] = beyond(right, own_right_ref[...])
    row = lax.broadcasted_iota(jnp.int32, (azimuths, radials), 0)
    new_lt = []
    for l in range(layers + 2):
        missing = jnp.where(
            row == 0,
            left[l : l + 1, :],
            jnp.where(row == azimuths - 1, right[l : l + 1, :], 0.0),
        )
        new_lt.append(lt_ref[l] + 0.15 * missing)
        new_lt_ref[l] = new_lt[l]
    new_lt = new_lt[1:-1]
    one = [1.0 + 0.2 * decoded(info_ref, rec_ref, 2, l, 0) for l in range(layers)]
    two = [1.0 + 0.2 * decoded(info_ref, rec_ref, 1, l, 0) for l in range(layers)]
    lr = [lr_ref[layer] for layer in range(layers)]
    lr = [a - 0.3 * old_lt_ref[l] for l, a in enumerate(answered(one, lr, decay))]
    lr = [a - 0.3 * new_lt[l] for l, a in enumerate(answered(two, lr, decay))]
    _, later = chain(lr, decay, nothing)
    share = [None] * layers
    power = jnp.ones_like(decay)
    for layer in reversed(range(layers)):
        share[layer] = power
        power = decay * power
    _, weight = chain(answered(two, share, decay), decay, nothing)
    halves(info_ref, (later, weight), scratch, keep_ref, give_ref)


def pair_carry_body(
    info_ref, keep_ref, got_ref, more_ref, more_got_ref, sums_ref, length_ref,
    mine_ref, other_ref, out_ref,
):
    _, fall, cross = half_powers(info_ref, length_ref)
    above = climbed(info_ref, sums_ref, fall, cross)
    upper, _ = cores(info_ref, keep_ref, got_ref)
    below = applied(above, upper, fall, cross)
    share_out(info_ref, above, below, mine_ref, other_ref)
    upper, lower = cores(info_ref, more_ref, more_got_ref)
    upper = upper[0] + upper[1] * above[0] + cross * above[1]
    lower = lower[0] + lower[1] * below[0] + cross * below[1]
    total = lower + fall * upper
    for peer in range(out_ref.shape[0]):
        out_ref[peer] = jnp.where(info_ref[64] // 2 == peer // 2, upper, total)


def third_body(
    info_ref, rec_ref, seed_ref, one_ref, lt_ref, lr_ref, sides_ref, length_ref, face_ref,
    mine_ref, got_ref, new_lt_ref, new_lr_ref, flux_ref, low_out, high_out, left_out, right_out,
    scratch,
):
    layers, azimuths, radials = lr_ref.shape
    decay, _, _ = powers(length_ref[...])
    one, two = restored(info_ref, mine_ref, got_ref, scratch)
    before = [one_ref[layer] for layer in range(layers)]
    lt = [lt_ref[layer + 1] for layer in range(layers)]
    lr = [lr_ref[layer] for layer in range(layers)]
    climbs, _ = chain(lr, decay, one)
    lr = [
        -0.3 * before[l]
        + (1.0 + 0.2 * decoded(info_ref, rec_ref, 2, l, 0)) * lr[l]
        + climbs[l]
        for l in range(layers)
    ]
    sides = sides_ref[...]
    spread = laplace(lt, lt_ref[0], lt_ref[layers + 1], sides[:layers], sides[layers:])
    new_lt = [
        lt[l] + 0.15 * spread[l] + decoded(info_ref, rec_ref, 1, l, 1) * lr[l]
        for l in range(layers)
    ]
    put_edges(new_lt, low_out, high_out, left_out, right_out)
    climbs, _ = chain(lr, decay, two)
    for l in range(layers):
        new_lt_ref[l] = new_lt[l]
        new_lr_ref[l] = (
            -0.3 * lt[l] + (1.0 + 0.2 * decoded(info_ref, rec_ref, 1, l, 0)) * lr[l] + climbs[l]
        )
    lane = lax.broadcasted_iota(jnp.int32, (azimuths, radials), 1)
    ones = jnp.ones((8, radials), jnp.float32)
    for l in range(layers):
        kept = jnp.where(
            lane == face_ref[l], (seed_ref[l] + before[l]) + (lt[l] + new_lt[l]), 0.0
        )
        row = lax.dot_general(
            ones,
            kept,
            (((1,), (1,)), ((), ())),
            precision=lax.Precision.HIGHEST,
            preferred_element_type=jnp.float32,
        )[0:1, :]
        twice = jnp.concatenate([row, row], axis=1)
        flux_ref[l : l + 1, :] = twice
        left_out[layers + l : layers + l + 1, :] = twice
        right_out[layers + l : layers + l + 1, :] = twice


def last_body(
    info_ref, weight_ref, rec_ref, lt_ref, lr_ref, low_ref, high_ref, left_ref, right_ref,
    length_ref, sums_ref, flux_ref, new_lt_ref, new_lr_ref, heat_ref,
):
    layers, azimuths, radials = lt_ref.shape
    band = weight_ref.shape[0] // 2
    decay, fall, _ = powers(length_ref[...])
    chips = sums_ref.shape[0] // 2
    here = info_ref[64] // 2

    def total_of(chip):
        return jnp.concatenate([sums_ref[2 * chip], sums_ref[2 * chip + 1]], axis=0)

    above = lax.fori_loop(
        0,
        chips - 1 - here,
        lambda k, value: fall * fall * value + total_of(chips - 1 - k),
        jnp.zeros_like(fall),
    )
    three = jnp.where(info_ref[64] % 2 == 1, above, fall * above + total_of(here))
    lt = [lt_ref[layer] for layer in range(layers)]
    lr = [lr_ref[layer] for layer in range(layers)]
    spread = laplace(lt, *halos(info_ref, low_ref, high_ref, left_ref, right_ref))
    climbs, _ = chain(lr, decay, three)
    for l in range(layers):
        new_lt_ref[l] = lt[l] + 0.15 * spread[l] + decoded(info_ref, rec_ref, 0, l, 1) * lr[l]
        new_lr_ref[l] = (
            -0.3 * lt[l]
            + (1.0 + 0.2 * decoded(info_ref, rec_ref, 0, l, 0)) * lr[l]
            + climbs[l]
        )
    lane = lax.broadcasted_iota(jnp.int32, (layers, radials), 1)
    ring = jnp.where(
        lane < azimuths,
        flux_ref[...],
        jnp.where(
            lane < azimuths + band,
            right_ref[layers : 2 * layers, :],
            left_ref[layers : 2 * layers, :],
        ),
    )
    heat = jnp.zeros_like(ring)
    for offset in range(-band, band + 1):
        heat = heat + weight_ref[offset + band] * pltpu.roll(ring, (-offset) % radials, axis=1)
    heat_ref[...] = heat[:, :azimuths]


def run(body, scalars, args, shapes, scratch=()):
    smem = pl.BlockSpec(memory_space=pltpu.SMEM)
    vmem = pl.BlockSpec(memory_space=pltpu.VMEM)
    return pl.pallas_call(
        body,
        in_specs=[smem] * len(scalars) + [vmem] * len(args),
        out_specs=[vmem] * len(shapes),
        out_shape=[jax.ShapeDtypeStruct(shape, jnp.float32) for shape in shapes],
        scratch_shapes=[pltpu.VMEM(shape, jnp.float32) for shape in scratch],
        compiler_params=pltpu.CompilerParams(vmem_limit_bytes=STEP_VMEM),
    )(*scalars, *args)


def turned(value, axis, shift):
    count = lax.axis_size(axis)
    return lax.ppermute(value, axis, [(i, (i + shift) % count) for i in range(count)])


def exchanged(low, high, left, right):
    return (
        turned(high, "axial", 1),
        turned(low, "axial", -1),
        turned(right, "azim", 1),
        turned(left, "azim", -1),
    )


def swapped(value):
    return lax.ppermute(value, "axial", [(i, i ^ 1) for i in range(lax.axis_size("axial"))])


def between_chips(value):
    axial = lax.axis_size("axial")
    groups = [list(range(core, axial, 2)) for core in range(2)]
    return lax.all_to_all(value, "axial", 0, 0, tiled=True, axis_index_groups=groups)


def local(stored, holder, seed_temp, seed_disloc, decay_length, face_radius, kernel):
    layers, azimuths, radials = seed_temp.shape
    axial, me = lax.axis_size("axial"), lax.axis_index("axial")
    wanted = lax.dynamic_index_in_dim(holder, me, 1, keepdims=False).reshape(-1)
    info = jnp.concatenate([wanted, jnp.stack([me, axial]).astype(jnp.int32)])
    plane = (azimuths, radials)
    side = (layers, radials)
    wide = (2 * layers, radials)
    block = (layers, azimuths, radials)

    def half(count):
        return (count, azimuths // 2, radials)

    def copies(count):
        return (axial // 2, *half(count))

    codes = encode(stored, seed_disloc, decay_length)
    pieces = lax.all_to_all(codes, "axial", 0, 0, tiled=True)
    halo = exchanged(
        seed_temp[0], seed_temp[layers - 1], seed_temp[:, 0], seed_temp[:, azimuths - 1]
    )
    pieces, *halo = lax.optimization_barrier((pieces, *halo))
    mine, other = run(seed_carry_body, (info,), (pieces, decay_length), [half(1)] * 2)
    lt1, lr1, source, up, down, keep, give = run(
        first_body,
        (info,),
        (pieces, seed_temp, seed_disloc, *halo, decay_length, mine, swapped(other)),
        [block, block, block, (3, *plane), (3, *plane), half(2), half(2)],
        [(1, *plane), (2, *plane)],
    )
    got = swapped(give)
    low, high = turned(up, "axial", 1), turned(down, "axial", -1)
    got, low, high = lax.optimization_barrier((got, low, high))
    (total,) = run(pair_chip_body, (info,), (keep, got, decay_length), [copies(2)])
    sums = between_chips(total)
    lt2, left, right = run(
        reach_body,
        (info,),
        (lt1, source, low, high),
        [(layers + 2, *plane), (16, radials), (16, radials)],
    )
    before, after = turned(right, "azim", 1), turned(left, "azim", -1)
    lt2, sides, more, give = run(
        second_body,
        (info,),
        (pieces, lt1, lr1, lt2, left, right, before, after, decay_length),
        [(layers + 2, *plane), wide, half(2), half(2)],
        [(2, *plane)],
    )
    more_got = swapped(give)
    sums, more_got = lax.optimization_barrier((sums, more_got))
    mine, other, total = run(
        pair_carry_body,
        (info,),
        (keep, got, more, more_got, sums, decay_length),
        [half(2), half(2), (axial, *half(1)[1:])],
    )
    sums = lax.all_to_all(total, "axial", 0, 0, tiled=True)
    lt3, lr3, flux, *rim = run(
        third_body,
        (info,),
        (
            pieces, seed_temp, lt1, lt2, lr1, sides, decay_length, face_radius[:, :, None],
            mine, swapped(other),
        ),
        [block, block, side, plane, plane, wide, wide],
        [(2, *plane)],
    )
    halo = exchanged(*rim)
    return tuple(
        run(
            last_body,
            (info, kernel),
            (pieces, lt3, lr3, *halo, decay_length, sums, flux),
            [block, block, (layers, azimuths)],
        )
    )


def solution(mesh):
    in_specs = (
        P(None, "axial", "azim", None, None, None, None),
        P(),
        P("axial", "azim", None),
        P("axial", "azim", None),
        P("azim", None),
        P("axial", "azim"),
        P(),
    )
    out_specs = (P("axial", "azim", None), P("axial", "azim", None), P("axial", "azim"))
    return jax.shard_map(local, mesh=mesh, in_specs=in_specs, out_specs=out_specs, check_vma=False)
```

```python
import jax
import jax.numpy as jnp
from jax import lax
from jax.experimental import pallas as pl
from jax.experimental.pallas import tpu as pltpu
from jax.sharding import PartitionSpec as P

ROWS = 16
LANES = 128
RATE_MID = 3.7
RATE_SCALE = 10500.0
COEF_SCALE = 1374.0
COEF_BASE = 23.0
SEED_SCALE = 1023.0
SEED_BASE = 31.0
SUM_SCALE = 728.0
SUM_BASE = 36.0
ENCODE_VMEM = 60 * 1024 * 1024
STEP_VMEM = 16 * 1024 * 1024
SPAN_FLOPS = 1_000_000_000
SPAN_BYTES = 3_000_000
CHIP_SPAN = 50
REACH_SPAN = 100
THIRD_SPAN = 100


def squeezed(value, base, scale):
    size = jnp.log2(jnp.maximum(jnp.abs(value), 2.0**-base))
    size = size * scale + (base * scale + 0.5)
    return jnp.where(value < 0.0, -size, size).astype(jnp.int32)


def spread_out(code, base, scale):
    code = code.astype(jnp.int32).astype(jnp.float32)
    size = jnp.exp2(jnp.abs(code) * (1.0 / scale) - base)
    return jnp.where(code > 0.0, size, jnp.where(code < 0.0, -size, 0.0))


def encode_body(
    stored_ref, seed_ref, length_ref, out_ref, pieces, seed, length, codes, in_sems, more_sems,
    out_sems,
):
    steps, slots = stored_ref.shape[:2]
    owners = out_ref.shape[0]
    cap = slots // owners
    rows = 8 * ROWS
    first = [
        pltpu.make_async_copy(seed_ref, seed, more_sems.at[0]),
        pltpu.make_async_copy(length_ref, length, more_sems.at[1]),
    ]
    arrivals = [
        pltpu.make_async_copy(stored_ref.at[step], pieces.at[step], in_sems.at[step])
        for step in range(steps)
    ]
    for copy in first + arrivals:
        copy.start()
    row = lax.broadcasted_iota(jnp.int32, (rows, rows), 0)
    column = lax.broadcasted_iota(jnp.int32, (rows, rows), 1)
    picked = (row % ROWS) * 8 + row // ROWS == column
    order = jnp.where(picked, 1.0, 0.0).astype(jnp.bfloat16)
    for copy in first:
        copy.wait()
    decay, _, _ = powers(length[...])
    field = [seed[layer] for layer in range(seed.shape[0])]
    _, total = chain(field, decay, jnp.zeros_like(decay))
    total = squeezed(total, SEED_BASE, SEED_SCALE).astype(jnp.int16)
    per = 2 * cap
    half = total.shape[0] // 2
    for owner in range(owners):
        for block in range(half // ROWS):
            top = half * (owner % 2) + ROWS * block
            codes[owner, steps * per + block] = total[top : top + ROWS, :]

    def mixed(step, slot):
        cells = pieces[step, slot].astype(jnp.float32)
        return jnp.concatenate(
            [cells[:, LANES * r : LANES * (r + 1)] for r in range(ROWS)], axis=0
        ).astype(jnp.bfloat16)

    departures = []

    def depart(start, count):
        copy = pltpu.make_async_copy(
            codes.at[:, pl.ds(start, count)],
            out_ref.at[:, pl.ds(start, count)],
            out_sems.at[len(departures)],
        )
        copy.start()
        departures.append(copy)

    depart(steps * per, half // ROWS)
    for step in range(steps):
        arrivals[step].wait()
        for slot in range(0, slots, cap):
            both = jnp.concatenate([mixed(step, slot + c) for c in range(cap)], axis=1)
            parts = jnp.dot(order, both, preferred_element_type=jnp.float32)

            def part(index):
                return parts[ROWS * index : ROWS * (index + 1), :]

            squares = part(1) * part(1)
            for index in range(2, 7):
                squares = squares + part(index) * part(index)
            slope = jnp.tanh(part(0))
            total = 1.0 + squares * (1.0 / 6.0)
            rate = total * lax.rsqrt(total) * jnp.exp(0.5 * slope)
            coef = (0.1 * part(7)) * rate * (1.0 - slope * slope)
            coef_code = squeezed(coef, COEF_BASE, COEF_SCALE).astype(jnp.int16)
            rate_code = jnp.round((rate - RATE_MID) * RATE_SCALE)
            rate_code = rate_code.astype(jnp.int32).astype(jnp.int16)
            for c in range(cap):
                lanes = slice(LANES * c, LANES * (c + 1))
                codes[slot // cap, per * step + 2 * c] = rate_code[:, lanes]
                codes[slot // cap, per * step + 2 * c + 1] = coef_code[:, lanes]
        depart(per * step, per)
    for copy in departures:
        copy.wait()


def encode(stored, seed, length):
    steps, _, _, owners, cap, comps, cells = stored.shape
    flat = stored.reshape(steps, owners * cap, comps, cells)
    shape = (owners, steps * cap * 2 + seed.shape[1] // (2 * ROWS), ROWS, LANES)
    return pl.pallas_call(
        encode_body,
        in_specs=[pl.BlockSpec(memory_space=pl.ANY)] * 3,
        out_specs=pl.BlockSpec(memory_space=pl.ANY),
        out_shape=jax.ShapeDtypeStruct(shape, jnp.int16),
        scratch_shapes=[
            pltpu.VMEM(flat.shape, jnp.bfloat16),
            pltpu.VMEM(seed.shape, jnp.float32),
            pltpu.VMEM(length.shape, jnp.float32),
            pltpu.VMEM(shape, jnp.int16),
            pltpu.SemaphoreType.DMA((steps,)),
            pltpu.SemaphoreType.DMA((2,)),
            pltpu.SemaphoreType.DMA((steps + 1,)),
        ],
        compiler_params=pltpu.CompilerParams(vmem_limit_bytes=ENCODE_VMEM),
    )(flat, seed, length)


def decoded(info_ref, rec_ref, step, layer, field):
    pieces = []
    for quarter in range(4):
        held = info_ref[16 * step + 4 * layer + quarter]
        code = rec_ref[held // 2, 4 * step + 2 * (held % 2) + field]
        if field == 0:
            code = code.astype(jnp.int32).astype(jnp.float32)
            pieces.append(code * (1.0 / RATE_SCALE) + RATE_MID)
        else:
            pieces.append(spread_out(code, COEF_BASE, COEF_SCALE))
    return jnp.concatenate(pieces, axis=0)


def halos(info_ref, low_ref, high_ref, left_ref, right_ref):
    low = jnp.where(info_ref[64] == 0, 0.0, low_ref[...])
    high = jnp.where(info_ref[64] == info_ref[65] - 1, 0.0, high_ref[...])
    return low, high, left_ref[...], right_ref[...]


def radial(x):
    lane = lax.broadcasted_iota(jnp.int32, x.shape, 1)
    inner = jnp.where(lane == 0, 0.0, pltpu.roll(x, 1, axis=1))
    outer = jnp.where(lane == x.shape[1] - 1, 0.0, pltpu.roll(x, x.shape[1] - 1, axis=1))
    return inner + outer


def laplace(field, low, high, left=None, right=None):
    layers = len(field)
    azimuths = field[0].shape[0]
    row = lax.broadcasted_iota(jnp.int32, field[0].shape, 0)
    out = []
    for layer in range(layers):
        x = field[layer]
        below = low if layer == 0 else field[layer - 1]
        above = high if layer == layers - 1 else field[layer + 1]
        first = 0.0 if left is None else left[layer : layer + 1, :]
        last = 0.0 if right is None else right[layer : layer + 1, :]
        before = jnp.where(row == 0, first, pltpu.roll(x, 1, axis=0))
        after = jnp.where(row == azimuths - 1, last, pltpu.roll(x, azimuths - 1, axis=0))
        out.append(((below + above) + (before + after)) + radial(x) - 6.0 * x)
    return out


def chain(field, decay, carry):
    layers = len(field)
    out = [None] * layers
    for layer in reversed(range(layers)):
        out[layer] = carry
        carry = decay * carry + (1.0 - decay) * field[layer]
    return out, carry


def put_edges(field, low_ref, high_ref, left_ref, right_ref):
    layers = len(field)
    azimuths = field[0].shape[0]
    low_ref[...] = field[0]
    high_ref[...] = field[-1]
    for layer in range(layers):
        left_ref[layer : layer + 1, :] = field[layer][0:1, :]
        right_ref[layer : layer + 1, :] = field[layer][azimuths - 1 : azimuths, :]


def powers(length):
    decay = jnp.exp(-1.0 / length)
    cube = decay * decay * decay
    return decay, decay * cube, 4.0 * (1.0 - decay) * cube


def half_powers(info_ref, length_ref):
    half = length_ref.shape[0] // 2
    return powers(length_ref[pl.ds(half * (info_ref[64] % 2), half), :])


def halves(info_ref, values, scratch, keep_ref, give_ref):
    mine = info_ref[64] % 2
    half = scratch.shape[1] // 2
    for index, value in enumerate(values):
        scratch[index] = value
    for index in range(len(values)):
        keep_ref[index] = scratch[index, pl.ds(half * mine, half), :]
        give_ref[index] = scratch[index, pl.ds(half * (1 - mine), half), :]


def restored(info_ref, mine_ref, got_ref, scratch):
    mine = info_ref[64] % 2
    half = scratch.shape[1] // 2
    count = scratch.shape[0]
    for index in range(count):
        scratch[index, pl.ds(half * mine, half), :] = mine_ref[index]
        scratch[index, pl.ds(half * (1 - mine), half), :] = got_ref[index]
    return [scratch[index] for index in range(count)]


def cores(info_ref, keep_ref, got_ref):
    upper_here = info_ref[64] % 2 == 1
    own = [keep_ref[index] for index in range(keep_ref.shape[0])]
    other = [got_ref[index] for index in range(len(own))]
    upper = [jnp.where(upper_here, a, b) for a, b in zip(own, other)]
    lower = [jnp.where(upper_here, b, a) for a, b in zip(own, other)]
    return upper, lower


def share_out(info_ref, upper, lower, mine_ref, other_ref):
    upper_here = info_ref[64] % 2 == 1
    for index, (a, b) in enumerate(zip(upper, lower)):
        mine_ref[index] = jnp.where(upper_here, a, b)
        other_ref[index] = jnp.where(upper_here, b, a)


def applied(carry, here, fall, cross):
    out = [sums + fall * value for value, sums in zip(carry, here)]
    if len(carry) > 1:
        out[1] = out[1] + cross * carry[0]
    return tuple(out)


def put_sum(out_ref, at, start, code):
    code = code.astype(jnp.int16)
    for block in range(code.shape[0] // ROWS):
        out_ref[at, start + block] = code[ROWS * block : ROWS * (block + 1), :]


def got_sum(sums_ref, at, start, count):
    code = [sums_ref[at, start + block] for block in range(count)]
    return jnp.concatenate([spread_out(part, SUM_BASE, SUM_SCALE) for part in code], axis=0)


def climbed(info_ref, sums_ref, fall, cross):
    chips, blocks = sums_ref.shape[:2]
    per = fall.shape[0] // ROWS
    count = blocks // per

    def climb(k, total):
        here = [got_sum(sums_ref, chips - 1 - k, per * index, per) for index in range(count)]
        return applied(total, here, fall * fall, 2.0 * fall * cross)

    zero = jnp.zeros_like(fall)
    return lax.fori_loop(0, chips - 1 - info_ref[64] // 2, climb, (zero,) * count)


def answered(gain, share, decay):
    climbs, _ = chain(share, decay, jnp.zeros_like(decay))
    return [g * s + c for g, s, c in zip(gain, share, climbs)]


def seed_carry_body(info_ref, rec_ref, length_ref, mine_ref, other_ref):
    _, fall, _ = half_powers(info_ref, length_ref)
    peers, blocks = rec_ref.shape[:2]
    count = fall.shape[0] // ROWS

    def total_of(peer):
        code = [rec_ref[peer, blocks - count + block] for block in range(count)]
        return jnp.concatenate(
            [spread_out(part, SEED_BASE, SEED_SCALE) for part in code], axis=0
        )

    upper = info_ref[64] // 2 * 2 + 1
    above = lax.fori_loop(
        0,
        peers - 1 - upper,
        lambda k, value: fall * value + total_of(peers - 1 - k),
        jnp.zeros_like(fall),
    )
    below = fall * above + total_of(upper)
    share_out(info_ref, (above,), (below,), mine_ref, other_ref)


def first_body(
    info_ref, rec_ref, lt_ref, lr_ref, low_ref, high_ref, left_ref, right_ref, length_ref,
    mine_ref, got_ref, new_lt_ref, new_lr_ref, source_ref, far_ref, keep_ref, give_ref,
    carried, scratch,
):
    layers = lt_ref.shape[0]
    decay, _, _ = powers(length_ref[...])
    (zero,) = restored(info_ref, mine_ref, got_ref, carried)
    lt = [lt_ref[layer] for layer in range(layers)]
    lr = [lr_ref[layer] for layer in range(layers)]
    spread = laplace(lt, *halos(info_ref, low_ref, high_ref, left_ref, right_ref))
    new_lt = [
        lt[l] + 0.15 * spread[l] + decoded(info_ref, rec_ref, 3, l, 1) * lr[l]
        for l in range(layers)
    ]
    climbs, _ = chain(lr, decay, zero)
    lr = [
        -0.3 * lt[l] + (1.0 + 0.2 * decoded(info_ref, rec_ref, 3, l, 0)) * lr[l] + climbs[l]
        for l in range(layers)
    ]
    source = [decoded(info_ref, rec_ref, 2, l, 1) * lr[l] for l in range(layers)]
    half = decay.shape[0] // 2
    up, down = (new_lt[-2], new_lt[-1], source[-1]), (new_lt[0], new_lt[1], source[0])
    upper_here = info_ref[64] % 2 == 1
    for index in range(3):
        far_ref[index] = jnp.where(upper_here, up[index], down[index])
        near = jnp.where(upper_here, down[index], up[index])
        give_ref[2 + 2 * index] = near[:half]
        give_ref[3 + 2 * index] = near[half:]
    nothing = jnp.zeros_like(decay)
    _, now = chain(lr, decay, nothing)
    gain = [1.0 + 0.2 * decoded(info_ref, rec_ref, 2, l, 0) for l in range(layers)]
    after = [a - 0.3 * new_lt[l] for l, a in enumerate(answered(gain, lr, decay))]
    _, later = chain(after, decay, nothing)
    halves(info_ref, (now, later), scratch, keep_ref, give_ref)
    for l in range(layers):
        new_lt_ref[l] = new_lt[l]
        new_lr_ref[l] = lr[l]
        source_ref[l] = source[l]


def pair_chip_body(info_ref, keep_ref, got_ref, length_ref, out_ref):
    _, fall, cross = half_powers(info_ref, length_ref)
    upper, lower = cores(info_ref, keep_ref, got_ref)
    total = applied(upper, lower, fall, cross)
    total = [squeezed(value, SUM_BASE, SUM_SCALE) for value in total]
    per = fall.shape[0] // ROWS
    for chip in range(out_ref.shape[0]):
        for index, value in enumerate(total):
            put_sum(out_ref, chip, per * index, value)


def reach_body(
    info_ref, lt_ref, source_ref, near_ref, far_ref, new_lt_ref, left_out, right_out,
):
    layers, azimuths, _ = lt_ref.shape
    bottom = info_ref[64] == 0
    top = info_ref[64] == info_ref[65] - 1
    upper_here = info_ref[64] % 2 == 1
    low, high = [], []
    for index in range(3):
        near = jnp.concatenate([near_ref[2 + 2 * index], near_ref[3 + 2 * index]], axis=0)
        far = jnp.where(jnp.logical_or(bottom, top), 0.0, far_ref[index])
        low.append(jnp.where(upper_here, near, far))
        high.append(jnp.where(upper_here, far, near))
    lt = [low[1], *[lt_ref[l] for l in range(layers)], high[0]]
    source = [low[2], *[source_ref[l] for l in range(layers)], high[2]]
    spread = laplace(lt, low[0], high[1])
    new_lt = [lt[l] + 0.15 * spread[l] + source[l] for l in range(layers + 2)]
    new_lt[0] = jnp.where(bottom, 0.0, new_lt[0])
    new_lt[-1] = jnp.where(top, 0.0, new_lt[-1])
    sides = ((left_out, 0, 1), (right_out, azimuths - 1, azimuths - 2))
    for out, edge, inside in sides:
        for l in range(layers + 2):
            out[l : l + 1, :] = lt[l][edge : edge + 1, :]
        out[layers + 2 : layers + 4, :] = jnp.zeros_like(out[layers + 2 : layers + 4, :])
        for l in range(layers):
            out[8 + l : 9 + l, :] = lt[l + 1][inside : inside + 1, :]
            out[12 + l : 13 + l, :] = source[l + 1][edge : edge + 1, :]
    for l in range(layers + 2):
        new_lt_ref[l] = new_lt[l]


def beyond(there, here):
    middle = there[1:5]
    total = (there[0:4] + there[2:6]) + (there[8:12] + here[1:5]) + radial(middle)
    return middle + 0.15 * (total - 6.0 * middle) + there[12:16]


def second_body(
    info_ref, rec_ref, old_lt_ref, lr_ref, lt_ref, own_left_ref, own_right_ref, left_ref,
    right_ref, length_ref, new_lt_ref, sides_ref, keep_ref, give_ref, scratch,
):
    layers, azimuths, radials = lr_ref.shape
    decay, _, _ = powers(length_ref[...])
    nothing = jnp.zeros_like(decay)
    left, right = left_ref[...], right_ref[...]
    sides_ref[0:layers, :] = beyond(left, own_left_ref[...])
    sides_ref[layers : 2 * layers, :] = beyond(right, own_right_ref[...])
    row = lax.broadcasted_iota(jnp.int32, (azimuths, radials), 0)
    new_lt = []
    for l in range(layers + 2):
        missing = jnp.where(
            row == 0,
            left[l : l + 1, :],
            jnp.where(row == azimuths - 1, right[l : l + 1, :], 0.0),
        )
        new_lt.append(lt_ref[l] + 0.15 * missing)
        new_lt_ref[l] = new_lt[l]
    new_lt = new_lt[1:-1]
    one = [1.0 + 0.2 * decoded(info_ref, rec_ref, 2, l, 0) for l in range(layers)]
    two = [1.0 + 0.2 * decoded(info_ref, rec_ref, 1, l, 0) for l in range(layers)]
    lr = [lr_ref[layer] for layer in range(layers)]
    lr = [a - 0.3 * old_lt_ref[l] for l, a in enumerate(answered(one, lr, decay))]
    lr = [a - 0.3 * new_lt[l] for l, a in enumerate(answered(two, lr, decay))]
    _, later = chain(lr, decay, nothing)
    share = [None] * layers
    power = jnp.ones_like(decay)
    for layer in reversed(range(layers)):
        share[layer] = power
        power = decay * power
    _, weight = chain(answered(two, share, decay), decay, nothing)
    halves(info_ref, (later, weight), scratch, keep_ref, give_ref)


def pair_carry_body(
    info_ref, keep_ref, got_ref, more_ref, more_got_ref, sums_ref, length_ref,
    mine_ref, other_ref, out_ref,
):
    _, fall, cross = half_powers(info_ref, length_ref)
    above = climbed(info_ref, sums_ref, fall, cross)
    upper, _ = cores(info_ref, keep_ref, got_ref)
    below = applied(above, upper, fall, cross)
    share_out(info_ref, above, below, mine_ref, other_ref)
    upper, lower = cores(info_ref, more_ref, more_got_ref)
    upper = upper[0] + upper[1] * above[0] + cross * above[1]
    lower = lower[0] + lower[1] * below[0] + cross * below[1]
    total = squeezed(lower + fall * upper, SUM_BASE, SUM_SCALE)
    upper = squeezed(upper, SUM_BASE, SUM_SCALE)
    for peer in range(out_ref.shape[0]):
        put_sum(out_ref, peer, 0, jnp.where(info_ref[64] // 2 == peer // 2, upper, total))


def third_body(
    info_ref, rec_ref, seed_ref, one_ref, lt_ref, lr_ref, sides_ref, length_ref, face_ref,
    mine_ref, got_ref, new_lt_ref, new_lr_ref, flux_ref, near_out, far_out, left_out, right_out,
    scratch,
):
    layers, azimuths, radials = lr_ref.shape
    decay, _, _ = powers(length_ref[...])
    one, two = restored(info_ref, mine_ref, got_ref, scratch)
    before = [one_ref[layer] for layer in range(layers)]
    lt = [lt_ref[layer + 1] for layer in range(layers)]
    lr = [lr_ref[layer] for layer in range(layers)]
    climbs, _ = chain(lr, decay, one)
    lr = [
        -0.3 * before[l]
        + (1.0 + 0.2 * decoded(info_ref, rec_ref, 2, l, 0)) * lr[l]
        + climbs[l]
        for l in range(layers)
    ]
    sides = sides_ref[...]
    spread = laplace(lt, lt_ref[0], lt_ref[layers + 1], sides[:layers], sides[layers:])
    new_lt = [
        lt[l] + 0.15 * spread[l] + decoded(info_ref, rec_ref, 1, l, 1) * lr[l]
        for l in range(layers)
    ]
    upper_here = info_ref[64] % 2 == 1
    near_out[...] = jnp.where(upper_here, new_lt[0], new_lt[-1])
    far_out[...] = jnp.where(upper_here, new_lt[-1], new_lt[0])
    for l in range(layers):
        left_out[l : l + 1, :] = new_lt[l][0:1, :]
        right_out[l : l + 1, :] = new_lt[l][azimuths - 1 : azimuths, :]
    climbs, _ = chain(lr, decay, two)
    for l in range(layers):
        new_lt_ref[l] = new_lt[l]
        new_lr_ref[l] = (
            -0.3 * lt[l] + (1.0 + 0.2 * decoded(info_ref, rec_ref, 1, l, 0)) * lr[l] + climbs[l]
        )
    lane = lax.broadcasted_iota(jnp.int32, (azimuths, radials), 1)
    ones = jnp.ones((8, radials), jnp.float32)
    for l in range(layers):
        kept = jnp.where(
            lane == face_ref[l], (seed_ref[l] + before[l]) + (lt[l] + new_lt[l]), 0.0
        )
        row = lax.dot_general(
            ones,
            kept,
            (((1,), (1,)), ((), ())),
            precision=lax.Precision.HIGHEST,
            preferred_element_type=jnp.float32,
        )[0:1, :]
        twice = jnp.concatenate([row, row], axis=1)
        flux_ref[l : l + 1, :] = twice
        left_out[layers + l : layers + l + 1, :] = twice
        right_out[layers + l : layers + l + 1, :] = twice


def last_body(
    info_ref, weight_ref, rec_ref, lt_ref, lr_ref, near_ref, far_ref, left_ref, right_ref,
    length_ref, sums_ref, flux_ref, new_lt_ref, new_lr_ref, heat_ref,
):
    layers, azimuths, radials = lt_ref.shape
    band = weight_ref.shape[0] // 2
    decay, fall, _ = powers(length_ref[...])
    chips = sums_ref.shape[0] // 2
    here = info_ref[64] // 2

    per = sums_ref.shape[1]

    def total_of(chip):
        return jnp.concatenate(
            [got_sum(sums_ref, 2 * chip + core, 0, per) for core in range(2)], axis=0
        )

    above = lax.fori_loop(
        0,
        chips - 1 - here,
        lambda k, value: fall * fall * value + total_of(chips - 1 - k),
        jnp.zeros_like(fall),
    )
    three = jnp.where(info_ref[64] % 2 == 1, above, fall * above + total_of(here))
    lt = [lt_ref[layer] for layer in range(layers)]
    lr = [lr_ref[layer] for layer in range(layers)]
    end = jnp.logical_or(info_ref[64] == 0, info_ref[64] == info_ref[65] - 1)
    near, far = near_ref[...], jnp.where(end, 0.0, far_ref[...])
    upper_here = info_ref[64] % 2 == 1
    low, high = jnp.where(upper_here, near, far), jnp.where(upper_here, far, near)
    spread = laplace(lt, low, high, left_ref[...], right_ref[...])
    climbs, _ = chain(lr, decay, three)
    for l in range(layers):
        new_lt_ref[l] = lt[l] + 0.15 * spread[l] + decoded(info_ref, rec_ref, 0, l, 1) * lr[l]
        new_lr_ref[l] = (
            -0.3 * lt[l]
            + (1.0 + 0.2 * decoded(info_ref, rec_ref, 0, l, 0)) * lr[l]
            + climbs[l]
        )
    lane = lax.broadcasted_iota(jnp.int32, (layers, radials), 1)
    ring = jnp.where(
        lane < azimuths,
        flux_ref[...],
        jnp.where(
            lane < azimuths + band,
            right_ref[layers : 2 * layers, :],
            left_ref[layers : 2 * layers, :],
        ),
    )
    heat = jnp.zeros_like(ring)
    for offset in range(-band, band + 1):
        heat = heat + weight_ref[offset + band] * pltpu.roll(ring, (-offset) % radials, axis=1)
    heat_ref[...] = heat[:, :azimuths]


def run(body, scalars, args, shapes, scratch=(), span=1):
    smem = pl.BlockSpec(memory_space=pltpu.SMEM)
    vmem = pl.BlockSpec(memory_space=pltpu.VMEM)
    return pl.pallas_call(
        body,
        in_specs=[smem] * len(scalars) + [vmem] * len(args),
        out_specs=[vmem] * len(shapes),
        out_shape=[
            jax.ShapeDtypeStruct(shape, jnp.int16 if len(shape) == 4 else jnp.float32)
            for shape in shapes
        ],
        scratch_shapes=[pltpu.VMEM(shape, jnp.float32) for shape in scratch],
        compiler_params=pltpu.CompilerParams(vmem_limit_bytes=STEP_VMEM),
        cost_estimate=pl.CostEstimate(
            flops=span * SPAN_FLOPS, bytes_accessed=span * SPAN_BYTES, transcendentals=0
        ),
    )(*scalars, *args)


def turned(value, axis, shift):
    count = lax.axis_size(axis)
    return lax.ppermute(value, axis, [(i, (i + shift) % count) for i in range(count)])


def exchanged(low, high, left, right):
    return (
        turned(high, "axial", 1),
        turned(low, "axial", -1),
        turned(right, "azim", 1),
        turned(left, "azim", -1),
    )


def swapped(value):
    return lax.ppermute(value, "axial", [(i, i ^ 1) for i in range(lax.axis_size("axial"))])


def crossed(value):
    axial = lax.axis_size("axial")
    return lax.ppermute(
        value, "axial", [(i, (i - 1 + 2 * (i % 2)) % axial) for i in range(axial)]
    )


def between_chips(value):
    axial = lax.axis_size("axial")
    groups = [list(range(core, axial, 2)) for core in range(2)]
    return lax.all_to_all(value, "axial", 0, 0, tiled=True, axis_index_groups=groups)


def local(stored, holder, seed_temp, seed_disloc, decay_length, face_radius, kernel):
    layers, azimuths, radials = seed_temp.shape
    axial, me = lax.axis_size("axial"), lax.axis_index("axial")
    wanted = lax.dynamic_index_in_dim(holder, me, 1, keepdims=False).reshape(-1)
    info = jnp.concatenate([wanted, jnp.stack([me, axial]).astype(jnp.int32)])
    plane = (azimuths, radials)
    side = (layers, radials)
    wide = (2 * layers, radials)
    block = (layers, azimuths, radials)

    def half(count):
        return (count, azimuths // 2, radials)

    def copies(peers, count):
        return (peers, count * azimuths // (2 * ROWS), ROWS, radials)

    codes = encode(stored, seed_disloc, decay_length)
    pieces = lax.all_to_all(codes, "axial", 0, 0, tiled=True)
    halo = exchanged(
        seed_temp[0], seed_temp[layers - 1], seed_temp[:, 0], seed_temp[:, azimuths - 1]
    )
    pieces, *halo = lax.optimization_barrier((pieces, *halo))
    mine, other = run(seed_carry_body, (info,), (pieces, decay_length), [half(1)] * 2)
    lt1, lr1, source, far, keep, give = run(
        first_body,
        (info,),
        (pieces, seed_temp, seed_disloc, *halo, decay_length, mine, swapped(other)),
        [block, block, block, (3, *plane), half(2), half(8)],
        [(1, *plane), (2, *plane)],
    )
    got = swapped(give)
    far = crossed(far)
    (total,) = run(
        pair_chip_body, (info,), (keep, got, decay_length), [copies(axial // 2, 2)], span=CHIP_SPAN
    )
    sums = between_chips(total)
    lt2, left, right = run(
        reach_body,
        (info,),
        (lt1, source, got, far),
        [(layers + 2, *plane), (16, radials), (16, radials)],
        span=REACH_SPAN,
    )
    before, after = turned(right, "azim", 1), turned(left, "azim", -1)
    lt2, sides, more, give = run(
        second_body,
        (info,),
        (pieces, lt1, lr1, lt2, left, right, before, after, decay_length),
        [(layers + 2, *plane), wide, half(2), half(2)],
        [(2, *plane)],
    )
    more_got = swapped(give)
    sums, more_got = lax.optimization_barrier((sums, more_got))
    mine, other, total = run(
        pair_carry_body,
        (info,),
        (keep, got, more, more_got, sums, decay_length),
        [half(2), half(2), copies(axial, 1)],
    )
    sums = lax.all_to_all(total, "axial", 0, 0, tiled=True)
    lt3, lr3, flux, near, far, left, right = run(
        third_body,
        (info,),
        (
            pieces, seed_temp, lt1, lt2, lr1, sides, decay_length, face_radius[:, :, None],
            mine, swapped(other),
        ),
        [block, block, side, plane, plane, wide, wide],
        [(2, *plane)],
        span=THIRD_SPAN,
    )
    halo = (
        swapped(near),
        crossed(far),
        turned(right, "azim", 1),
        turned(left, "azim", -1),
    )
    return tuple(
        run(
            last_body,
            (info, kernel),
            (pieces, lt3, lr3, *halo, decay_length, sums, flux),
            [block, block, (layers, azimuths)],
        )
    )


def solution(mesh):
    in_specs = (
        P(None, "axial", "azim", None, None, None, None),
        P(),
        P("axial", "azim", None),
        P("axial", "azim", None),
        P("azim", None),
        P("axial", "azim"),
        P(),
    )
    out_specs = (P("axial", "azim", None), P("axial", "azim", None), P("axial", "azim"))
    return jax.shard_map(local, mesh=mesh, in_specs=in_specs, out_specs=out_specs, check_vma=False)
```

```python
import jax
import jax.numpy as jnp
from jax import lax
from jax.experimental import pallas as pl
from jax.experimental.pallas import tpu as pltpu
from jax.sharding import PartitionSpec as P

ROWS = 16
LANES = 128
RATE_MID = 3.7
RATE_SCALE = 10500.0
COEF_SCALE = 1374.0
COEF_BASE = 23.0
SEED_SCALE = 1023.0
SEED_BASE = 31.0
SUM_SCALE = 728.0
SUM_BASE = 36.0
ENCODE_VMEM = 60 * 1024 * 1024
STEP_VMEM = 16 * 1024 * 1024
SPAN_FLOPS = 1_000_000_000
SPAN_BYTES = 3_000_000
CHIP_SPAN = 50
REACH_SPAN = 100
THIRD_SPAN = 100


def squeezed(value, base, scale):
    size = jnp.log2(jnp.maximum(jnp.abs(value), 2.0**-base))
    size = size * scale + (base * scale + 0.5)
    return jnp.where(value < 0.0, -size, size).astype(jnp.int32)


def spread_out(code, base, scale):
    code = code.astype(jnp.int32).astype(jnp.float32)
    size = jnp.exp2(jnp.abs(code) * (1.0 / scale) - base)
    return jnp.where(code > 0.0, size, jnp.where(code < 0.0, -size, 0.0))


def encode_body(
    stored_ref, seed_ref, length_ref, out_ref, pieces, seed, length, codes, in_sems, more_sems,
    out_sems,
):
    steps, slots = stored_ref.shape[:2]
    owners = out_ref.shape[0]
    cap = slots // owners
    rows = 8 * ROWS
    first = [
        pltpu.make_async_copy(seed_ref, seed, more_sems.at[0]),
        pltpu.make_async_copy(length_ref, length, more_sems.at[1]),
    ]
    half_way = steps // 2
    cuts = [*range(half_way), half_way, steps]
    arrivals = {
        start: pltpu.make_async_copy(
            stored_ref.at[pl.ds(start, end - start)],
            pieces.at[pl.ds(start, end - start)],
            in_sems.at[start],
        )
        for start, end in zip(cuts[:-1], cuts[1:])
    }
    for copy in [*first, *arrivals.values()]:
        copy.start()
    row = lax.broadcasted_iota(jnp.int32, (rows, rows), 0)
    column = lax.broadcasted_iota(jnp.int32, (rows, rows), 1)
    picked = (row % ROWS) * 8 + row // ROWS == column
    order = jnp.where(picked, 1.0, 0.0).astype(jnp.bfloat16)
    for copy in first:
        copy.wait()
    decay, _, _ = powers(length[...])
    field = [seed[layer] for layer in range(seed.shape[0])]
    _, total = chain(field, decay, jnp.zeros_like(decay))
    total = squeezed(total, SEED_BASE, SEED_SCALE).astype(jnp.int16)
    per = 2 * cap
    half = total.shape[0] // 2
    for owner in range(owners):
        for block in range(half // ROWS):
            top = half * (owner % 2) + ROWS * block
            codes[owner, steps * per + block] = total[top : top + ROWS, :]

    def mixed(step, slot):
        cells = pieces[step, slot].astype(jnp.float32)
        return jnp.concatenate(
            [cells[:, LANES * r : LANES * (r + 1)] for r in range(ROWS)], axis=0
        ).astype(jnp.bfloat16)

    departures = []

    def depart(start, count):
        copy = pltpu.make_async_copy(
            codes.at[:, pl.ds(start, count)],
            out_ref.at[:, pl.ds(start, count)],
            out_sems.at[len(departures)],
        )
        copy.start()
        departures.append(copy)

    for step in range(steps):
        if step in arrivals:
            arrivals[step].wait()
        for slot in range(0, slots, cap):
            both = jnp.concatenate([mixed(step, slot + c) for c in range(cap)], axis=1)
            parts = jnp.dot(order, both, preferred_element_type=jnp.float32)

            def part(index):
                return parts[ROWS * index : ROWS * (index + 1), :]

            squares = part(1) * part(1)
            for index in range(2, 7):
                squares = squares + part(index) * part(index)
            slope = jnp.tanh(part(0))
            total = 1.0 + squares * (1.0 / 6.0)
            rate = total * lax.rsqrt(total) * jnp.exp(0.5 * slope)
            coef = (0.1 * part(7)) * rate * (1.0 - slope * slope)
            coef_code = squeezed(coef, COEF_BASE, COEF_SCALE).astype(jnp.int16)
            rate_code = jnp.round((rate - RATE_MID) * RATE_SCALE)
            rate_code = rate_code.astype(jnp.int32).astype(jnp.int16)
            for c in range(cap):
                lanes = slice(LANES * c, LANES * (c + 1))
                codes[slot // cap, per * step + 2 * c] = rate_code[:, lanes]
                codes[slot // cap, per * step + 2 * c + 1] = coef_code[:, lanes]
        if step + 1 == half_way:
            depart(0, per * half_way)
    depart(per * half_way, out_ref.shape[1] - per * half_way)
    for copy in departures:
        copy.wait()


def encode(stored, seed, length):
    steps, _, _, owners, cap, comps, cells = stored.shape
    flat = stored.reshape(steps, owners * cap, comps, cells)
    shape = (owners, steps * cap * 2 + seed.shape[1] // (2 * ROWS), ROWS, LANES)
    return pl.pallas_call(
        encode_body,
        in_specs=[pl.BlockSpec(memory_space=pl.ANY)] * 3,
        out_specs=pl.BlockSpec(memory_space=pl.ANY),
        out_shape=jax.ShapeDtypeStruct(shape, jnp.int16),
        scratch_shapes=[
            pltpu.VMEM(flat.shape, jnp.bfloat16),
            pltpu.VMEM(seed.shape, jnp.float32),
            pltpu.VMEM(length.shape, jnp.float32),
            pltpu.VMEM(shape, jnp.int16),
            pltpu.SemaphoreType.DMA((steps,)),
            pltpu.SemaphoreType.DMA((2,)),
            pltpu.SemaphoreType.DMA((steps + 1,)),
        ],
        compiler_params=pltpu.CompilerParams(vmem_limit_bytes=ENCODE_VMEM),
    )(flat, seed, length)


def decoded(info_ref, rec_ref, step, layer, field):
    pieces = []
    for quarter in range(4):
        held = info_ref[16 * step + 4 * layer + quarter]
        code = rec_ref[held // 2, 4 * step + 2 * (held % 2) + field]
        if field == 0:
            code = code.astype(jnp.int32).astype(jnp.float32)
            pieces.append(code * (1.0 / RATE_SCALE) + RATE_MID)
        else:
            pieces.append(spread_out(code, COEF_BASE, COEF_SCALE))
    return jnp.concatenate(pieces, axis=0)


def halos(info_ref, low_ref, high_ref, left_ref, right_ref):
    low = jnp.where(info_ref[64] == 0, 0.0, low_ref[...])
    high = jnp.where(info_ref[64] == info_ref[65] - 1, 0.0, high_ref[...])
    return low, high, left_ref[...], right_ref[...]


def radial(x):
    lane = lax.broadcasted_iota(jnp.int32, x.shape, 1)
    inner = jnp.where(lane == 0, 0.0, pltpu.roll(x, 1, axis=1))
    outer = jnp.where(lane == x.shape[1] - 1, 0.0, pltpu.roll(x, x.shape[1] - 1, axis=1))
    return inner + outer


def laplace(field, low, high, left=None, right=None):
    layers = len(field)
    azimuths = field[0].shape[0]
    row = lax.broadcasted_iota(jnp.int32, field[0].shape, 0)
    out = []
    for layer in range(layers):
        x = field[layer]
        below = low if layer == 0 else field[layer - 1]
        above = high if layer == layers - 1 else field[layer + 1]
        first = 0.0 if left is None else left[layer : layer + 1, :]
        last = 0.0 if right is None else right[layer : layer + 1, :]
        before = jnp.where(row == 0, first, pltpu.roll(x, 1, axis=0))
        after = jnp.where(row == azimuths - 1, last, pltpu.roll(x, azimuths - 1, axis=0))
        out.append(((below + above) + (before + after)) + radial(x) - 6.0 * x)
    return out


def chain(field, decay, carry):
    layers = len(field)
    out = [None] * layers
    for layer in reversed(range(layers)):
        out[layer] = carry
        carry = decay * carry + (1.0 - decay) * field[layer]
    return out, carry


def put_edges(field, low_ref, high_ref, left_ref, right_ref):
    layers = len(field)
    azimuths = field[0].shape[0]
    low_ref[...] = field[0]
    high_ref[...] = field[-1]
    for layer in range(layers):
        left_ref[layer : layer + 1, :] = field[layer][0:1, :]
        right_ref[layer : layer + 1, :] = field[layer][azimuths - 1 : azimuths, :]


def powers(length):
    decay = jnp.exp(-1.0 / length)
    cube = decay * decay * decay
    return decay, decay * cube, 4.0 * (1.0 - decay) * cube


def half_powers(info_ref, length_ref):
    half = length_ref.shape[0] // 2
    return powers(length_ref[pl.ds(half * (info_ref[64] % 2), half), :])


def halves(info_ref, values, scratch, keep_ref, give_ref):
    mine = info_ref[64] % 2
    half = scratch.shape[1] // 2
    for index, value in enumerate(values):
        scratch[index] = value
    for index in range(len(values)):
        keep_ref[index] = scratch[index, pl.ds(half * mine, half), :]
        give_ref[index] = scratch[index, pl.ds(half * (1 - mine), half), :]


def restored(info_ref, mine_ref, got_ref, scratch):
    mine = info_ref[64] % 2
    half = scratch.shape[1] // 2
    count = scratch.shape[0]
    for index in range(count):
        scratch[index, pl.ds(half * mine, half), :] = mine_ref[index]
        scratch[index, pl.ds(half * (1 - mine), half), :] = got_ref[index]
    return [scratch[index] for index in range(count)]


def cores(info_ref, keep_ref, got_ref):
    upper_here = info_ref[64] % 2 == 1
    own = [keep_ref[index] for index in range(keep_ref.shape[0])]
    other = [got_ref[index] for index in range(len(own))]
    upper = [jnp.where(upper_here, a, b) for a, b in zip(own, other)]
    lower = [jnp.where(upper_here, b, a) for a, b in zip(own, other)]
    return upper, lower


def share_out(info_ref, upper, lower, mine_ref, other_ref):
    upper_here = info_ref[64] % 2 == 1
    for index, (a, b) in enumerate(zip(upper, lower)):
        mine_ref[index] = jnp.where(upper_here, a, b)
        other_ref[index] = jnp.where(upper_here, b, a)


def applied(carry, here, fall, cross):
    out = [sums + fall * value for value, sums in zip(carry, here)]
    if len(carry) > 1:
        out[1] = out[1] + cross * carry[0]
    return tuple(out)


def put_sum(out_ref, at, start, code):
    code = code.astype(jnp.int16)
    for block in range(code.shape[0] // ROWS):
        out_ref[at, start + block] = code[ROWS * block : ROWS * (block + 1), :]


def got_sum(sums_ref, at, start, count):
    code = [sums_ref[at, start + block] for block in range(count)]
    return jnp.concatenate([spread_out(part, SUM_BASE, SUM_SCALE) for part in code], axis=0)


def climbed(info_ref, sums_ref, fall, cross):
    chips, blocks = sums_ref.shape[:2]
    per = fall.shape[0] // ROWS
    count = blocks // per
    total = (jnp.zeros_like(fall),) * count
    for chip in reversed(range(1, chips)):
        here = [got_sum(sums_ref, chip, per * index, per) for index in range(count)]
        new = applied(total, here, fall * fall, 2.0 * fall * cross)
        inside = chip > info_ref[64] // 2
        total = tuple(jnp.where(inside, a, b) for a, b in zip(new, total))
    return total


def answered(gain, share, decay):
    climbs, _ = chain(share, decay, jnp.zeros_like(decay))
    return [g * s + c for g, s, c in zip(gain, share, climbs)]


def seed_carry_body(info_ref, rec_ref, length_ref, mine_ref, other_ref):
    _, fall, _ = half_powers(info_ref, length_ref)
    peers, blocks = rec_ref.shape[:2]
    count = fall.shape[0] // ROWS

    def total_of(peer):
        code = [rec_ref[peer, blocks - count + block] for block in range(count)]
        return jnp.concatenate(
            [spread_out(part, SEED_BASE, SEED_SCALE) for part in code], axis=0
        )

    upper = info_ref[64] // 2 * 2 + 1
    above = jnp.zeros_like(fall)
    for peer in reversed(range(2, peers)):
        above = jnp.where(peer > upper, fall * above + total_of(peer), above)
    below = fall * above + total_of(upper)
    share_out(info_ref, (above,), (below,), mine_ref, other_ref)


def first_body(
    info_ref, rec_ref, lt_ref, lr_ref, low_ref, high_ref, left_ref, right_ref, length_ref,
    mine_ref, got_ref, new_lt_ref, new_lr_ref, source_ref, far_ref, keep_ref, give_ref,
    carried, scratch,
):
    layers = lt_ref.shape[0]
    decay, _, _ = powers(length_ref[...])
    (zero,) = restored(info_ref, mine_ref, got_ref, carried)
    lt = [lt_ref[layer] for layer in range(layers)]
    lr = [lr_ref[layer] for layer in range(layers)]
    spread = laplace(lt, *halos(info_ref, low_ref, high_ref, left_ref, right_ref))
    new_lt = [
        lt[l] + 0.15 * spread[l] + decoded(info_ref, rec_ref, 3, l, 1) * lr[l]
        for l in range(layers)
    ]
    climbs, _ = chain(lr, decay, zero)
    lr = [
        -0.3 * lt[l] + (1.0 + 0.2 * decoded(info_ref, rec_ref, 3, l, 0)) * lr[l] + climbs[l]
        for l in range(layers)
    ]
    source = [decoded(info_ref, rec_ref, 2, l, 1) * lr[l] for l in range(layers)]
    half = decay.shape[0] // 2
    up, down = (new_lt[-2], new_lt[-1], source[-1]), (new_lt[0], new_lt[1], source[0])
    upper_here = info_ref[64] % 2 == 1
    for index in range(3):
        far_ref[index] = jnp.where(upper_here, up[index], down[index])
        near = jnp.where(upper_here, down[index], up[index])
        give_ref[2 + 2 * index] = near[:half]
        give_ref[3 + 2 * index] = near[half:]
    for l in range(layers):
        give_ref[8, l : l + 1, :] = new_lt[l][0:1, :]
        give_ref[8, layers + l : layers + l + 1, :] = new_lt[l][2 * half - 1 : 2 * half, :]
    nothing = jnp.zeros_like(decay)
    _, now = chain(lr, decay, nothing)
    gain = [1.0 + 0.2 * decoded(info_ref, rec_ref, 2, l, 0) for l in range(layers)]
    after = [a - 0.3 * new_lt[l] for l, a in enumerate(answered(gain, lr, decay))]
    _, later = chain(after, decay, nothing)
    halves(info_ref, (now, later), scratch, keep_ref, give_ref)
    for l in range(layers):
        new_lt_ref[l] = new_lt[l]
        new_lr_ref[l] = lr[l]
        source_ref[l] = source[l]


def pair_chip_body(info_ref, keep_ref, got_ref, length_ref, out_ref):
    _, fall, cross = half_powers(info_ref, length_ref)
    upper, lower = cores(info_ref, keep_ref, got_ref)
    total = applied(upper, lower, fall, cross)
    total = [squeezed(value, SUM_BASE, SUM_SCALE) for value in total]
    per = fall.shape[0] // ROWS
    for chip in range(out_ref.shape[0]):
        for index, value in enumerate(total):
            put_sum(out_ref, chip, per * index, value)


def reach_body(
    info_ref, rec_ref, lt_ref, lr_ref, source_ref, near_ref, far_ref, length_ref,
    new_lt_ref, left_out, right_out, keep_ref, give_ref, scratch,
):
    layers, azimuths, _ = lt_ref.shape
    bottom = info_ref[64] == 0
    top = info_ref[64] == info_ref[65] - 1
    upper_here = info_ref[64] % 2 == 1
    low, high = [], []
    for index in range(3):
        near = jnp.concatenate([near_ref[2 + 2 * index], near_ref[3 + 2 * index]], axis=0)
        far = jnp.where(jnp.logical_or(bottom, top), 0.0, far_ref[index])
        low.append(jnp.where(upper_here, near, far))
        high.append(jnp.where(upper_here, far, near))
    lt = [low[1], *[lt_ref[l] for l in range(layers)], high[0]]
    source = [low[2], *[source_ref[l] for l in range(layers)], high[2]]
    spread = laplace(lt, low[0], high[1])
    new_lt = [lt[l] + 0.15 * spread[l] + source[l] for l in range(layers + 2)]
    new_lt[0] = jnp.where(bottom, 0.0, new_lt[0])
    new_lt[-1] = jnp.where(top, 0.0, new_lt[-1])
    sides = ((left_out, 0, 1, 0), (right_out, azimuths - 1, azimuths - 2, layers))
    for out, edge, inside, other in sides:
        for l in range(layers + 2):
            out[l : l + 1, :] = lt[l][edge : edge + 1, :]
        out[layers + 2 : layers + 4, :] = jnp.zeros_like(out[layers + 2 : layers + 4, :])
        for l in range(layers):
            out[8 + l : 9 + l, :] = lt[l + 1][inside : inside + 1, :]
            out[12 + l : 13 + l, :] = source[l + 1][edge : edge + 1, :]
        out[16:20, :] = near_ref[8, other : other + layers, :]
        out[20:24, :] = jnp.zeros_like(out[20:24, :])
    for l in range(layers + 2):
        new_lt_ref[l] = new_lt[l]
    new_lt = new_lt[1:-1]
    decay, _, _ = powers(length_ref[...])
    nothing = jnp.zeros_like(decay)
    one = [1.0 + 0.2 * decoded(info_ref, rec_ref, 2, l, 0) for l in range(layers)]
    two = [1.0 + 0.2 * decoded(info_ref, rec_ref, 1, l, 0) for l in range(layers)]
    lr = [lr_ref[layer] for layer in range(layers)]
    lr = [a - 0.3 * lt_ref[l] for l, a in enumerate(answered(one, lr, decay))]
    lr = [a - 0.3 * new_lt[l] for l, a in enumerate(answered(two, lr, decay))]
    _, later = chain(lr, decay, nothing)
    share = [None] * layers
    power = jnp.ones_like(decay)
    for layer in reversed(range(layers)):
        share[layer] = power
        power = decay * power
    _, weight = chain(answered(two, share, decay), decay, nothing)
    halves(info_ref, (later, weight), scratch, keep_ref, give_ref)


def beyond(there, here):
    middle = there[1:5]
    total = (there[0:4] + there[2:6]) + (there[8:12] + here[1:5]) + radial(middle)
    return middle + 0.15 * (total - 6.0 * middle) + there[12:16]


def pair_carry_body(
    info_ref, keep_ref, got_ref, more_ref, more_got_ref, sums_ref, left_ref, right_ref,
    length_ref, mine_ref, other_ref, out_ref,
):
    _, fall, cross = half_powers(info_ref, length_ref)
    above = climbed(info_ref, sums_ref, fall, cross)
    upper, _ = cores(info_ref, keep_ref, got_ref)
    below = applied(above, upper, fall, cross)
    share_out(info_ref, above, below, mine_ref, other_ref)
    upper, lower = cores(info_ref, more_ref, more_got_ref)
    upper = upper[0] + upper[1] * above[0] + cross * above[1]
    lower = lower[0] + lower[1] * below[0] + cross * below[1]
    upper_here = info_ref[64] % 2 == 1
    end = length_ref.shape[0] - 1
    beside = jnp.where(upper_here, right_ref[...], left_ref[...])
    decay, _, _ = powers(jnp.where(upper_here, length_ref[end:, :], length_ref[0:1, :]))
    row = lax.broadcasted_iota(jnp.int32, fall.shape, 0)
    edge = row == jnp.where(upper_here, fall.shape[0] - 1, 0)
    weight = (-0.3 * 0.15) * (1.0 - decay)
    own, other = jnp.zeros_like(decay), jnp.zeros_like(decay)
    for layer in range(4):
        own = own + weight * beside[1 + layer : 2 + layer, :]
        other = other + weight * beside[16 + layer : 17 + layer, :]
        weight = weight * decay
    upper = upper + jnp.where(edge, jnp.where(upper_here, own, other), 0.0)
    lower = lower + jnp.where(edge, jnp.where(upper_here, other, own), 0.0)
    total = squeezed(lower + fall * upper, SUM_BASE, SUM_SCALE)
    upper = squeezed(upper, SUM_BASE, SUM_SCALE)
    for peer in range(out_ref.shape[0]):
        put_sum(out_ref, peer, 0, jnp.where(info_ref[64] // 2 == peer // 2, upper, total))


def third_body(
    info_ref, rec_ref, seed_ref, one_ref, lt_ref, lr_ref, own_left_ref, own_right_ref,
    left_ref, right_ref, length_ref, face_ref,
    mine_ref, got_ref, new_lt_ref, new_lr_ref, flux_ref, near_out, far_out, left_out, right_out,
    scratch,
):
    layers, azimuths, radials = lr_ref.shape
    decay, _, _ = powers(length_ref[...])
    one, two = restored(info_ref, mine_ref, got_ref, scratch)
    before = [one_ref[layer] for layer in range(layers)]
    left, right = left_ref[...], right_ref[...]
    row = lax.broadcasted_iota(jnp.int32, (azimuths, radials), 0)
    full = []
    for l in range(layers + 2):
        missing = jnp.where(
            row == 0,
            left[l : l + 1, :],
            jnp.where(row == azimuths - 1, right[l : l + 1, :], 0.0),
        )
        full.append(lt_ref[l] + 0.15 * missing)
    lt = full[1:-1]
    lr = [lr_ref[layer] for layer in range(layers)]
    climbs, _ = chain(lr, decay, one)
    lr = [
        -0.3 * before[l]
        + (1.0 + 0.2 * decoded(info_ref, rec_ref, 2, l, 0)) * lr[l]
        + climbs[l]
        for l in range(layers)
    ]
    spread = laplace(
        lt,
        full[0],
        full[-1],
        beyond(left, own_left_ref[...]),
        beyond(right, own_right_ref[...]),
    )
    new_lt = [
        lt[l] + 0.15 * spread[l] + decoded(info_ref, rec_ref, 1, l, 1) * lr[l]
        for l in range(layers)
    ]
    upper_here = info_ref[64] % 2 == 1
    near_out[...] = jnp.where(upper_here, new_lt[0], new_lt[-1])
    far_out[...] = jnp.where(upper_here, new_lt[-1], new_lt[0])
    for l in range(layers):
        left_out[l : l + 1, :] = new_lt[l][0:1, :]
        right_out[l : l + 1, :] = new_lt[l][azimuths - 1 : azimuths, :]
    climbs, _ = chain(lr, decay, two)
    for l in range(layers):
        new_lt_ref[l] = new_lt[l]
        new_lr_ref[l] = (
            -0.3 * lt[l] + (1.0 + 0.2 * decoded(info_ref, rec_ref, 1, l, 0)) * lr[l] + climbs[l]
        )
    lane = lax.broadcasted_iota(jnp.int32, (azimuths, radials), 1)
    ones = jnp.ones((8, radials), jnp.float32)
    for l in range(layers):
        kept = jnp.where(
            lane == face_ref[l], (seed_ref[l] + before[l]) + (lt[l] + new_lt[l]), 0.0
        )
        line = lax.dot_general(
            ones,
            kept,
            (((1,), (1,)), ((), ())),
            precision=lax.Precision.HIGHEST,
            preferred_element_type=jnp.float32,
        )[0:1, :]
        twice = jnp.concatenate([line, line], axis=1)
        flux_ref[l : l + 1, :] = twice
        left_out[layers + l : layers + l + 1, :] = twice
        right_out[layers + l : layers + l + 1, :] = twice


def last_body(
    info_ref, weight_ref, rec_ref, lt_ref, lr_ref, near_ref, far_ref, left_ref, right_ref,
    length_ref, sums_ref, flux_ref, new_lt_ref, new_lr_ref, heat_ref,
):
    layers, azimuths, radials = lt_ref.shape
    band = weight_ref.shape[0] // 2
    decay, fall, _ = powers(length_ref[...])
    chips = sums_ref.shape[0] // 2
    here = info_ref[64] // 2

    per = sums_ref.shape[1]

    def total_of(chip):
        return jnp.concatenate(
            [got_sum(sums_ref, 2 * chip + core, 0, per) for core in range(2)], axis=0
        )

    above = jnp.zeros_like(fall)
    for chip in reversed(range(1, chips)):
        above = jnp.where(chip > here, fall * fall * above + total_of(chip), above)
    three = jnp.where(info_ref[64] % 2 == 1, above, fall * above + total_of(here))
    lt = [lt_ref[layer] for layer in range(layers)]
    lr = [lr_ref[layer] for layer in range(layers)]
    end = jnp.logical_or(info_ref[64] == 0, info_ref[64] == info_ref[65] - 1)
    near, far = near_ref[...], jnp.where(end, 0.0, far_ref[...])
    upper_here = info_ref[64] % 2 == 1
    low, high = jnp.where(upper_here, near, far), jnp.where(upper_here, far, near)
    spread = laplace(lt, low, high, left_ref[...], right_ref[...])
    climbs, _ = chain(lr, decay, three)
    for l in range(layers):
        new_lt_ref[l] = lt[l] + 0.15 * spread[l] + decoded(info_ref, rec_ref, 0, l, 1) * lr[l]
        new_lr_ref[l] = (
            -0.3 * lt[l]
            + (1.0 + 0.2 * decoded(info_ref, rec_ref, 0, l, 0)) * lr[l]
            + climbs[l]
        )
    lane = lax.broadcasted_iota(jnp.int32, (layers, radials), 1)
    ring = jnp.where(
        lane < azimuths,
        flux_ref[...],
        jnp.where(
            lane < azimuths + band,
            right_ref[layers : 2 * layers, :],
            left_ref[layers : 2 * layers, :],
        ),
    )
    heat = jnp.zeros_like(ring)
    for offset in range(-band, band + 1):
        heat = heat + weight_ref[offset + band] * pltpu.roll(ring, (-offset) % radials, axis=1)
    heat_ref[...] = heat[:, :azimuths]


def run(body, scalars, args, shapes, scratch=(), span=1):
    smem = pl.BlockSpec(memory_space=pltpu.SMEM)
    vmem = pl.BlockSpec(memory_space=pltpu.VMEM)
    return pl.pallas_call(
        body,
        in_specs=[smem] * len(scalars) + [vmem] * len(args),
        out_specs=[vmem] * len(shapes),
        out_shape=[
            jax.ShapeDtypeStruct(shape, jnp.int16 if len(shape) == 4 else jnp.float32)
            for shape in shapes
        ],
        scratch_shapes=[pltpu.VMEM(shape, jnp.float32) for shape in scratch],
        compiler_params=pltpu.CompilerParams(vmem_limit_bytes=STEP_VMEM),
        cost_estimate=pl.CostEstimate(
            flops=span * SPAN_FLOPS, bytes_accessed=span * SPAN_BYTES, transcendentals=0
        ),
    )(*scalars, *args)


def turned(value, axis, shift):
    count = lax.axis_size(axis)
    return lax.ppermute(value, axis, [(i, (i + shift) % count) for i in range(count)])


def exchanged(low, high, left, right):
    return (
        turned(high, "axial", 1),
        turned(low, "axial", -1),
        turned(right, "azim", 1),
        turned(left, "azim", -1),
    )


def swapped(value):
    return lax.ppermute(value, "axial", [(i, i ^ 1) for i in range(lax.axis_size("axial"))])


def crossed(value):
    axial = lax.axis_size("axial")
    return lax.ppermute(
        value, "axial", [(i, (i - 1 + 2 * (i % 2)) % axial) for i in range(axial)]
    )


def between_chips(value):
    axial = lax.axis_size("axial")
    groups = [list(range(core, axial, 2)) for core in range(2)]
    return lax.all_to_all(value, "axial", 0, 0, tiled=True, axis_index_groups=groups)


def local(stored, holder, seed_temp, seed_disloc, decay_length, face_radius, kernel):
    layers, azimuths, radials = seed_temp.shape
    axial, me = lax.axis_size("axial"), lax.axis_index("axial")
    wanted = lax.dynamic_index_in_dim(holder, me, 1, keepdims=False).reshape(-1)
    info = jnp.concatenate([wanted, jnp.stack([me, axial]).astype(jnp.int32)])
    plane = (azimuths, radials)
    side = (layers, radials)
    wide = (2 * layers, radials)
    block = (layers, azimuths, radials)

    def half(count):
        return (count, azimuths // 2, radials)

    def copies(peers, count):
        return (peers, count * azimuths // (2 * ROWS), ROWS, radials)

    codes = encode(stored, seed_disloc, decay_length)
    pieces = lax.all_to_all(codes, "axial", 0, 0, tiled=True)
    halo = exchanged(
        seed_temp[0], seed_temp[layers - 1], seed_temp[:, 0], seed_temp[:, azimuths - 1]
    )
    pieces, *halo = lax.optimization_barrier((pieces, *halo))
    mine, other = run(seed_carry_body, (info,), (pieces, decay_length), [half(1)] * 2)
    lt1, lr1, source, far, keep, give = run(
        first_body,
        (info,),
        (pieces, seed_temp, seed_disloc, *halo, decay_length, mine, swapped(other)),
        [block, block, block, (3, *plane), half(2), half(9)],
        [(1, *plane), (2, *plane)],
    )
    got = swapped(give)
    far = crossed(far)
    (total,) = run(
        pair_chip_body, (info,), (keep, got, decay_length), [copies(axial // 2, 2)], span=CHIP_SPAN
    )
    sums = between_chips(total)
    lt2, left, right, more, give = run(
        reach_body,
        (info,),
        (pieces, lt1, lr1, source, got, far, decay_length),
        [(layers + 2, *plane), (24, radials), (24, radials), half(2), half(2)],
        [(2, *plane)],
        span=REACH_SPAN,
    )
    more_got = swapped(give)
    sides = (turned(right, "azim", 1), turned(left, "azim", -1))
    sums, *sides = lax.optimization_barrier((sums, *sides))
    mine, other, total = run(
        pair_carry_body,
        (info,),
        (keep, got, more, more_got, sums, *sides, decay_length),
        [half(2), half(2), copies(axial, 1)],
    )
    sums = lax.all_to_all(total, "axial", 0, 0, tiled=True)
    lt3, lr3, flux, near, far, left, right = run(
        third_body,
        (info,),
        (
            pieces, seed_temp, lt1, lt2, lr1, left, right, *sides, decay_length,
            face_radius[:, :, None], mine, swapped(other),
        ),
        [block, block, side, plane, plane, wide, wide],
        [(2, *plane)],
        span=THIRD_SPAN,
    )
    halo = (
        swapped(near),
        crossed(far),
        turned(right, "azim", 1),
        turned(left, "azim", -1),
    )
    return tuple(
        run(
            last_body,
            (info, kernel),
            (pieces, lt3, lr3, *halo, decay_length, sums, flux),
            [block, block, (layers, azimuths)],
        )
    )


def solution(mesh):
    in_specs = (
        P(None, "axial", "azim", None, None, None, None),
        P(),
        P("axial", "azim", None),
        P("axial", "azim", None),
        P("azim", None),
        P("axial", "azim"),
        P(),
    )
    out_specs = (P("axial", "azim", None), P("axial", "azim", None), P("axial", "azim"))
    return jax.shard_map(local, mesh=mesh, in_specs=in_specs, out_specs=out_specs, check_vma=False)
```

```python
import jax
import jax.numpy as jnp
from jax import lax
from jax.experimental import pallas as pl
from jax.experimental.pallas import tpu as pltpu
from jax.sharding import PartitionSpec as P

ROWS = 16
LANES = 128
RATE_MID = 3.7
RATE_SCALE = 10500.0
COEF_SCALE = 1374.0
COEF_BASE = 23.0
SUM_SCALE = 728.0
SUM_BASE = 36.0
ENCODE_VMEM = 60 * 1024 * 1024
STEP_VMEM = 16 * 1024 * 1024
SPAN_FLOPS = 1_000_000_000
SPAN_BYTES = 3_000_000
CHIP_SPAN = 50
REACH_SPAN = 100
THIRD_SPAN = 100


def squeezed(value, base, scale):
    size = jnp.log2(jnp.maximum(jnp.abs(value), 2.0**-base))
    size = size * scale + (base * scale + 0.5)
    return jnp.where(value < 0.0, -size, size).astype(jnp.int32)


def spread_out(code, base, scale):
    code = code.astype(jnp.int32).astype(jnp.float32)
    size = jnp.exp2(jnp.abs(code) * (1.0 / scale) - base)
    return jnp.where(code > 0.0, size, jnp.where(code < 0.0, -size, 0.0))


def encode_body(stored_ref, out_ref, pieces, codes, in_sems, out_sems):
    steps, slots = stored_ref.shape[:2]
    cap = slots // out_ref.shape[0]
    rows = 8 * ROWS
    per = 2 * cap
    half_way = steps // 2
    cuts = [*range(half_way), half_way, steps]
    arrivals = {
        start: pltpu.make_async_copy(
            stored_ref.at[pl.ds(start, end - start)],
            pieces.at[pl.ds(start, end - start)],
            in_sems.at[start],
        )
        for start, end in zip(cuts[:-1], cuts[1:])
    }
    for copy in arrivals.values():
        copy.start()
    row = lax.broadcasted_iota(jnp.int32, (rows, rows), 0)
    column = lax.broadcasted_iota(jnp.int32, (rows, rows), 1)
    picked = (row % ROWS) * 8 + row // ROWS == column
    order = jnp.where(picked, 1.0, 0.0).astype(jnp.bfloat16)

    def mixed(step, slot):
        cells = pieces[step, slot].astype(jnp.float32)
        return jnp.concatenate(
            [cells[:, LANES * r : LANES * (r + 1)] for r in range(ROWS)], axis=0
        ).astype(jnp.bfloat16)

    departures = []

    def depart(start, count):
        copy = pltpu.make_async_copy(
            codes.at[:, pl.ds(start, count)],
            out_ref.at[:, pl.ds(start, count)],
            out_sems.at[len(departures)],
        )
        copy.start()
        departures.append(copy)

    for step in range(steps):
        if step in arrivals:
            arrivals[step].wait()
        for slot in range(0, slots, cap):
            both = jnp.concatenate([mixed(step, slot + c) for c in range(cap)], axis=1)
            parts = jnp.dot(order, both, preferred_element_type=jnp.float32)

            def part(index):
                return parts[ROWS * index : ROWS * (index + 1), :]

            squares = part(1) * part(1)
            for index in range(2, 7):
                squares = squares + part(index) * part(index)
            slope = jnp.tanh(part(0))
            total = 1.0 + squares * (1.0 / 6.0)
            rate = total * lax.rsqrt(total) * jnp.exp(0.5 * slope)
            coef = (0.1 * part(7)) * rate * (1.0 - slope * slope)
            coef_code = squeezed(coef, COEF_BASE, COEF_SCALE).astype(jnp.int16)
            rate_code = jnp.round((rate - RATE_MID) * RATE_SCALE)
            rate_code = rate_code.astype(jnp.int32).astype(jnp.int16)
            for c in range(cap):
                lanes = slice(LANES * c, LANES * (c + 1))
                codes[slot // cap, per * step + 2 * c] = rate_code[:, lanes]
                codes[slot // cap, per * step + 2 * c + 1] = coef_code[:, lanes]
        if step + 1 == half_way:
            depart(0, per * half_way)
    depart(per * half_way, out_ref.shape[1] - per * half_way)
    for copy in departures:
        copy.wait()


def encode(stored):
    steps, _, _, owners, cap, comps, cells = stored.shape
    flat = stored.reshape(steps, owners * cap, comps, cells)
    shape = (owners, steps * cap * 2, ROWS, LANES)
    return pl.pallas_call(
        encode_body,
        in_specs=[pl.BlockSpec(memory_space=pl.ANY)],
        out_specs=pl.BlockSpec(memory_space=pl.ANY),
        out_shape=jax.ShapeDtypeStruct(shape, jnp.int16),
        scratch_shapes=[
            pltpu.VMEM(flat.shape, jnp.bfloat16),
            pltpu.VMEM(shape, jnp.int16),
            pltpu.SemaphoreType.DMA((steps,)),
            pltpu.SemaphoreType.DMA((2,)),
        ],
        compiler_params=pltpu.CompilerParams(vmem_limit_bytes=ENCODE_VMEM),
    )(flat)


def decoded(info_ref, rec_ref, step, layer, field):
    pieces = []
    for quarter in range(4):
        held = info_ref[16 * step + 4 * layer + quarter]
        code = rec_ref[held // 2, 4 * step + 2 * (held % 2) + field]
        if field == 0:
            code = code.astype(jnp.int32).astype(jnp.float32)
            pieces.append(code * (1.0 / RATE_SCALE) + RATE_MID)
        else:
            pieces.append(spread_out(code, COEF_BASE, COEF_SCALE))
    return jnp.concatenate(pieces, axis=0)


def halos(info_ref, low_ref, high_ref, left_ref, right_ref):
    low = jnp.where(info_ref[64] == 0, 0.0, low_ref[...])
    high = jnp.where(info_ref[64] == info_ref[65] - 1, 0.0, high_ref[...])
    return low, high, left_ref[...], right_ref[...]


def radial(x):
    lane = lax.broadcasted_iota(jnp.int32, x.shape, 1)
    inner = jnp.where(lane == 0, 0.0, pltpu.roll(x, 1, axis=1))
    outer = jnp.where(lane == x.shape[1] - 1, 0.0, pltpu.roll(x, x.shape[1] - 1, axis=1))
    return inner + outer


def laplace(field, low, high, left=None, right=None):
    layers = len(field)
    azimuths = field[0].shape[0]
    row = lax.broadcasted_iota(jnp.int32, field[0].shape, 0)
    out = []
    for layer in range(layers):
        x = field[layer]
        below = low if layer == 0 else field[layer - 1]
        above = high if layer == layers - 1 else field[layer + 1]
        first = 0.0 if left is None else left[layer : layer + 1, :]
        last = 0.0 if right is None else right[layer : layer + 1, :]
        before = jnp.where(row == 0, first, pltpu.roll(x, 1, axis=0))
        after = jnp.where(row == azimuths - 1, last, pltpu.roll(x, azimuths - 1, axis=0))
        out.append(((below + above) + (before + after)) + radial(x) - 6.0 * x)
    return out


def chain(field, decay, carry):
    layers = len(field)
    out = [None] * layers
    for layer in reversed(range(layers)):
        out[layer] = carry
        carry = decay * carry + (1.0 - decay) * field[layer]
    return out, carry


def put_edges(field, low_ref, high_ref, left_ref, right_ref):
    layers = len(field)
    azimuths = field[0].shape[0]
    low_ref[...] = field[0]
    high_ref[...] = field[-1]
    for layer in range(layers):
        left_ref[layer : layer + 1, :] = field[layer][0:1, :]
        right_ref[layer : layer + 1, :] = field[layer][azimuths - 1 : azimuths, :]


def powers(length):
    decay = jnp.exp(-1.0 / length)
    cube = decay * decay * decay
    return decay, decay * cube, 4.0 * (1.0 - decay) * cube


def half_powers(info_ref, length_ref):
    half = length_ref.shape[0] // 2
    return powers(length_ref[pl.ds(half * (info_ref[64] % 2), half), :])


def halves(info_ref, values, scratch, keep_ref, give_ref):
    mine = info_ref[64] % 2
    half = scratch.shape[1] // 2
    for index, value in enumerate(values):
        scratch[index] = value
    for index in range(len(values)):
        keep_ref[index] = scratch[index, pl.ds(half * mine, half), :]
        give_ref[index] = scratch[index, pl.ds(half * (1 - mine), half), :]


def restored(info_ref, mine_ref, got_ref, scratch):
    mine = info_ref[64] % 2
    half = scratch.shape[1] // 2
    count = scratch.shape[0]
    for index in range(count):
        scratch[index, pl.ds(half * mine, half), :] = mine_ref[index]
        scratch[index, pl.ds(half * (1 - mine), half), :] = got_ref[index]
    return [scratch[index] for index in range(count)]


def cores(info_ref, keep_ref, got_ref):
    upper_here = info_ref[64] % 2 == 1
    own = [keep_ref[index] for index in range(min(4, keep_ref.shape[0]))]
    other = [got_ref[index] for index in range(len(own))]
    upper = [jnp.where(upper_here, a, b) for a, b in zip(own, other)]
    lower = [jnp.where(upper_here, b, a) for a, b in zip(own, other)]
    return upper, lower


def share_out(info_ref, upper, lower, mine_ref, other_ref):
    upper_here = info_ref[64] % 2 == 1
    for index, (a, b) in enumerate(zip(upper, lower)):
        mine_ref[index] = jnp.where(upper_here, a, b)
        other_ref[index] = jnp.where(upper_here, b, a)


def applied(carry, here, fall, cross):
    out = [sums + fall * value for value, sums in zip(carry, here)]
    if len(carry) > 1:
        out[1] = out[1] + cross * carry[0]
        out[2] = out[2] + cross * carry[1] + here[3] * carry[0]
    return tuple(out)


def put_sum(out_ref, at, start, code):
    code = code.astype(jnp.int16)
    for block in range(code.shape[0] // ROWS):
        out_ref[at, start + block] = code[ROWS * block : ROWS * (block + 1), :]


def got_sum(sums_ref, at, start, count):
    code = [sums_ref[at, start + block] for block in range(count)]
    return jnp.concatenate([spread_out(part, SUM_BASE, SUM_SCALE) for part in code], axis=0)


def answered(gain, share, decay):
    climbs, _ = chain(share, decay, jnp.zeros_like(decay))
    return [g * s + c for g, s, c in zip(gain, share, climbs)]


def shares(decay, layers):
    out = [None] * layers
    power = jnp.ones_like(decay)
    for layer in reversed(range(layers)):
        out[layer] = power
        power = decay * power
    return out


def first_body(
    info_ref, rec_ref, lt_ref, lr_ref, low_ref, high_ref, left_ref, right_ref, length_ref,
    new_lt_ref, new_lr_ref, source_ref, far_ref, keep_ref, give_ref, scratch,
):
    layers = lt_ref.shape[0]
    decay, _, _ = powers(length_ref[...])
    nothing = jnp.zeros_like(decay)
    lt = [lt_ref[layer] for layer in range(layers)]
    lr = [lr_ref[layer] for layer in range(layers)]
    low = jnp.where(info_ref[64] == 0, 0.0, low_ref[...])
    high = jnp.where(info_ref[64] == info_ref[65] - 1, 0.0, high_ref[0])
    spread = laplace(lt, low, high, left_ref[0:layers, :], right_ref[0:layers, :])
    new_lt = [
        lt[l] + 0.15 * spread[l] + decoded(info_ref, rec_ref, 3, l, 1) * lr[l]
        for l in range(layers)
    ]
    climbs, begin = chain(lr, decay, nothing)
    base = [
        -0.3 * lt[l] + (1.0 + 0.2 * decoded(info_ref, rec_ref, 3, l, 0)) * lr[l]
        for l in range(layers)
    ]
    lr = [base[l] + climbs[l] for l in range(layers)]
    gate = [decoded(info_ref, rec_ref, 2, l, 1) for l in range(layers)]
    half = decay.shape[0] // 2
    up = (new_lt[-2], new_lt[-1], gate[-1] * base[-1], gate[-1])
    down = (new_lt[0], new_lt[1], gate[0] * base[0], gate[0])
    upper_here = info_ref[64] % 2 == 1
    for index in range(4):
        far_ref[index] = jnp.where(upper_here, up[index], down[index])
        near = jnp.where(upper_here, down[index], up[index])
        give_ref[4 + 2 * index] = near[:half]
        give_ref[5 + 2 * index] = near[half:]
    for l in range(layers):
        give_ref[12, l : l + 1, :] = new_lt[l][0:1, :]
        give_ref[12, layers + l : layers + l + 1, :] = new_lt[l][2 * half - 1 : 2 * half, :]
    beyond_sums = []
    for ref in (left_ref, right_ref):
        side_decay, _, _ = powers(ref[2 * layers : 2 * layers + 1, :])
        side = [ref[layers + l : layers + l + 1, :] for l in range(layers)]
        beyond_sums.append(chain(side, side_decay, jnp.zeros_like(side_decay))[1])
    keep_ref[4] = jnp.zeros_like(keep_ref[4])
    give_ref[12, 8:, :] = jnp.zeros_like(give_ref[12, 8:, :])
    keep_ref[4, 0:1, :] = jnp.where(upper_here, beyond_sums[1], beyond_sums[0])
    give_ref[12, 8:9, :] = jnp.where(upper_here, beyond_sums[0], beyond_sums[1])
    _, now = chain(lr, decay, nothing)
    gain = [1.0 + 0.2 * decoded(info_ref, rec_ref, 2, l, 0) for l in range(layers)]
    after = [a - 0.3 * new_lt[l] for l, a in enumerate(answered(gain, lr, decay))]
    _, later = chain(after, decay, nothing)
    _, weight = chain(answered(gain, shares(decay, layers), decay), decay, nothing)
    halves(info_ref, (begin, now, later, weight), scratch, keep_ref, give_ref)
    for l in range(layers):
        new_lt_ref[l] = new_lt[l]
        new_lr_ref[l] = lr[l]
        source_ref[l] = gate[l] * lr[l]


def side_powers(info_ref, early_left_ref, early_right_ref):
    upper_here = info_ref[64] % 2 == 1
    length = jnp.where(upper_here, early_right_ref[8:9, :], early_left_ref[8:9, :])
    return powers(length)


def pair_chip_body(
    info_ref, keep_ref, got_ref, early_left_ref, early_right_ref, length_ref, out_ref,
):
    _, fall, cross = half_powers(info_ref, length_ref)
    _, side_fall, _ = side_powers(info_ref, early_left_ref, early_right_ref)
    upper, lower = cores(info_ref, keep_ref, got_ref)
    total = list(applied(upper[:3], lower, fall, cross))
    total.append(fall * (lower[3] + upper[3]) + cross * cross)
    upper_here = info_ref[64] % 2 == 1
    own, other = keep_ref[4, 0:1, :], got_ref[12, 8:9, :]
    side = jnp.where(upper_here, other, own) + side_fall * jnp.where(upper_here, own, other)
    total.append(jnp.broadcast_to(side, (ROWS, side.shape[1])))
    start = 0
    for value in total:
        code = squeezed(value, SUM_BASE, SUM_SCALE)
        for chip in range(out_ref.shape[0]):
            put_sum(out_ref, chip, start, code)
        start += value.shape[0] // ROWS


def reach_body(
    info_ref, rec_ref, lt_ref, lr_ref, source_ref, near_ref, far_ref, length_ref,
    new_lt_ref, left_out, right_out, keep_ref, give_ref, scratch,
):
    layers, azimuths, _ = lt_ref.shape
    bottom = info_ref[64] == 0
    top = info_ref[64] == info_ref[65] - 1
    upper_here = info_ref[64] % 2 == 1
    low, high = [], []
    for index in range(3):
        near = jnp.concatenate([near_ref[4 + 2 * index], near_ref[5 + 2 * index]], axis=0)
        far = jnp.where(jnp.logical_or(bottom, top), 0.0, far_ref[index])
        low.append(jnp.where(upper_here, near, far))
        high.append(jnp.where(upper_here, far, near))
    lt = [low[1], *[lt_ref[l] for l in range(layers)], high[0]]
    source = [low[2], *[source_ref[l] for l in range(layers)], high[2]]
    spread = laplace(lt, low[0], high[1])
    new_lt = [lt[l] + 0.15 * spread[l] + source[l] for l in range(layers + 2)]
    new_lt[0] = jnp.where(bottom, 0.0, new_lt[0])
    new_lt[-1] = jnp.where(top, 0.0, new_lt[-1])
    gate = [decoded(info_ref, rec_ref, 2, l, 1) for l in range(layers)]
    sides = ((left_out, 0, 1, 0), (right_out, azimuths - 1, azimuths - 2, layers))
    for out, edge, inside, other in sides:
        for l in range(layers + 2):
            out[l : l + 1, :] = lt[l][edge : edge + 1, :]
        out[layers + 2 : layers + 4, :] = jnp.zeros_like(out[layers + 2 : layers + 4, :])
        for l in range(layers):
            out[8 + l : 9 + l, :] = lt[l + 1][inside : inside + 1, :]
            out[12 + l : 13 + l, :] = source[l + 1][edge : edge + 1, :]
            out[20 + l : 21 + l, :] = gate[l][edge : edge + 1, :]
        out[16:20, :] = near_ref[12, other : other + layers, :]
    for l in range(layers + 2):
        new_lt_ref[l] = new_lt[l]
    new_lt = new_lt[1:-1]
    decay, _, _ = powers(length_ref[...])
    nothing = jnp.zeros_like(decay)
    one = [1.0 + 0.2 * decoded(info_ref, rec_ref, 2, l, 0) for l in range(layers)]
    two = [1.0 + 0.2 * decoded(info_ref, rec_ref, 1, l, 0) for l in range(layers)]
    lr = [lr_ref[layer] for layer in range(layers)]
    lr = [a - 0.3 * lt_ref[l] for l, a in enumerate(answered(one, lr, decay))]
    lr = [a - 0.3 * new_lt[l] for l, a in enumerate(answered(two, lr, decay))]
    _, later = chain(lr, decay, nothing)
    share = shares(decay, layers)
    by_zero = answered(two, answered(one, share, decay), decay)
    by_zero = [by_zero[l] - 0.3 * gate[l] * share[l] for l in range(layers)]
    _, one_weight = chain(answered(two, share, decay), decay, nothing)
    _, zero_weight = chain(by_zero, decay, nothing)
    halves(info_ref, (later, one_weight, zero_weight), scratch, keep_ref, give_ref)


def beyond(there, here):
    middle = there[1:5]
    total = (there[0:4] + there[2:6]) + (there[8:12] + here[1:5]) + radial(middle)
    return middle + 0.15 * (total - 6.0 * middle) + there[12:16]


def pair_carry_body(
    info_ref, keep_ref, got_ref, more_ref, more_got_ref, sums_ref, left_ref, right_ref,
    early_left_ref, early_right_ref, length_ref, mine_ref, other_ref, out_ref,
):
    _, fall, cross = half_powers(info_ref, length_ref)
    _, side_fall, _ = side_powers(info_ref, early_left_ref, early_right_ref)
    chips = sums_ref.shape[0]
    per = fall.shape[0] // ROWS
    above = (jnp.zeros_like(fall),) * 3
    side = jnp.zeros_like(side_fall)
    for chip in reversed(range(1, chips)):
        inside = chip > info_ref[64] // 2
        here = [got_sum(sums_ref, chip, per * index, per) for index in range(4)]
        new = applied(above, here, fall * fall, 2.0 * fall * cross)
        above = tuple(jnp.where(inside, a, b) for a, b in zip(new, above))
        new = got_sum(sums_ref, chip, 4 * per, 1)[0:1, :] + side_fall * side_fall * side
        side = jnp.where(inside, new, side)
    upper, _ = cores(info_ref, keep_ref, got_ref)
    below = applied(above, upper, fall, cross)
    share_out(info_ref, above, below, mine_ref, other_ref)
    upper_here = info_ref[64] % 2 == 1
    below_side = side_fall * side + jnp.where(
        upper_here, keep_ref[4, 0:1, :], got_ref[12, 8:9, :]
    )
    mine_ref[3] = jnp.zeros_like(fall)
    other_ref[3] = jnp.zeros_like(fall)
    mine_ref[3, 0:1, :] = jnp.where(upper_here, side, below_side)
    other_ref[3, 0:1, :] = jnp.where(upper_here, below_side, side)
    upper, lower = cores(info_ref, more_ref, more_got_ref)
    upper = upper[0] + upper[1] * above[1] + upper[2] * above[0] + cross * above[2]
    lower = lower[0] + lower[1] * below[1] + lower[2] * below[0] + cross * below[2]
    end = length_ref.shape[0] - 1
    beside = jnp.where(upper_here, right_ref[...], left_ref[...])
    decay, _, _ = powers(jnp.where(upper_here, length_ref[end:, :], length_ref[0:1, :]))
    row = lax.broadcasted_iota(jnp.int32, fall.shape, 0)
    edge = row == jnp.where(upper_here, fall.shape[0] - 1, 0)
    weight = (-0.3 * 0.15) * (1.0 - decay)
    own, other = jnp.zeros_like(decay), jnp.zeros_like(decay)
    for layer in range(4):
        own = own + weight * beside[1 + layer : 2 + layer, :]
        other = other + weight * beside[16 + layer : 17 + layer, :]
        weight = weight * decay
    upper = upper + jnp.where(edge, jnp.where(upper_here, own, other), 0.0)
    lower = lower + jnp.where(edge, jnp.where(upper_here, other, own), 0.0)
    total = squeezed(lower + fall * upper, SUM_BASE, SUM_SCALE)
    upper = squeezed(upper, SUM_BASE, SUM_SCALE)
    for peer in range(out_ref.shape[0]):
        put_sum(out_ref, peer, 0, jnp.where(info_ref[64] // 2 == peer // 2, upper, total))


def third_body(
    info_ref, rec_ref, seed_ref, seed_lr_ref, one_ref, lt_ref, lr_ref, own_left_ref,
    own_right_ref, left_ref, right_ref, near_ref, beyond_ref, high_ref, early_left_ref,
    early_right_ref, length_ref, face_ref,
    mine_ref, got_ref, new_lt_ref, new_lr_ref, flux_ref, near_out, far_out, left_out, right_out,
    scratch,
):
    layers, azimuths, radials = lr_ref.shape
    decay, _, _ = powers(length_ref[...])
    zero, one, two = restored(info_ref, mine_ref, got_ref, scratch)
    upper_here = info_ref[64] % 2 == 1
    share = shares(decay, layers)
    lift = [share[l] * zero for l in range(layers)]
    seed_lr = [seed_lr_ref[layer] for layer in range(layers)]
    _, under = chain(seed_lr, decay, zero)
    over = (zero - (1.0 - decay) * high_ref[1]) / decay
    near = jnp.concatenate([near_ref[10], near_ref[11]], axis=0)
    gate_low = jnp.where(upper_here, near, beyond_ref[3])
    gate_high = jnp.where(upper_here, beyond_ref[3], near)
    lifts = [
        jnp.where(info_ref[64] == 0, 0.0, gate_low * under),
        *[decoded(info_ref, rec_ref, 2, l, 1) * lift[l] for l in range(layers)],
        jnp.where(info_ref[64] == info_ref[65] - 1, 0.0, gate_high * over),
    ]
    mine_side, got_side = mine_ref[3, 0:1, :], got_ref[3, 0:1, :]

    def lifted(there, early_ref, side):
        side_decay, _, _ = powers(early_ref[8:9, :])
        side_share = jnp.concatenate(shares(side_decay, layers), axis=0)
        return there[20:24] * side_share * side

    before = [one_ref[layer] for layer in range(layers)]
    left, right = left_ref[...], right_ref[...]
    row = lax.broadcasted_iota(jnp.int32, (azimuths, radials), 0)
    full = []
    for l in range(layers + 2):
        missing = jnp.where(
            row == 0,
            left[l : l + 1, :],
            jnp.where(row == azimuths - 1, right[l : l + 1, :], 0.0),
        )
        full.append(lt_ref[l] + 0.15 * missing + lifts[l])
    lt = full[1:-1]
    lr = [lr_ref[layer] + lift[layer] for layer in range(layers)]
    climbs, _ = chain(lr, decay, one)
    lr = [
        -0.3 * before[l]
        + (1.0 + 0.2 * decoded(info_ref, rec_ref, 2, l, 0)) * lr[l]
        + climbs[l]
        for l in range(layers)
    ]
    spread = laplace(
        lt,
        full[0],
        full[-1],
        beyond(left, own_left_ref[...])
        + lifted(left, early_left_ref, jnp.where(upper_here, got_side, mine_side)),
        beyond(right, own_right_ref[...])
        + lifted(right, early_right_ref, jnp.where(upper_here, mine_side, got_side)),
    )
    new_lt = [
        lt[l] + 0.15 * spread[l] + decoded(info_ref, rec_ref, 1, l, 1) * lr[l]
        for l in range(layers)
    ]
    upper_here = info_ref[64] % 2 == 1
    near_out[...] = jnp.where(upper_here, new_lt[0], new_lt[-1])
    far_out[...] = jnp.where(upper_here, new_lt[-1], new_lt[0])
    for l in range(layers):
        left_out[l : l + 1, :] = new_lt[l][0:1, :]
        right_out[l : l + 1, :] = new_lt[l][azimuths - 1 : azimuths, :]
    climbs, _ = chain(lr, decay, two)
    for l in range(layers):
        new_lt_ref[l] = new_lt[l]
        new_lr_ref[l] = (
            -0.3 * lt[l] + (1.0 + 0.2 * decoded(info_ref, rec_ref, 1, l, 0)) * lr[l] + climbs[l]
        )
    lane = lax.broadcasted_iota(jnp.int32, (azimuths, radials), 1)
    ones = jnp.ones((8, radials), jnp.float32)
    for l in range(layers):
        kept = jnp.where(
            lane == face_ref[l], (seed_ref[l] + before[l]) + (lt[l] + new_lt[l]), 0.0
        )
        line = lax.dot_general(
            ones,
            kept,
            (((1,), (1,)), ((), ())),
            precision=lax.Precision.HIGHEST,
            preferred_element_type=jnp.float32,
        )[0:1, :]
        twice = jnp.concatenate([line, line], axis=1)
        flux_ref[l : l + 1, :] = twice
        left_out[layers + l : layers + l + 1, :] = twice
        right_out[layers + l : layers + l + 1, :] = twice


def last_body(
    info_ref, weight_ref, rec_ref, lt_ref, lr_ref, near_ref, far_ref, left_ref, right_ref,
    length_ref, sums_ref, flux_ref, new_lt_ref, new_lr_ref, heat_ref,
):
    layers, azimuths, radials = lt_ref.shape
    band = weight_ref.shape[0] // 2
    decay, fall, _ = powers(length_ref[...])
    chips = sums_ref.shape[0] // 2
    here = info_ref[64] // 2

    per = sums_ref.shape[1]

    def total_of(chip):
        return jnp.concatenate(
            [got_sum(sums_ref, 2 * chip + core, 0, per) for core in range(2)], axis=0
        )

    above = jnp.zeros_like(fall)
    for chip in reversed(range(1, chips)):
        above = jnp.where(chip > here, fall * fall * above + total_of(chip), above)
    three = jnp.where(info_ref[64] % 2 == 1, above, fall * above + total_of(here))
    lt = [lt_ref[layer] for layer in range(layers)]
    lr = [lr_ref[layer] for layer in range(layers)]
    end = jnp.logical_or(info_ref[64] == 0, info_ref[64] == info_ref[65] - 1)
    near, far = near_ref[...], jnp.where(end, 0.0, far_ref[...])
    upper_here = info_ref[64] % 2 == 1
    low, high = jnp.where(upper_here, near, far), jnp.where(upper_here, far, near)
    spread = laplace(lt, low, high, left_ref[...], right_ref[...])
    climbs, _ = chain(lr, decay, three)
    for l in range(layers):
        new_lt_ref[l] = lt[l] + 0.15 * spread[l] + decoded(info_ref, rec_ref, 0, l, 1) * lr[l]
        new_lr_ref[l] = (
            -0.3 * lt[l]
            + (1.0 + 0.2 * decoded(info_ref, rec_ref, 0, l, 0)) * lr[l]
            + climbs[l]
        )
    lane = lax.broadcasted_iota(jnp.int32, (layers, radials), 1)
    ring = jnp.where(
        lane < azimuths,
        flux_ref[...],
        jnp.where(
            lane < azimuths + band,
            right_ref[layers : 2 * layers, :],
            left_ref[layers : 2 * layers, :],
        ),
    )
    heat = jnp.zeros_like(ring)
    for offset in range(-band, band + 1):
        heat = heat + weight_ref[offset + band] * pltpu.roll(ring, (-offset) % radials, axis=1)
    heat_ref[...] = heat[:, :azimuths]


def run(body, scalars, args, shapes, scratch=(), span=1):
    smem = pl.BlockSpec(memory_space=pltpu.SMEM)
    vmem = pl.BlockSpec(memory_space=pltpu.VMEM)
    return pl.pallas_call(
        body,
        in_specs=[smem] * len(scalars) + [vmem] * len(args),
        out_specs=[vmem] * len(shapes),
        out_shape=[
            jax.ShapeDtypeStruct(shape, jnp.int16 if len(shape) == 4 else jnp.float32)
            for shape in shapes
        ],
        scratch_shapes=[pltpu.VMEM(shape, jnp.float32) for shape in scratch],
        compiler_params=pltpu.CompilerParams(vmem_limit_bytes=STEP_VMEM),
        cost_estimate=pl.CostEstimate(
            flops=span * SPAN_FLOPS, bytes_accessed=span * SPAN_BYTES, transcendentals=0
        ),
    )(*scalars, *args)


def turned(value, axis, shift):
    count = lax.axis_size(axis)
    return lax.ppermute(value, axis, [(i, (i + shift) % count) for i in range(count)])


def exchanged(low, high, left, right):
    return (
        turned(high, "axial", 1),
        turned(low, "axial", -1),
        turned(right, "azim", 1),
        turned(left, "azim", -1),
    )


def swapped(value):
    return lax.ppermute(value, "axial", [(i, i ^ 1) for i in range(lax.axis_size("axial"))])


def crossed(value):
    axial = lax.axis_size("axial")
    return lax.ppermute(
        value, "axial", [(i, (i - 1 + 2 * (i % 2)) % axial) for i in range(axial)]
    )


def between_chips(value):
    axial = lax.axis_size("axial")
    groups = [list(range(core, axial, 2)) for core in range(2)]
    return lax.all_to_all(value, "axial", 0, 0, tiled=True, axis_index_groups=groups)


def local(stored, holder, seed_temp, seed_disloc, decay_length, face_radius, kernel):
    layers, azimuths, radials = seed_temp.shape
    axial, me = lax.axis_size("axial"), lax.axis_index("axial")
    wanted = lax.dynamic_index_in_dim(holder, me, 1, keepdims=False).reshape(-1)
    info = jnp.concatenate([wanted, jnp.stack([me, axial]).astype(jnp.int32)])
    plane = (azimuths, radials)
    side = (layers, radials)
    wide = (2 * layers, radials)
    block = (layers, azimuths, radials)

    def half(count):
        return (count, azimuths // 2, radials)

    def copies(peers, count):
        return (peers, count * azimuths // (2 * ROWS), ROWS, radials)

    pieces = lax.all_to_all(encode(stored), "axial", 0, 0, tiled=True)

    def column(at):
        rows = [seed_temp[:, at], seed_disloc[:, at], decay_length[at : at + 1]]
        return jnp.pad(jnp.concatenate(rows, axis=0), ((0, 16 - 2 * layers - 1), (0, 0)))

    low = turned(seed_temp[layers - 1], "axial", 1)
    high = turned(jnp.stack([seed_temp[0], seed_disloc[0]]), "axial", -1)
    early = (turned(column(azimuths - 1), "azim", 1), turned(column(0), "azim", -1))
    pieces, low, high, *early = lax.optimization_barrier((pieces, low, high, *early))
    lt1, lr1, source, far, keep, give = run(
        first_body,
        (info,),
        (pieces, seed_temp, seed_disloc, low, high, *early, decay_length),
        [block, block, block, (4, *plane), half(5), half(13)],
        [(4, *plane)],
    )
    got = swapped(give)
    far = crossed(far)
    (total,) = run(
        pair_chip_body,
        (info,),
        (keep, got, *early, decay_length),
        [(axial // 2, azimuths // ROWS * 2 + 1, ROWS, radials)],
        span=CHIP_SPAN,
    )
    sums = between_chips(total)
    lt2, left, right, more, give = run(
        reach_body,
        (info,),
        (pieces, lt1, lr1, source, got, far, decay_length),
        [(layers + 2, *plane), (24, radials), (24, radials), half(3), half(3)],
        [(3, *plane)],
        span=REACH_SPAN,
    )
    more_got = swapped(give)
    sides = (turned(right, "azim", 1), turned(left, "azim", -1))
    sums, *sides = lax.optimization_barrier((sums, *sides))
    mine, other, total = run(
        pair_carry_body,
        (info,),
        (keep, got, more, more_got, sums, *sides, *early, decay_length),
        [half(4), half(4), copies(axial, 1)],
    )
    sums = lax.all_to_all(total, "axial", 0, 0, tiled=True)
    lt3, lr3, flux, near, far, left, right = run(
        third_body,
        (info,),
        (
            pieces, seed_temp, seed_disloc, lt1, lt2, lr1, left, right, *sides, got, far,
            high, *early, decay_length, face_radius[:, :, None], mine, swapped(other),
        ),
        [block, block, side, plane, plane, wide, wide],
        [(3, *plane)],
        span=THIRD_SPAN,
    )
    halo = (
        swapped(near),
        crossed(far),
        turned(right, "azim", 1),
        turned(left, "azim", -1),
    )
    return tuple(
        run(
            last_body,
            (info, kernel),
            (pieces, lt3, lr3, *halo, decay_length, sums, flux),
            [block, block, (layers, azimuths)],
        )
    )


def solution(mesh):
    in_specs = (
        P(None, "axial", "azim", None, None, None, None),
        P(),
        P("axial", "azim", None),
        P("axial", "azim", None),
        P("azim", None),
        P("axial", "azim"),
        P(),
    )
    out_specs = (P("axial", "azim", None), P("axial", "azim", None), P("axial", "azim"))
    return jax.shard_map(local, mesh=mesh, in_specs=in_specs, out_specs=out_specs, check_vma=False)
```

```python
import jax
import jax.numpy as jnp
from jax import lax
from jax.experimental import pallas as pl
from jax.experimental.pallas import tpu as pltpu
from jax.sharding import PartitionSpec as P

ROWS = 16
LANES = 128
RATE_MID = 3.7
RATE_SCALE = 10500.0
COEF_SCALE = 1374.0
COEF_BASE = 23.0
SUM_SCALE = 862.0
SUM_BASE = 29.0
PLANE_TOP = 32000.0
ENCODE_VMEM = 60 * 1024 * 1024
STEP_VMEM = 16 * 1024 * 1024
SPAN_FLOPS = 1_000_000_000
SPAN_BYTES = 3_000_000
CHIP_SPAN = 50
REACH_SPAN = 100
THIRD_SPAN = 100


def squeezed(value, base, scale):
    size = jnp.log2(jnp.maximum(jnp.abs(value), 2.0**-base))
    size = size * scale + (base * scale + 0.5)
    return jnp.where(value < 0.0, -size, size).astype(jnp.int32)


def spread_out(code, base, scale):
    code = code.astype(jnp.int32).astype(jnp.float32)
    size = jnp.exp2(jnp.abs(code) * (1.0 / scale) - base)
    return jnp.where(code > 0.0, size, jnp.where(code < 0.0, -size, 0.0))


def encode_body(stored_ref, out_ref, pieces, codes, in_sems, out_sems):
    steps, slots = stored_ref.shape[:2]
    cap = slots // out_ref.shape[0]
    rows = 8 * ROWS
    per = 2 * cap
    half_way = steps // 2
    cuts = [*range(half_way), half_way, steps]
    arrivals = {
        start: pltpu.make_async_copy(
            stored_ref.at[pl.ds(start, end - start)],
            pieces.at[pl.ds(start, end - start)],
            in_sems.at[start],
        )
        for start, end in zip(cuts[:-1], cuts[1:])
    }
    for copy in arrivals.values():
        copy.start()
    row = lax.broadcasted_iota(jnp.int32, (rows, rows), 0)
    column = lax.broadcasted_iota(jnp.int32, (rows, rows), 1)
    picked = (row % ROWS) * 8 + row // ROWS == column
    order = jnp.where(picked, 1.0, 0.0).astype(jnp.bfloat16)

    def mixed(step, slot):
        cells = pieces[step, slot].astype(jnp.float32)
        return jnp.concatenate(
            [cells[:, LANES * r : LANES * (r + 1)] for r in range(ROWS)], axis=0
        ).astype(jnp.bfloat16)

    departures = []

    def depart(start, count):
        copy = pltpu.make_async_copy(
            codes.at[:, pl.ds(start, count)],
            out_ref.at[:, pl.ds(start, count)],
            out_sems.at[len(departures)],
        )
        copy.start()
        departures.append(copy)

    for step in range(steps):
        if step in arrivals:
            arrivals[step].wait()
        for slot in range(0, slots, cap):
            both = jnp.concatenate([mixed(step, slot + c) for c in range(cap)], axis=1)
            parts = jnp.dot(order, both, preferred_element_type=jnp.float32)

            def part(index):
                return parts[ROWS * index : ROWS * (index + 1), :]

            squares = part(1) * part(1)
            for index in range(2, 7):
                squares = squares + part(index) * part(index)
            slope = jnp.tanh(part(0))
            total = 1.0 + squares * (1.0 / 6.0)
            rate = total * lax.rsqrt(total) * jnp.exp(0.5 * slope)
            coef = (0.1 * part(7)) * rate * (1.0 - slope * slope)
            coef_code = squeezed(coef, COEF_BASE, COEF_SCALE).astype(jnp.int16)
            rate_code = jnp.round((rate - RATE_MID) * RATE_SCALE)
            rate_code = rate_code.astype(jnp.int32).astype(jnp.int16)
            for c in range(cap):
                lanes = slice(LANES * c, LANES * (c + 1))
                codes[slot // cap, per * step + 2 * c] = rate_code[:, lanes]
                codes[slot // cap, per * step + 2 * c + 1] = coef_code[:, lanes]
        if step + 1 == half_way:
            depart(0, per * half_way)
    depart(per * half_way, out_ref.shape[1] - per * half_way)
    for copy in departures:
        copy.wait()


def encode(stored):
    steps, _, _, owners, cap, comps, cells = stored.shape
    flat = stored.reshape(steps, owners * cap, comps, cells)
    shape = (owners, steps * cap * 2, ROWS, LANES)
    return pl.pallas_call(
        encode_body,
        in_specs=[pl.BlockSpec(memory_space=pl.ANY)],
        out_specs=pl.BlockSpec(memory_space=pl.ANY),
        out_shape=jax.ShapeDtypeStruct(shape, jnp.int16),
        scratch_shapes=[
            pltpu.VMEM(flat.shape, jnp.bfloat16),
            pltpu.VMEM(shape, jnp.int16),
            pltpu.SemaphoreType.DMA((steps,)),
            pltpu.SemaphoreType.DMA((2,)),
        ],
        compiler_params=pltpu.CompilerParams(vmem_limit_bytes=ENCODE_VMEM),
    )(flat)


def decoded(info_ref, rec_ref, step, layer, field):
    pieces = []
    for quarter in range(4):
        held = info_ref[16 * step + 4 * layer + quarter]
        code = rec_ref[held // 2, 4 * step + 2 * (held % 2) + field]
        if field == 0:
            code = code.astype(jnp.int32).astype(jnp.float32)
            pieces.append(code * (1.0 / RATE_SCALE) + RATE_MID)
        else:
            pieces.append(spread_out(code, COEF_BASE, COEF_SCALE))
    return jnp.concatenate(pieces, axis=0)


def radial(x):
    lane = lax.broadcasted_iota(jnp.int32, x.shape, 1)
    inner = jnp.where(lane == 0, 0.0, pltpu.roll(x, 1, axis=1))
    outer = jnp.where(lane == x.shape[1] - 1, 0.0, pltpu.roll(x, x.shape[1] - 1, axis=1))
    return inner + outer


def laplace(field, low, high, left=None, right=None):
    layers = len(field)
    azimuths = field[0].shape[0]
    row = lax.broadcasted_iota(jnp.int32, field[0].shape, 0)
    out = []
    for layer in range(layers):
        x = field[layer]
        below = low if layer == 0 else field[layer - 1]
        above = high if layer == layers - 1 else field[layer + 1]
        first = 0.0 if left is None else left[layer : layer + 1, :]
        last = 0.0 if right is None else right[layer : layer + 1, :]
        before = jnp.where(row == 0, first, pltpu.roll(x, 1, axis=0))
        after = jnp.where(row == azimuths - 1, last, pltpu.roll(x, azimuths - 1, axis=0))
        out.append(((below + above) + (before + after)) + radial(x) - 6.0 * x)
    return out


def chain(field, decay, carry):
    layers = len(field)
    out = [None] * layers
    for layer in reversed(range(layers)):
        out[layer] = carry
        carry = decay * carry + (1.0 - decay) * field[layer]
    return out, carry


def powers(length):
    decay = jnp.exp(-1.0 / length)
    cube = decay * decay * decay
    return decay, decay * cube, 4.0 * (1.0 - decay) * cube


def half_powers(info_ref, length_ref):
    half = length_ref.shape[0] // 2
    return powers(length_ref[pl.ds(half * (info_ref[64] % 2), half), :])


def halves(info_ref, values, scratch, keep_ref, give_ref):
    mine = info_ref[64] % 2
    half = scratch.shape[1] // 2
    for index, value in enumerate(values):
        scratch[index] = value
    for index in range(len(values)):
        keep_ref[index] = scratch[index, pl.ds(half * mine, half), :]
        give_ref[index] = scratch[index, pl.ds(half * (1 - mine), half), :]


def restored(info_ref, mine_ref, got_ref, scratch):
    mine = info_ref[64] % 2
    half = scratch.shape[1] // 2
    count = scratch.shape[0]
    for index in range(count):
        scratch[index, pl.ds(half * mine, half), :] = mine_ref[index]
        scratch[index, pl.ds(half * (1 - mine), half), :] = got_ref[index]
    return [scratch[index] for index in range(count)]


def cores(info_ref, keep_ref, got_ref):
    upper_here = info_ref[64] % 2 == 1
    own = [keep_ref[index] for index in range(min(4, keep_ref.shape[0]))]
    other = [got_ref[index] for index in range(len(own))]
    upper = [jnp.where(upper_here, a, b) for a, b in zip(own, other)]
    lower = [jnp.where(upper_here, b, a) for a, b in zip(own, other)]
    return upper, lower


def share_out(info_ref, upper, lower, mine_ref, other_ref):
    upper_here = info_ref[64] % 2 == 1
    for index, (a, b) in enumerate(zip(upper, lower)):
        mine_ref[index] = jnp.where(upper_here, a, b)
        other_ref[index] = jnp.where(upper_here, b, a)


def applied(carry, here, fall, cross):
    out = [sums + fall * value for value, sums in zip(carry, here)]
    if len(carry) > 1:
        out[1] = out[1] + cross * carry[0]
        out[2] = out[2] + cross * carry[1] + here[3] * carry[0]
    return tuple(out)


def scaled(value):
    top = jnp.max(jnp.max(jnp.abs(value), axis=1, keepdims=True), axis=0, keepdims=True)
    size = jnp.ceil(jnp.log2(jnp.maximum(top, 2.0**-100)))
    code = jnp.round(value * jnp.exp2(-size) * PLANE_TOP)
    return code.astype(jnp.int32), jnp.broadcast_to(size, (1, value.shape[1])).astype(jnp.int32)


def unscaled(code, size):
    return code.astype(jnp.int32).astype(jnp.float32) * (jnp.exp2(size) * (1.0 / PLANE_TOP))


def put_sum(out_ref, at, start, code):
    code = code.astype(jnp.int16)
    for block in range(code.shape[0] // ROWS):
        out_ref[at, start + block] = code[ROWS * block : ROWS * (block + 1), :]


def got_sum(sums_ref, at, start, count):
    code = [sums_ref[at, start + block] for block in range(count)]
    return jnp.concatenate([spread_out(part, SUM_BASE, SUM_SCALE) for part in code], axis=0)


def answered(gain, share, decay):
    climbs, _ = chain(share, decay, jnp.zeros_like(decay))
    return [g * s + c for g, s, c in zip(gain, share, climbs)]


def shares(decay, layers):
    out = [None] * layers
    power = jnp.ones_like(decay)
    for layer in reversed(range(layers)):
        out[layer] = power
        power = decay * power
    return out


def first_body(
    info_ref, rec_ref, lt_ref, lr_ref, low_ref, high_ref, left_ref, right_ref, length_ref,
    new_lt_ref, new_lr_ref, source_ref, far_ref, keep_ref, give_ref, scratch,
):
    layers = lt_ref.shape[0]
    decay, _, _ = powers(length_ref[...])
    nothing = jnp.zeros_like(decay)
    lt = [lt_ref[layer] for layer in range(layers)]
    lr = [lr_ref[layer] for layer in range(layers)]
    low = jnp.where(info_ref[64] == 0, 0.0, low_ref[...])
    high = jnp.where(info_ref[64] == info_ref[65] - 1, 0.0, high_ref[0])
    spread = laplace(lt, low, high, left_ref[0:layers, :], right_ref[0:layers, :])
    new_lt = [
        lt[l] + 0.15 * spread[l] + decoded(info_ref, rec_ref, 3, l, 1) * lr[l]
        for l in range(layers)
    ]
    climbs, begin = chain(lr, decay, nothing)
    base = [
        -0.3 * lt[l] + (1.0 + 0.2 * decoded(info_ref, rec_ref, 3, l, 0)) * lr[l]
        for l in range(layers)
    ]
    lr = [base[l] + climbs[l] for l in range(layers)]
    gate = [decoded(info_ref, rec_ref, 2, l, 1) for l in range(layers)]
    half = decay.shape[0] // 2
    up = (new_lt[-2], new_lt[-1], gate[-1] * base[-1], gate[-1])
    down = (new_lt[0], new_lt[1], gate[0] * base[0], gate[0])
    upper_here = info_ref[64] % 2 == 1
    for index in range(4):
        far_ref[index] = jnp.where(upper_here, up[index], down[index])
        near = jnp.where(upper_here, down[index], up[index])
        give_ref[4 + 2 * index] = near[:half]
        give_ref[5 + 2 * index] = near[half:]
    for l in range(layers):
        give_ref[12, l : l + 1, :] = new_lt[l][0:1, :]
        give_ref[12, layers + l : layers + l + 1, :] = new_lt[l][2 * half - 1 : 2 * half, :]
    beyond_sums = []
    for ref in (left_ref, right_ref):
        side_decay, _, _ = powers(ref[2 * layers : 2 * layers + 1, :])
        side = [ref[layers + l : layers + l + 1, :] for l in range(layers)]
        beyond_sums.append(chain(side, side_decay, jnp.zeros_like(side_decay))[1])
    keep_ref[4] = jnp.zeros_like(keep_ref[4])
    give_ref[12, 8:, :] = jnp.zeros_like(give_ref[12, 8:, :])
    keep_ref[4, 0:1, :] = jnp.where(upper_here, beyond_sums[1], beyond_sums[0])
    give_ref[12, 8:9, :] = jnp.where(upper_here, beyond_sums[0], beyond_sums[1])
    _, now = chain(lr, decay, nothing)
    gain = [1.0 + 0.2 * decoded(info_ref, rec_ref, 2, l, 0) for l in range(layers)]
    after = [a - 0.3 * new_lt[l] for l, a in enumerate(answered(gain, lr, decay))]
    _, later = chain(after, decay, nothing)
    _, weight = chain(answered(gain, shares(decay, layers), decay), decay, nothing)
    halves(info_ref, (begin, now, later, weight), scratch, keep_ref, give_ref)
    for l in range(layers):
        new_lt_ref[l] = new_lt[l]
        new_lr_ref[l] = lr[l]
        source_ref[l] = gate[l] * lr[l]


def side_powers(info_ref, early_left_ref, early_right_ref):
    upper_here = info_ref[64] % 2 == 1
    length = jnp.where(upper_here, early_right_ref[8:9, :], early_left_ref[8:9, :])
    return powers(length)


def pair_chip_body(
    info_ref, keep_ref, got_ref, early_left_ref, early_right_ref, length_ref, out_ref,
):
    _, fall, cross = half_powers(info_ref, length_ref)
    _, side_fall, _ = side_powers(info_ref, early_left_ref, early_right_ref)
    upper, lower = cores(info_ref, keep_ref, got_ref)
    total = list(applied(upper[:3], lower, fall, cross))
    total.append(fall * (lower[3] + upper[3]) + cross * cross)
    upper_here = info_ref[64] % 2 == 1
    own, other = keep_ref[4, 0:1, :], got_ref[12, 8:9, :]
    side = jnp.where(upper_here, other, own) + side_fall * jnp.where(upper_here, own, other)
    codes, sizes = zip(*[scaled(value) for value in [*total, side]])
    filler = jnp.zeros((ROWS - 1 - len(sizes), side.shape[1]), jnp.int32)
    last = jnp.concatenate([codes[-1], *sizes, filler], axis=0)
    for chip in range(out_ref.shape[0]):
        start = 0
        for code in (*codes[:-1], last):
            put_sum(out_ref, chip, start, code)
            start += code.shape[0] // ROWS


def reach_body(
    info_ref, rec_ref, lt_ref, lr_ref, source_ref, near_ref, far_ref, length_ref,
    new_lt_ref, left_out, right_out, keep_ref, give_ref, scratch,
):
    layers, azimuths, _ = lt_ref.shape
    bottom = info_ref[64] == 0
    top = info_ref[64] == info_ref[65] - 1
    upper_here = info_ref[64] % 2 == 1
    low, high = [], []
    for index in range(3):
        near = jnp.concatenate([near_ref[4 + 2 * index], near_ref[5 + 2 * index]], axis=0)
        far = jnp.where(jnp.logical_or(bottom, top), 0.0, far_ref[index])
        low.append(jnp.where(upper_here, near, far))
        high.append(jnp.where(upper_here, far, near))
    lt = [low[1], *[lt_ref[l] for l in range(layers)], high[0]]
    source = [low[2], *[source_ref[l] for l in range(layers)], high[2]]
    spread = laplace(lt, low[0], high[1])
    new_lt = [lt[l] + 0.15 * spread[l] + source[l] for l in range(layers + 2)]
    new_lt[0] = jnp.where(bottom, 0.0, new_lt[0])
    new_lt[-1] = jnp.where(top, 0.0, new_lt[-1])
    gate = [decoded(info_ref, rec_ref, 2, l, 1) for l in range(layers)]
    sides = ((left_out, 0, 1, 0), (right_out, azimuths - 1, azimuths - 2, layers))
    for out, edge, inside, other in sides:
        for l in range(layers + 2):
            out[l : l + 1, :] = lt[l][edge : edge + 1, :]
        out[layers + 2 : layers + 4, :] = jnp.zeros_like(out[layers + 2 : layers + 4, :])
        for l in range(layers):
            out[8 + l : 9 + l, :] = lt[l + 1][inside : inside + 1, :]
            out[12 + l : 13 + l, :] = source[l + 1][edge : edge + 1, :]
            out[20 + l : 21 + l, :] = gate[l][edge : edge + 1, :]
        out[16:20, :] = near_ref[12, other : other + layers, :]
    for l in range(layers + 2):
        new_lt_ref[l] = new_lt[l]
    new_lt = new_lt[1:-1]
    decay, _, _ = powers(length_ref[...])
    nothing = jnp.zeros_like(decay)
    one = [1.0 + 0.2 * decoded(info_ref, rec_ref, 2, l, 0) for l in range(layers)]
    two = [1.0 + 0.2 * decoded(info_ref, rec_ref, 1, l, 0) for l in range(layers)]
    lr = [lr_ref[layer] for layer in range(layers)]
    lr = [a - 0.3 * lt_ref[l] for l, a in enumerate(answered(one, lr, decay))]
    lr = [a - 0.3 * new_lt[l] for l, a in enumerate(answered(two, lr, decay))]
    _, later = chain(lr, decay, nothing)
    share = shares(decay, layers)
    by_zero = answered(two, answered(one, share, decay), decay)
    by_zero = [by_zero[l] - 0.3 * gate[l] * share[l] for l in range(layers)]
    _, one_weight = chain(answered(two, share, decay), decay, nothing)
    _, zero_weight = chain(by_zero, decay, nothing)
    halves(info_ref, (later, one_weight, zero_weight), scratch, keep_ref, give_ref)


def beyond(there, here):
    middle = there[1:5]
    total = (there[0:4] + there[2:6]) + (there[8:12] + here[1:5]) + radial(middle)
    return middle + 0.15 * (total - 6.0 * middle) + there[12:16]


def pair_carry_body(
    info_ref, keep_ref, got_ref, more_ref, more_got_ref, sums_ref, left_ref, right_ref,
    early_left_ref, early_right_ref, length_ref, mine_ref, other_ref, out_ref,
):
    _, fall, cross = half_powers(info_ref, length_ref)
    _, side_fall, _ = side_powers(info_ref, early_left_ref, early_right_ref)
    chips = sums_ref.shape[0]
    per = fall.shape[0] // ROWS
    above = (jnp.zeros_like(fall),) * 3
    side = jnp.zeros_like(side_fall)
    for chip in reversed(range(1, chips)):
        inside = chip > info_ref[64] // 2
        tail = sums_ref[chip, 4 * per].astype(jnp.int32).astype(jnp.float32)
        here = [
            jnp.concatenate(
                [
                    unscaled(sums_ref[chip, per * index + block], tail[1 + index : 2 + index])
                    for block in range(per)
                ],
                axis=0,
            )
            for index in range(4)
        ]
        new = applied(above, here, fall * fall, 2.0 * fall * cross)
        above = tuple(jnp.where(inside, a, b) for a, b in zip(new, above))
        new = tail[0:1] * (jnp.exp2(tail[5:6]) * (1.0 / PLANE_TOP)) + side_fall * side_fall * side
        side = jnp.where(inside, new, side)
    upper, _ = cores(info_ref, keep_ref, got_ref)
    below = applied(above, upper, fall, cross)
    share_out(info_ref, above, below, mine_ref, other_ref)
    upper_here = info_ref[64] % 2 == 1
    below_side = side_fall * side + jnp.where(
        upper_here, keep_ref[4, 0:1, :], got_ref[12, 8:9, :]
    )
    mine_ref[3] = jnp.zeros_like(fall)
    other_ref[3] = jnp.zeros_like(fall)
    mine_ref[3, 0:1, :] = jnp.where(upper_here, side, below_side)
    other_ref[3, 0:1, :] = jnp.where(upper_here, below_side, side)
    upper, lower = cores(info_ref, more_ref, more_got_ref)
    upper = upper[0] + upper[1] * above[1] + upper[2] * above[0] + cross * above[2]
    lower = lower[0] + lower[1] * below[1] + lower[2] * below[0] + cross * below[2]
    end = length_ref.shape[0] - 1
    beside = jnp.where(upper_here, right_ref[...], left_ref[...])
    decay, _, _ = powers(jnp.where(upper_here, length_ref[end:, :], length_ref[0:1, :]))
    row = lax.broadcasted_iota(jnp.int32, fall.shape, 0)
    edge = row == jnp.where(upper_here, fall.shape[0] - 1, 0)
    weight = (-0.3 * 0.15) * (1.0 - decay)
    own, other = jnp.zeros_like(decay), jnp.zeros_like(decay)
    for layer in range(4):
        own = own + weight * beside[1 + layer : 2 + layer, :]
        other = other + weight * beside[16 + layer : 17 + layer, :]
        weight = weight * decay
    upper = upper + jnp.where(edge, jnp.where(upper_here, own, other), 0.0)
    lower = lower + jnp.where(edge, jnp.where(upper_here, other, own), 0.0)
    total = squeezed(lower + fall * upper, SUM_BASE, SUM_SCALE)
    upper = squeezed(upper, SUM_BASE, SUM_SCALE)
    for peer in range(out_ref.shape[0]):
        put_sum(out_ref, peer, 0, jnp.where(info_ref[64] // 2 == peer // 2, upper, total))


def third_body(
    info_ref, rec_ref, seed_ref, seed_lr_ref, one_ref, lt_ref, lr_ref, own_left_ref,
    own_right_ref, left_ref, right_ref, near_ref, beyond_ref, high_ref, early_left_ref,
    early_right_ref, length_ref, face_ref,
    mine_ref, got_ref, new_lt_ref, new_lr_ref, flux_ref, near_out, far_out, left_out, right_out,
    scratch,
):
    layers, azimuths, radials = lr_ref.shape
    decay, _, _ = powers(length_ref[...])
    zero, one, two = restored(info_ref, mine_ref, got_ref, scratch)
    upper_here = info_ref[64] % 2 == 1
    share = shares(decay, layers)
    lift = [share[l] * zero for l in range(layers)]
    seed_lr = [seed_lr_ref[layer] for layer in range(layers)]
    _, under = chain(seed_lr, decay, zero)
    over = (zero - (1.0 - decay) * high_ref[1]) / decay
    near = jnp.concatenate([near_ref[10], near_ref[11]], axis=0)
    gate_low = jnp.where(upper_here, near, beyond_ref[3])
    gate_high = jnp.where(upper_here, beyond_ref[3], near)
    lifts = [
        jnp.where(info_ref[64] == 0, 0.0, gate_low * under),
        *[decoded(info_ref, rec_ref, 2, l, 1) * lift[l] for l in range(layers)],
        jnp.where(info_ref[64] == info_ref[65] - 1, 0.0, gate_high * over),
    ]
    mine_side, got_side = mine_ref[3, 0:1, :], got_ref[3, 0:1, :]

    def lifted(there, early_ref, side):
        side_decay, _, _ = powers(early_ref[8:9, :])
        side_share = jnp.concatenate(shares(side_decay, layers), axis=0)
        return there[20:24] * side_share * side

    before = [one_ref[layer] for layer in range(layers)]
    left, right = left_ref[...], right_ref[...]
    row = lax.broadcasted_iota(jnp.int32, (azimuths, radials), 0)
    full = []
    for l in range(layers + 2):
        missing = jnp.where(
            row == 0,
            left[l : l + 1, :],
            jnp.where(row == azimuths - 1, right[l : l + 1, :], 0.0),
        )
        full.append(lt_ref[l] + 0.15 * missing + lifts[l])
    lt = full[1:-1]
    lr = [lr_ref[layer] + lift[layer] for layer in range(layers)]
    climbs, _ = chain(lr, decay, one)
    lr = [
        -0.3 * before[l]
        + (1.0 + 0.2 * decoded(info_ref, rec_ref, 2, l, 0)) * lr[l]
        + climbs[l]
        for l in range(layers)
    ]
    spread = laplace(
        lt,
        full[0],
        full[-1],
        beyond(left, own_left_ref[...])
        + lifted(left, early_left_ref, jnp.where(upper_here, got_side, mine_side)),
        beyond(right, own_right_ref[...])
        + lifted(right, early_right_ref, jnp.where(upper_here, mine_side, got_side)),
    )
    new_lt = [
        lt[l] + 0.15 * spread[l] + decoded(info_ref, rec_ref, 1, l, 1) * lr[l]
        for l in range(layers)
    ]
    upper_here = info_ref[64] % 2 == 1
    near_out[...] = jnp.where(upper_here, new_lt[0], new_lt[-1])
    far_out[...] = jnp.where(upper_here, new_lt[-1], new_lt[0])
    for l in range(layers):
        left_out[l : l + 1, :] = new_lt[l][0:1, :]
        right_out[l : l + 1, :] = new_lt[l][azimuths - 1 : azimuths, :]
    climbs, _ = chain(lr, decay, two)
    for l in range(layers):
        new_lt_ref[l] = new_lt[l]
        new_lr_ref[l] = (
            -0.3 * lt[l] + (1.0 + 0.2 * decoded(info_ref, rec_ref, 1, l, 0)) * lr[l] + climbs[l]
        )
    lane = lax.broadcasted_iota(jnp.int32, (azimuths, radials), 1)
    ones = jnp.ones((8, radials), jnp.float32)
    for l in range(layers):
        kept = jnp.where(
            lane == face_ref[l], (seed_ref[l] + before[l]) + (lt[l] + new_lt[l]), 0.0
        )
        line = lax.dot_general(
            ones,
            kept,
            (((1,), (1,)), ((), ())),
            precision=lax.Precision.HIGHEST,
            preferred_element_type=jnp.float32,
        )[0:1, :]
        twice = jnp.concatenate([line, line], axis=1)
        flux_ref[l : l + 1, :] = twice
        left_out[layers + l : layers + l + 1, :] = twice
        right_out[layers + l : layers + l + 1, :] = twice


def last_body(
    info_ref, weight_ref, rec_ref, lt_ref, lr_ref, near_ref, far_ref, left_ref, right_ref,
    length_ref, sums_ref, flux_ref, new_lt_ref, new_lr_ref, heat_ref,
):
    layers, azimuths, radials = lt_ref.shape
    band = weight_ref.shape[0] // 2
    decay, fall, _ = powers(length_ref[...])
    chips = sums_ref.shape[0] // 2
    here = info_ref[64] // 2

    per = sums_ref.shape[1]

    def total_of(chip):
        return jnp.concatenate(
            [got_sum(sums_ref, 2 * chip + core, 0, per) for core in range(2)], axis=0
        )

    above = jnp.zeros_like(fall)
    for chip in reversed(range(1, chips)):
        above = jnp.where(chip > here, fall * fall * above + total_of(chip), above)
    three = jnp.where(info_ref[64] % 2 == 1, above, fall * above + total_of(here))
    lt = [lt_ref[layer] for layer in range(layers)]
    lr = [lr_ref[layer] for layer in range(layers)]
    end = jnp.logical_or(info_ref[64] == 0, info_ref[64] == info_ref[65] - 1)
    near, far = near_ref[...], jnp.where(end, 0.0, far_ref[...])
    upper_here = info_ref[64] % 2 == 1
    low, high = jnp.where(upper_here, near, far), jnp.where(upper_here, far, near)
    spread = laplace(lt, low, high, left_ref[...], right_ref[...])
    climbs, _ = chain(lr, decay, three)
    for l in range(layers):
        new_lt_ref[l] = lt[l] + 0.15 * spread[l] + decoded(info_ref, rec_ref, 0, l, 1) * lr[l]
        new_lr_ref[l] = (
            -0.3 * lt[l]
            + (1.0 + 0.2 * decoded(info_ref, rec_ref, 0, l, 0)) * lr[l]
            + climbs[l]
        )
    lane = lax.broadcasted_iota(jnp.int32, (layers, radials), 1)
    ring = jnp.where(
        lane < azimuths,
        flux_ref[...],
        jnp.where(
            lane < azimuths + band,
            right_ref[layers : 2 * layers, :],
            left_ref[layers : 2 * layers, :],
        ),
    )
    heat = jnp.zeros_like(ring)
    for offset in range(-band, band + 1):
        heat = heat + weight_ref[offset + band] * pltpu.roll(ring, (-offset) % radials, axis=1)
    heat_ref[...] = heat[:, :azimuths]


def run(body, scalars, args, shapes, scratch=(), span=1):
    smem = pl.BlockSpec(memory_space=pltpu.SMEM)
    vmem = pl.BlockSpec(memory_space=pltpu.VMEM)
    return pl.pallas_call(
        body,
        in_specs=[smem] * len(scalars) + [vmem] * len(args),
        out_specs=[vmem] * len(shapes),
        out_shape=[
            jax.ShapeDtypeStruct(shape, jnp.int16 if len(shape) == 4 else jnp.float32)
            for shape in shapes
        ],
        scratch_shapes=[pltpu.VMEM(shape, jnp.float32) for shape in scratch],
        compiler_params=pltpu.CompilerParams(vmem_limit_bytes=STEP_VMEM),
        cost_estimate=pl.CostEstimate(
            flops=span * SPAN_FLOPS, bytes_accessed=span * SPAN_BYTES, transcendentals=0
        ),
    )(*scalars, *args)


def turned(value, axis, shift):
    count = lax.axis_size(axis)
    return lax.ppermute(value, axis, [(i, (i + shift) % count) for i in range(count)])


def swapped(value):
    return lax.ppermute(value, "axial", [(i, i ^ 1) for i in range(lax.axis_size("axial"))])


def crossed(value):
    axial = lax.axis_size("axial")
    return lax.ppermute(
        value, "axial", [(i, (i - 1 + 2 * (i % 2)) % axial) for i in range(axial)]
    )


def between_chips(value):
    axial = lax.axis_size("axial")
    groups = [list(range(core, axial, 2)) for core in range(2)]
    return lax.all_to_all(value, "axial", 0, 0, tiled=True, axis_index_groups=groups)


def local(stored, holder, seed_temp, seed_disloc, decay_length, face_radius, kernel):
    layers, azimuths, radials = seed_temp.shape
    axial, me = lax.axis_size("axial"), lax.axis_index("axial")
    wanted = lax.dynamic_index_in_dim(holder, me, 1, keepdims=False).reshape(-1)
    info = jnp.concatenate([wanted, jnp.stack([me, axial]).astype(jnp.int32)])
    plane = (azimuths, radials)
    side = (layers, radials)
    wide = (2 * layers, radials)
    block = (layers, azimuths, radials)

    def half(count):
        return (count, azimuths // 2, radials)

    def copies(peers, count):
        return (peers, count * azimuths // (2 * ROWS), ROWS, radials)

    pieces = lax.all_to_all(encode(stored), "axial", 0, 0, tiled=True)

    def column(at):
        rows = [seed_temp[:, at], seed_disloc[:, at], decay_length[at : at + 1]]
        return jnp.pad(jnp.concatenate(rows, axis=0), ((0, 16 - 2 * layers - 1), (0, 0)))

    low = turned(seed_temp[layers - 1], "axial", 1)
    high = turned(jnp.stack([seed_temp[0], seed_disloc[0]]), "axial", -1)
    early = (turned(column(azimuths - 1), "azim", 1), turned(column(0), "azim", -1))
    face = face_radius[:, :, None]
    pieces, low, high, face, *early = lax.optimization_barrier(
        (pieces, low, high, face, *early)
    )
    lt1, lr1, source, far, keep, give = run(
        first_body,
        (info,),
        (pieces, seed_temp, seed_disloc, low, high, *early, decay_length),
        [block, block, block, (4, *plane), half(5), half(13)],
        [(4, *plane)],
    )
    got = swapped(give)
    far = crossed(far)
    (total,) = run(
        pair_chip_body,
        (info,),
        (keep, got, *early, decay_length),
        [(axial // 2, azimuths // ROWS * 2 + 1, ROWS, radials)],
        span=CHIP_SPAN,
    )
    sums = between_chips(total)
    lt2, left, right, more, give = run(
        reach_body,
        (info,),
        (pieces, lt1, lr1, source, got, far, decay_length),
        [(layers + 2, *plane), (24, radials), (24, radials), half(3), half(3)],
        [(3, *plane)],
        span=REACH_SPAN,
    )
    more_got = swapped(give)
    sides = (turned(right, "azim", 1), turned(left, "azim", -1))
    sums, *sides = lax.optimization_barrier((sums, *sides))
    mine, other, total = run(
        pair_carry_body,
        (info,),
        (keep, got, more, more_got, sums, *sides, *early, decay_length),
        [half(4), half(4), copies(axial, 1)],
    )
    sums = lax.all_to_all(total, "axial", 0, 0, tiled=True)
    lt3, lr3, flux, near, far, left, right = run(
        third_body,
        (info,),
        (
            pieces, seed_temp, seed_disloc, lt1, lt2, lr1, left, right, *sides, got, far,
            high, *early, decay_length, face, mine, swapped(other),
        ),
        [block, block, side, plane, plane, wide, wide],
        [(3, *plane)],
        span=THIRD_SPAN,
    )
    halo = (
        swapped(near),
        crossed(far),
        turned(right, "azim", 1),
        turned(left, "azim", -1),
    )
    return tuple(
        run(
            last_body,
            (info, kernel),
            (pieces, lt3, lr3, *halo, decay_length, sums, flux),
            [block, block, (layers, azimuths)],
        )
    )


def solution(mesh):
    in_specs = (
        P(None, "axial", "azim", None, None, None, None),
        P(),
        P("axial", "azim", None),
        P("axial", "azim", None),
        P("azim", None),
        P("axial", "azim"),
        P(),
    )
    out_specs = (P("axial", "azim", None), P("axial", "azim", None), P("axial", "azim"))
    return jax.shard_map(local, mesh=mesh, in_specs=in_specs, out_specs=out_specs, check_vma=False)
```

```python
import jax
import jax.numpy as jnp
from jax import lax
from jax.experimental import pallas as pl
from jax.experimental.pallas import tpu as pltpu
from jax.sharding import PartitionSpec as P

ROWS = 16
LANES = 128
RATE_MID = 3.7
RATE_SCALE = 10500.0
COEF_SCALE = 1374.0
COEF_BASE = 23.0
SUM_SCALE = 862.0
SUM_BASE = 29.0
PLANE_TOP = 32000.0
ENCODE_VMEM = 60 * 1024 * 1024
STEP_VMEM = 16 * 1024 * 1024
SPAN_FLOPS = 1_000_000_000
SPAN_BYTES = 3_000_000
CHIP_SPAN = 50
REACH_SPAN = 100
THIRD_SPAN = 100


def squeezed(value, base, scale):
    size = jnp.log2(jnp.maximum(jnp.abs(value), 2.0**-base))
    size = size * scale + (base * scale + 0.5)
    return jnp.where(value < 0.0, -size, size).astype(jnp.int32)


def spread_out(code, base, scale):
    code = code.astype(jnp.int32).astype(jnp.float32)
    size = jnp.exp2(jnp.abs(code) * (1.0 / scale) - base)
    return jnp.where(code > 0.0, size, jnp.where(code < 0.0, -size, 0.0))


def encode_body(stored_ref, out_ref, pieces, codes, in_sems, out_sems):
    steps, slots = stored_ref.shape[:2]
    cap = slots // out_ref.shape[0]
    rows = 8 * ROWS
    per = 2 * cap
    half_way = steps // 2
    cuts = [*range(half_way), half_way, steps]
    arrivals = {
        start: pltpu.make_async_copy(
            stored_ref.at[pl.ds(start, end - start)],
            pieces.at[pl.ds(start, end - start)],
            in_sems.at[start],
        )
        for start, end in zip(cuts[:-1], cuts[1:])
    }
    for copy in arrivals.values():
        copy.start()
    row = lax.broadcasted_iota(jnp.int32, (rows, rows), 0)
    column = lax.broadcasted_iota(jnp.int32, (rows, rows), 1)
    picked = (row % ROWS) * 8 + row // ROWS == column
    order = jnp.where(picked, 1.0, 0.0).astype(jnp.bfloat16)

    def mixed(step, slot):
        cells = pieces[step, slot].astype(jnp.float32)
        return jnp.concatenate(
            [cells[:, LANES * r : LANES * (r + 1)] for r in range(ROWS)], axis=0
        ).astype(jnp.bfloat16)

    departures = []

    def depart(start, count):
        copy = pltpu.make_async_copy(
            codes.at[:, pl.ds(start, count)],
            out_ref.at[:, pl.ds(start, count)],
            out_sems.at[len(departures)],
        )
        copy.start()
        departures.append(copy)

    for step in range(steps):
        if step in arrivals:
            arrivals[step].wait()
        for slot in range(0, slots, cap):
            both = jnp.concatenate([mixed(step, slot + c) for c in range(cap)], axis=1)
            parts = jnp.dot(order, both, preferred_element_type=jnp.float32)

            def part(index):
                return parts[ROWS * index : ROWS * (index + 1), :]

            squares = part(1) * part(1)
            for index in range(2, 7):
                squares = squares + part(index) * part(index)
            slope = jnp.tanh(part(0))
            total = 1.0 + squares * (1.0 / 6.0)
            rate = total * lax.rsqrt(total) * jnp.exp(0.5 * slope)
            coef = (0.1 * part(7)) * rate * (1.0 - slope * slope)
            coef_code = squeezed(coef, COEF_BASE, COEF_SCALE).astype(jnp.int16)
            rate_code = jnp.round((rate - RATE_MID) * RATE_SCALE)
            rate_code = rate_code.astype(jnp.int32).astype(jnp.int16)
            for c in range(cap):
                lanes = slice(LANES * c, LANES * (c + 1))
                codes[slot // cap, per * step + 2 * c] = rate_code[:, lanes]
                codes[slot // cap, per * step + 2 * c + 1] = coef_code[:, lanes]
        if step + 1 == half_way:
            depart(0, per * half_way)
    depart(per * half_way, out_ref.shape[1] - per * half_way)
    for copy in departures:
        copy.wait()


def encode(stored):
    steps, _, _, owners, cap, comps, cells = stored.shape
    flat = stored.reshape(steps, owners * cap, comps, cells)
    shape = (owners, steps * cap * 2, ROWS, LANES)
    return pl.pallas_call(
        encode_body,
        in_specs=[pl.BlockSpec(memory_space=pl.ANY)],
        out_specs=pl.BlockSpec(memory_space=pl.ANY),
        out_shape=jax.ShapeDtypeStruct(shape, jnp.int16),
        scratch_shapes=[
            pltpu.VMEM(flat.shape, jnp.bfloat16),
            pltpu.VMEM(shape, jnp.int16),
            pltpu.SemaphoreType.DMA((steps,)),
            pltpu.SemaphoreType.DMA((2,)),
        ],
        compiler_params=pltpu.CompilerParams(vmem_limit_bytes=ENCODE_VMEM),
    )(flat)


def decoded(info_ref, rec_ref, step, layer, field):
    pieces = []
    for quarter in range(4):
        held = info_ref[16 * step + 4 * layer + quarter]
        code = rec_ref[held // 2, 4 * step + 2 * (held % 2) + field]
        if field == 0:
            code = code.astype(jnp.int32).astype(jnp.float32)
            pieces.append(code * (1.0 / RATE_SCALE) + RATE_MID)
        else:
            pieces.append(spread_out(code, COEF_BASE, COEF_SCALE))
    return jnp.concatenate(pieces, axis=0)


def radial(x):
    lane = lax.broadcasted_iota(jnp.int32, x.shape, 1)
    inner = jnp.where(lane == 0, 0.0, pltpu.roll(x, 1, axis=1))
    outer = jnp.where(lane == x.shape[1] - 1, 0.0, pltpu.roll(x, x.shape[1] - 1, axis=1))
    return inner + outer


def laplace(field, low, high, left=None, right=None):
    layers = len(field)
    azimuths = field[0].shape[0]
    row = lax.broadcasted_iota(jnp.int32, field[0].shape, 0)
    out = []
    for layer in range(layers):
        x = field[layer]
        below = low if layer == 0 else field[layer - 1]
        above = high if layer == layers - 1 else field[layer + 1]
        first = 0.0 if left is None else left[layer : layer + 1, :]
        last = 0.0 if right is None else right[layer : layer + 1, :]
        before = jnp.where(row == 0, first, pltpu.roll(x, 1, axis=0))
        after = jnp.where(row == azimuths - 1, last, pltpu.roll(x, azimuths - 1, axis=0))
        out.append(((below + above) + (before + after)) + radial(x) - 6.0 * x)
    return out


def chain(field, decay, carry):
    layers = len(field)
    out = [None] * layers
    for layer in reversed(range(layers)):
        out[layer] = carry
        carry = decay * carry + (1.0 - decay) * field[layer]
    return out, carry


def powers(length):
    decay = jnp.exp(-1.0 / length)
    cube = decay * decay * decay
    return decay, decay * cube, 4.0 * (1.0 - decay) * cube


def place():
    return {64: lax.axis_index("axial"), 65: lax.axis_size("axial")}


def half_powers(info_ref, length_ref):
    half = length_ref.shape[0] // 2
    return powers(length_ref[pl.ds(half * (info_ref[64] % 2), half), :])


def halves(info_ref, values, scratch, keep_ref, give_ref):
    mine = info_ref[64] % 2
    half = scratch.shape[1] // 2
    for index, value in enumerate(values):
        scratch[index] = value
    for index in range(len(values)):
        keep_ref[index] = scratch[index, pl.ds(half * mine, half), :]
        give_ref[index] = scratch[index, pl.ds(half * (1 - mine), half), :]


def restored(info_ref, mine_ref, got_ref, scratch):
    mine = info_ref[64] % 2
    half = scratch.shape[1] // 2
    count = scratch.shape[0]
    for index in range(count):
        scratch[index, pl.ds(half * mine, half), :] = mine_ref[index]
        scratch[index, pl.ds(half * (1 - mine), half), :] = got_ref[index]
    return [scratch[index] for index in range(count)]


def cores(info_ref, keep_ref, got_ref):
    upper_here = info_ref[64] % 2 == 1
    own = [keep_ref[index] for index in range(min(4, keep_ref.shape[0]))]
    other = [got_ref[index] for index in range(len(own))]
    upper = [jnp.where(upper_here, a, b) for a, b in zip(own, other)]
    lower = [jnp.where(upper_here, b, a) for a, b in zip(own, other)]
    return upper, lower


def share_out(info_ref, upper, lower, mine_ref, other_ref):
    upper_here = info_ref[64] % 2 == 1
    for index, (a, b) in enumerate(zip(upper, lower)):
        mine_ref[index] = jnp.where(upper_here, a, b)
        other_ref[index] = jnp.where(upper_here, b, a)


def applied(carry, here, fall, cross):
    out = [sums + fall * value for value, sums in zip(carry, here)]
    if len(carry) > 1:
        out[1] = out[1] + cross * carry[0]
        out[2] = out[2] + cross * carry[1] + here[3] * carry[0]
    return tuple(out)


def scaled(value):
    top = jnp.max(jnp.max(jnp.abs(value), axis=1, keepdims=True), axis=0, keepdims=True)
    size = jnp.ceil(jnp.log2(jnp.maximum(top, 2.0**-100)))
    code = jnp.round(value * jnp.exp2(-size) * PLANE_TOP)
    return code.astype(jnp.int32), jnp.broadcast_to(size, (1, value.shape[1])).astype(jnp.int32)


def unscaled(code, size):
    return code.astype(jnp.int32).astype(jnp.float32) * (jnp.exp2(size) * (1.0 / PLANE_TOP))


def put_sum(out_ref, at, start, code):
    code = code.astype(jnp.int16)
    for block in range(code.shape[0] // ROWS):
        out_ref[at, start + block] = code[ROWS * block : ROWS * (block + 1), :]


def got_sum(sums_ref, at, start, count):
    code = [sums_ref[at, start + block] for block in range(count)]
    return jnp.concatenate([spread_out(part, SUM_BASE, SUM_SCALE) for part in code], axis=0)


def answered(gain, share, decay):
    climbs, _ = chain(share, decay, jnp.zeros_like(decay))
    return [g * s + c for g, s, c in zip(gain, share, climbs)]


def shares(decay, layers):
    out = [None] * layers
    power = jnp.ones_like(decay)
    for layer in reversed(range(layers)):
        out[layer] = power
        power = decay * power
    return out


def first_body(
    info_ref, rec_ref, lt_ref, lr_ref, low_ref, high_ref, left_ref, right_ref, length_ref,
    new_lt_ref, new_lr_ref, source_ref, far_ref, keep_ref, give_ref, scratch,
):
    layers = lt_ref.shape[0]
    decay, _, _ = powers(length_ref[...])
    nothing = jnp.zeros_like(decay)
    lt = [lt_ref[layer] for layer in range(layers)]
    lr = [lr_ref[layer] for layer in range(layers)]
    low = jnp.where(info_ref[64] == 0, 0.0, low_ref[...])
    high = jnp.where(info_ref[64] == info_ref[65] - 1, 0.0, high_ref[0])
    spread = laplace(lt, low, high, left_ref[0:layers, :], right_ref[0:layers, :])
    new_lt = [
        lt[l] + 0.15 * spread[l] + decoded(info_ref, rec_ref, 3, l, 1) * lr[l]
        for l in range(layers)
    ]
    climbs, begin = chain(lr, decay, nothing)
    base = [
        -0.3 * lt[l] + (1.0 + 0.2 * decoded(info_ref, rec_ref, 3, l, 0)) * lr[l]
        for l in range(layers)
    ]
    lr = [base[l] + climbs[l] for l in range(layers)]
    gate = [decoded(info_ref, rec_ref, 2, l, 1) for l in range(layers)]
    half = decay.shape[0] // 2
    up = (new_lt[-2], new_lt[-1], gate[-1] * base[-1], gate[-1])
    down = (new_lt[0], new_lt[1], gate[0] * base[0], gate[0])
    upper_here = info_ref[64] % 2 == 1
    for index in range(4):
        far_ref[index] = jnp.where(upper_here, up[index], down[index])
        near = jnp.where(upper_here, down[index], up[index])
        give_ref[4 + 2 * index] = near[:half]
        give_ref[5 + 2 * index] = near[half:]
    for l in range(layers):
        give_ref[12, l : l + 1, :] = new_lt[l][0:1, :]
        give_ref[12, layers + l : layers + l + 1, :] = new_lt[l][2 * half - 1 : 2 * half, :]
    beyond_sums = []
    for ref in (left_ref, right_ref):
        side_decay, _, _ = powers(ref[2 * layers : 2 * layers + 1, :])
        side = [ref[layers + l : layers + l + 1, :] for l in range(layers)]
        beyond_sums.append(chain(side, side_decay, jnp.zeros_like(side_decay))[1])
    keep_ref[4] = jnp.zeros_like(keep_ref[4])
    give_ref[12, 8:, :] = jnp.zeros_like(give_ref[12, 8:, :])
    keep_ref[4, 0:1, :] = jnp.where(upper_here, beyond_sums[1], beyond_sums[0])
    give_ref[12, 8:9, :] = jnp.where(upper_here, beyond_sums[0], beyond_sums[1])
    _, now = chain(lr, decay, nothing)
    gain = [1.0 + 0.2 * decoded(info_ref, rec_ref, 2, l, 0) for l in range(layers)]
    after = [a - 0.3 * new_lt[l] for l, a in enumerate(answered(gain, lr, decay))]
    _, later = chain(after, decay, nothing)
    _, weight = chain(answered(gain, shares(decay, layers), decay), decay, nothing)
    halves(info_ref, (begin, now, later, weight), scratch, keep_ref, give_ref)
    for l in range(layers):
        new_lt_ref[l] = new_lt[l]
        new_lr_ref[l] = lr[l]
        source_ref[l] = gate[l] * lr[l]


def side_powers(info_ref, early_left_ref, early_right_ref):
    upper_here = info_ref[64] % 2 == 1
    length = jnp.where(upper_here, early_right_ref[8:9, :], early_left_ref[8:9, :])
    return powers(length)


def pair_chip_body(
    keep_ref, got_ref, early_left_ref, early_right_ref, length_ref, out_ref,
):
    info_ref = place()
    _, fall, cross = half_powers(info_ref, length_ref)
    _, side_fall, _ = side_powers(info_ref, early_left_ref, early_right_ref)
    upper, lower = cores(info_ref, keep_ref, got_ref)
    total = list(applied(upper[:3], lower, fall, cross))
    total.append(fall * (lower[3] + upper[3]) + cross * cross)
    upper_here = info_ref[64] % 2 == 1
    own, other = keep_ref[4, 0:1, :], got_ref[12, 8:9, :]
    side = jnp.where(upper_here, other, own) + side_fall * jnp.where(upper_here, own, other)
    codes, sizes = zip(*[scaled(value) for value in [*total, side]])
    filler = jnp.zeros((ROWS - 1 - len(sizes), side.shape[1]), jnp.int32)
    last = jnp.concatenate([codes[-1], *sizes, filler], axis=0)
    for chip in range(out_ref.shape[0]):
        start = 0
        for code in (*codes[:-1], last):
            put_sum(out_ref, chip, start, code)
            start += code.shape[0] // ROWS


def reach_body(
    info_ref, rec_ref, lt_ref, lr_ref, source_ref, near_ref, far_ref, length_ref,
    new_lt_ref, left_out, right_out, keep_ref, give_ref, fields_ref, scratch,
):
    layers, azimuths, _ = lt_ref.shape
    bottom = info_ref[64] == 0
    top = info_ref[64] == info_ref[65] - 1
    upper_here = info_ref[64] % 2 == 1
    low, high = [], []
    for index in range(3):
        near = jnp.concatenate([near_ref[4 + 2 * index], near_ref[5 + 2 * index]], axis=0)
        far = jnp.where(jnp.logical_or(bottom, top), 0.0, far_ref[index])
        low.append(jnp.where(upper_here, near, far))
        high.append(jnp.where(upper_here, far, near))
    lt = [low[1], *[lt_ref[l] for l in range(layers)], high[0]]
    source = [low[2], *[source_ref[l] for l in range(layers)], high[2]]
    spread = laplace(lt, low[0], high[1])
    new_lt = [lt[l] + 0.15 * spread[l] + source[l] for l in range(layers + 2)]
    new_lt[0] = jnp.where(bottom, 0.0, new_lt[0])
    new_lt[-1] = jnp.where(top, 0.0, new_lt[-1])
    gate = [decoded(info_ref, rec_ref, 2, l, 1) for l in range(layers)]
    sides = ((left_out, 0, 1, 0), (right_out, azimuths - 1, azimuths - 2, layers))
    for out, edge, inside, other in sides:
        for l in range(layers + 2):
            out[l : l + 1, :] = lt[l][edge : edge + 1, :]
        out[layers + 2 : layers + 4, :] = jnp.zeros_like(out[layers + 2 : layers + 4, :])
        for l in range(layers):
            out[8 + l : 9 + l, :] = lt[l + 1][inside : inside + 1, :]
            out[12 + l : 13 + l, :] = source[l + 1][edge : edge + 1, :]
            out[20 + l : 21 + l, :] = gate[l][edge : edge + 1, :]
        out[16:20, :] = near_ref[12, other : other + layers, :]
    for l in range(layers + 2):
        new_lt_ref[l] = new_lt[l]
    new_lt = new_lt[1:-1]
    decay, _, _ = powers(length_ref[...])
    nothing = jnp.zeros_like(decay)
    one = [1.0 + 0.2 * decoded(info_ref, rec_ref, 2, l, 0) for l in range(layers)]
    two = [1.0 + 0.2 * decoded(info_ref, rec_ref, 1, l, 0) for l in range(layers)]
    lr = [lr_ref[layer] for layer in range(layers)]
    lr = [a - 0.3 * lt_ref[l] for l, a in enumerate(answered(one, lr, decay))]
    lr = [a - 0.3 * new_lt[l] for l, a in enumerate(answered(two, lr, decay))]
    _, later = chain(lr, decay, nothing)
    share = shares(decay, layers)
    by_zero = answered(two, answered(one, share, decay), decay)
    by_zero = [by_zero[l] - 0.3 * gate[l] * share[l] for l in range(layers)]
    _, one_weight = chain(answered(two, share, decay), decay, nothing)
    _, zero_weight = chain(by_zero, decay, nothing)
    halves(info_ref, (later, one_weight, zero_weight), scratch, keep_ref, give_ref)
    for l in range(layers):
        fields_ref[l] = 1.0 + 0.2 * decoded(info_ref, rec_ref, 0, l, 0)
        fields_ref[layers + l] = decoded(info_ref, rec_ref, 0, l, 1)


def beyond(there, here):
    middle = there[1:5]
    total = (there[0:4] + there[2:6]) + (there[8:12] + here[1:5]) + radial(middle)
    return middle + 0.15 * (total - 6.0 * middle) + there[12:16]


def pair_carry_body(
    keep_ref, got_ref, more_ref, more_got_ref, sums_ref, left_ref, right_ref,
    early_left_ref, early_right_ref, length_ref, mine_ref, other_ref, out_ref,
):
    info_ref = place()
    _, fall, cross = half_powers(info_ref, length_ref)
    _, side_fall, _ = side_powers(info_ref, early_left_ref, early_right_ref)
    chips = sums_ref.shape[0]
    per = fall.shape[0] // ROWS
    above = (jnp.zeros_like(fall),) * 3
    side = jnp.zeros_like(side_fall)
    for chip in reversed(range(1, chips)):
        inside = chip > info_ref[64] // 2
        tail = sums_ref[chip, 4 * per].astype(jnp.int32).astype(jnp.float32)
        here = [
            jnp.concatenate(
                [
                    unscaled(sums_ref[chip, per * index + block], tail[1 + index : 2 + index])
                    for block in range(per)
                ],
                axis=0,
            )
            for index in range(4)
        ]
        new = applied(above, here, fall * fall, 2.0 * fall * cross)
        above = tuple(jnp.where(inside, a, b) for a, b in zip(new, above))
        new = tail[0:1] * (jnp.exp2(tail[5:6]) * (1.0 / PLANE_TOP)) + side_fall * side_fall * side
        side = jnp.where(inside, new, side)
    upper, _ = cores(info_ref, keep_ref, got_ref)
    below = applied(above, upper, fall, cross)
    share_out(info_ref, above, below, mine_ref, other_ref)
    upper_here = info_ref[64] % 2 == 1
    below_side = side_fall * side + jnp.where(
        upper_here, keep_ref[4, 0:1, :], got_ref[12, 8:9, :]
    )
    mine_ref[3] = jnp.zeros_like(fall)
    other_ref[3] = jnp.zeros_like(fall)
    mine_ref[3, 0:1, :] = jnp.where(upper_here, side, below_side)
    other_ref[3, 0:1, :] = jnp.where(upper_here, below_side, side)
    upper, lower = cores(info_ref, more_ref, more_got_ref)
    upper = upper[0] + upper[1] * above[1] + upper[2] * above[0] + cross * above[2]
    lower = lower[0] + lower[1] * below[1] + lower[2] * below[0] + cross * below[2]
    end = length_ref.shape[0] - 1
    beside = jnp.where(upper_here, right_ref[...], left_ref[...])
    decay, _, _ = powers(jnp.where(upper_here, length_ref[end:, :], length_ref[0:1, :]))
    row = lax.broadcasted_iota(jnp.int32, fall.shape, 0)
    edge = row == jnp.where(upper_here, fall.shape[0] - 1, 0)
    weight = (-0.3 * 0.15) * (1.0 - decay)
    own, other = jnp.zeros_like(decay), jnp.zeros_like(decay)
    for layer in range(4):
        own = own + weight * beside[1 + layer : 2 + layer, :]
        other = other + weight * beside[16 + layer : 17 + layer, :]
        weight = weight * decay
    upper = upper + jnp.where(edge, jnp.where(upper_here, own, other), 0.0)
    lower = lower + jnp.where(edge, jnp.where(upper_here, other, own), 0.0)
    total = squeezed(lower + fall * upper, SUM_BASE, SUM_SCALE)
    upper = squeezed(upper, SUM_BASE, SUM_SCALE)
    for peer in range(out_ref.shape[0]):
        put_sum(out_ref, peer, 0, jnp.where(info_ref[64] // 2 == peer // 2, upper, total))


def third_body(
    info_ref, rec_ref, seed_ref, seed_lr_ref, one_ref, lt_ref, lr_ref, own_left_ref,
    own_right_ref, left_ref, right_ref, near_ref, beyond_ref, high_ref, early_left_ref,
    early_right_ref, length_ref, face_ref,
    mine_ref, got_ref, new_lt_ref, new_lr_ref, flux_ref, near_out, far_out, left_out, right_out,
    scratch,
):
    layers, azimuths, radials = lr_ref.shape
    decay, _, _ = powers(length_ref[...])
    zero, one, two = restored(info_ref, mine_ref, got_ref, scratch)
    upper_here = info_ref[64] % 2 == 1
    share = shares(decay, layers)
    lift = [share[l] * zero for l in range(layers)]
    seed_lr = [seed_lr_ref[layer] for layer in range(layers)]
    _, under = chain(seed_lr, decay, zero)
    over = (zero - (1.0 - decay) * high_ref[1]) / decay
    near = jnp.concatenate([near_ref[10], near_ref[11]], axis=0)
    gate_low = jnp.where(upper_here, near, beyond_ref[3])
    gate_high = jnp.where(upper_here, beyond_ref[3], near)
    lifts = [
        jnp.where(info_ref[64] == 0, 0.0, gate_low * under),
        *[decoded(info_ref, rec_ref, 2, l, 1) * lift[l] for l in range(layers)],
        jnp.where(info_ref[64] == info_ref[65] - 1, 0.0, gate_high * over),
    ]
    mine_side, got_side = mine_ref[3, 0:1, :], got_ref[3, 0:1, :]

    def lifted(there, early_ref, side):
        side_decay, _, _ = powers(early_ref[8:9, :])
        side_share = jnp.concatenate(shares(side_decay, layers), axis=0)
        return there[20:24] * side_share * side

    before = [one_ref[layer] for layer in range(layers)]
    left, right = left_ref[...], right_ref[...]
    row = lax.broadcasted_iota(jnp.int32, (azimuths, radials), 0)
    full = []
    for l in range(layers + 2):
        missing = jnp.where(
            row == 0,
            left[l : l + 1, :],
            jnp.where(row == azimuths - 1, right[l : l + 1, :], 0.0),
        )
        full.append(lt_ref[l] + 0.15 * missing + lifts[l])
    lt = full[1:-1]
    lr = [lr_ref[layer] + lift[layer] for layer in range(layers)]
    climbs, _ = chain(lr, decay, one)
    lr = [
        -0.3 * before[l]
        + (1.0 + 0.2 * decoded(info_ref, rec_ref, 2, l, 0)) * lr[l]
        + climbs[l]
        for l in range(layers)
    ]
    spread = laplace(
        lt,
        full[0],
        full[-1],
        beyond(left, own_left_ref[...])
        + lifted(left, early_left_ref, jnp.where(upper_here, got_side, mine_side)),
        beyond(right, own_right_ref[...])
        + lifted(right, early_right_ref, jnp.where(upper_here, mine_side, got_side)),
    )
    new_lt = [
        lt[l] + 0.15 * spread[l] + decoded(info_ref, rec_ref, 1, l, 1) * lr[l]
        for l in range(layers)
    ]
    upper_here = info_ref[64] % 2 == 1
    near_out[...] = jnp.where(upper_here, new_lt[0], new_lt[-1])
    far_out[...] = jnp.where(upper_here, new_lt[-1], new_lt[0])
    for l in range(layers):
        left_out[l : l + 1, :] = new_lt[l][0:1, :]
        right_out[l : l + 1, :] = new_lt[l][azimuths - 1 : azimuths, :]
    climbs, _ = chain(lr, decay, two)
    for l in range(layers):
        new_lt_ref[l] = new_lt[l]
        new_lr_ref[l] = (
            -0.3 * lt[l] + (1.0 + 0.2 * decoded(info_ref, rec_ref, 1, l, 0)) * lr[l] + climbs[l]
        )
    lane = lax.broadcasted_iota(jnp.int32, (azimuths, radials), 1)
    ones = jnp.ones((8, radials), jnp.float32)
    for l in range(layers):
        kept = jnp.where(
            lane == face_ref[l], (seed_ref[l] + before[l]) + (lt[l] + new_lt[l]), 0.0
        )
        line = lax.dot_general(
            ones,
            kept,
            (((1,), (1,)), ((), ())),
            precision=lax.Precision.HIGHEST,
            preferred_element_type=jnp.float32,
        )[0:1, :]
        twice = jnp.concatenate([line, line], axis=1)
        flux_ref[l : l + 1, :] = twice
        left_out[layers + l : layers + l + 1, :] = twice
        right_out[layers + l : layers + l + 1, :] = twice


def last_body(
    weight_ref, fields_ref, lt_ref, lr_ref, near_ref, far_ref, left_ref, right_ref,
    length_ref, sums_ref, flux_ref, new_lt_ref, new_lr_ref, heat_ref,
):
    info_ref = place()
    layers, azimuths, radials = lt_ref.shape
    band = weight_ref.shape[0] // 2
    decay, fall, _ = powers(length_ref[...])
    chips = sums_ref.shape[0] // 2
    here = info_ref[64] // 2

    per = sums_ref.shape[1]

    def total_of(chip):
        return jnp.concatenate(
            [got_sum(sums_ref, 2 * chip + core, 0, per) for core in range(2)], axis=0
        )

    above = jnp.zeros_like(fall)
    for chip in reversed(range(1, chips)):
        above = jnp.where(chip > here, fall * fall * above + total_of(chip), above)
    three = jnp.where(info_ref[64] % 2 == 1, above, fall * above + total_of(here))
    lt = [lt_ref[layer] for layer in range(layers)]
    lr = [lr_ref[layer] for layer in range(layers)]
    end = jnp.logical_or(info_ref[64] == 0, info_ref[64] == info_ref[65] - 1)
    near, far = near_ref[...], jnp.where(end, 0.0, far_ref[...])
    upper_here = info_ref[64] % 2 == 1
    low, high = jnp.where(upper_here, near, far), jnp.where(upper_here, far, near)
    spread = laplace(lt, low, high, left_ref[...], right_ref[...])
    climbs, _ = chain(lr, decay, three)
    for l in range(layers):
        new_lt_ref[l] = lt[l] + 0.15 * spread[l] + fields_ref[layers + l] * lr[l]
        new_lr_ref[l] = (
            -0.3 * lt[l]
            + fields_ref[l] * lr[l]
            + climbs[l]
        )
    lane = lax.broadcasted_iota(jnp.int32, (layers, radials), 1)
    ring = jnp.where(
        lane < azimuths,
        flux_ref[...],
        jnp.where(
            lane < azimuths + band,
            right_ref[layers : 2 * layers, :],
            left_ref[layers : 2 * layers, :],
        ),
    )
    heat = jnp.zeros_like(ring)
    for offset in range(-band, band + 1):
        heat = heat + weight_ref[offset + band : offset + band + 1, :] * pltpu.roll(ring, (-offset) % radials, axis=1)
    heat_ref[...] = heat[:, :azimuths]


def run(body, scalars, args, shapes, scratch=(), span=1):
    smem = pl.BlockSpec(memory_space=pltpu.SMEM)
    vmem = pl.BlockSpec(memory_space=pltpu.VMEM)
    return pl.pallas_call(
        body,
        in_specs=[smem] * len(scalars) + [vmem] * len(args),
        out_specs=[vmem] * len(shapes),
        out_shape=[
            jax.ShapeDtypeStruct(shape, jnp.int16 if len(shape) == 4 else jnp.float32)
            for shape in shapes
        ],
        scratch_shapes=[pltpu.VMEM(shape, jnp.float32) for shape in scratch],
        compiler_params=pltpu.CompilerParams(vmem_limit_bytes=STEP_VMEM),
        cost_estimate=pl.CostEstimate(
            flops=span * SPAN_FLOPS, bytes_accessed=span * SPAN_BYTES, transcendentals=0
        ),
    )(*scalars, *args)


def turned(value, axis, shift):
    count = lax.axis_size(axis)
    return lax.ppermute(value, axis, [(i, (i + shift) % count) for i in range(count)])


def swapped(value):
    return lax.ppermute(value, "axial", [(i, i ^ 1) for i in range(lax.axis_size("axial"))])


def crossed(value):
    axial = lax.axis_size("axial")
    return lax.ppermute(
        value, "axial", [(i, (i - 1 + 2 * (i % 2)) % axial) for i in range(axial)]
    )


def between_chips(value):
    axial = lax.axis_size("axial")
    groups = [list(range(core, axial, 2)) for core in range(2)]
    return lax.all_to_all(value, "axial", 0, 0, tiled=True, axis_index_groups=groups)


def local(stored, holder, seed_temp, seed_disloc, decay_length, face_radius, kernel):
    layers, azimuths, radials = seed_temp.shape
    axial, me = lax.axis_size("axial"), lax.axis_index("axial")
    wanted = lax.dynamic_index_in_dim(holder, me, 1, keepdims=False).reshape(-1)
    info = jnp.concatenate([wanted, jnp.stack([me, axial]).astype(jnp.int32)])
    weights = jnp.broadcast_to(kernel[:, None], (kernel.shape[0], radials))
    plane = (azimuths, radials)
    side = (layers, radials)
    wide = (2 * layers, radials)
    block = (layers, azimuths, radials)

    def half(count):
        return (count, azimuths // 2, radials)

    def copies(peers, count):
        return (peers, count * azimuths // (2 * ROWS), ROWS, radials)

    pieces = lax.all_to_all(encode(stored), "axial", 0, 0, tiled=True)

    def column(at):
        rows = [seed_temp[:, at], seed_disloc[:, at], decay_length[at : at + 1]]
        return jnp.pad(jnp.concatenate(rows, axis=0), ((0, 16 - 2 * layers - 1), (0, 0)))

    low = turned(seed_temp[layers - 1], "axial", 1)
    high = turned(jnp.stack([seed_temp[0], seed_disloc[0]]), "axial", -1)
    early = (turned(column(azimuths - 1), "azim", 1), turned(column(0), "azim", -1))
    face = face_radius[:, :, None]
    pieces, low, high, face, *early = lax.optimization_barrier(
        (pieces, low, high, face, *early)
    )
    lt1, lr1, source, far, keep, give = run(
        first_body,
        (info,),
        (pieces, seed_temp, seed_disloc, low, high, *early, decay_length),
        [block, block, block, (4, *plane), half(5), half(13)],
        [(4, *plane)],
    )
    got = swapped(give)
    far = crossed(far)
    (total,) = run(
        pair_chip_body,
        (),
        (keep, got, *early, decay_length),
        [(axial // 2, azimuths // ROWS * 2 + 1, ROWS, radials)],
        span=CHIP_SPAN,
    )
    sums = between_chips(total)
    lt2, left, right, more, give, fields = run(
        reach_body,
        (info,),
        (pieces, lt1, lr1, source, got, far, decay_length),
        [
            (layers + 2, *plane), (24, radials), (24, radials), half(3), half(3),
            (2 * layers, *plane),
        ],
        [(3, *plane)],
        span=REACH_SPAN,
    )
    more_got = swapped(give)
    sides = (turned(right, "azim", 1), turned(left, "azim", -1))
    sums, *sides = lax.optimization_barrier((sums, *sides))
    mine, other, total = run(
        pair_carry_body,
        (),
        (keep, got, more, more_got, sums, *sides, *early, decay_length),
        [half(4), half(4), copies(axial, 1)],
    )
    sums = lax.all_to_all(total, "axial", 0, 0, tiled=True)
    lt3, lr3, flux, near, far, left, right = run(
        third_body,
        (info,),
        (
            pieces, seed_temp, seed_disloc, lt1, lt2, lr1, left, right, *sides, got, far,
            high, *early, decay_length, face, mine, swapped(other),
        ),
        [block, block, side, plane, plane, wide, wide],
        [(3, *plane)],
        span=THIRD_SPAN,
    )
    halo = (
        swapped(near),
        crossed(far),
        turned(right, "azim", 1),
        turned(left, "azim", -1),
    )
    return tuple(
        run(
            last_body,
            (),
            (weights, fields, lt3, lr3, *halo, decay_length, sums, flux),
            [block, block, (layers, azimuths)],
        )
    )


def solution(mesh):
    in_specs = (
        P(None, "axial", "azim", None, None, None, None),
        P(),
        P("axial", "azim", None),
        P("axial", "azim", None),
        P("azim", None),
        P("axial", "azim"),
        P(),
    )
    out_specs = (P("axial", "azim", None), P("axial", "azim", None), P("axial", "azim"))
    return jax.shard_map(local, mesh=mesh, in_specs=in_specs, out_specs=out_specs, check_vma=False)
```

```python
import jax
import jax.numpy as jnp
from jax import lax
from jax.experimental import pallas as pl
from jax.experimental.pallas import tpu as pltpu
from jax.sharding import PartitionSpec as P

ROWS = 16
LANES = 128
RATE_MID = 3.7
RATE_SCALE = 10500.0
COEF_SCALE = 1374.0
COEF_BASE = 23.0
SUM_SCALE = 862.0
SUM_BASE = 29.0
PLANE_TOP = 32000.0
ENCODE_VMEM = 60 * 1024 * 1024
STEP_VMEM = 16 * 1024 * 1024
SPAN_FLOPS = 1_000_000_000
SPAN_BYTES = 3_000_000
CHIP_SPAN = 50
REACH_SPAN = 100
THIRD_SPAN = 100


def squeezed(value, base, scale):
    size = jnp.log2(jnp.maximum(jnp.abs(value), 2.0**-base))
    size = size * scale + (base * scale + 0.5)
    return jnp.where(value < 0.0, -size, size).astype(jnp.int32)


def spread_out(code, base, scale):
    code = code.astype(jnp.int32).astype(jnp.float32)
    size = jnp.exp2(jnp.abs(code) * (1.0 / scale) - base)
    return jnp.where(code > 0.0, size, jnp.where(code < 0.0, -size, 0.0))


def encode_body(stored_ref, out_ref, pieces, codes, in_sems, out_sems):
    steps, slots = stored_ref.shape[:2]
    cap = slots // out_ref.shape[0]
    rows = 8 * ROWS
    per = 2 * cap
    half_way = steps // 2
    cuts = [*range(half_way), half_way, steps]
    arrivals = {
        start: pltpu.make_async_copy(
            stored_ref.at[pl.ds(start, end - start)],
            pieces.at[pl.ds(start, end - start)],
            in_sems.at[start],
        )
        for start, end in zip(cuts[:-1], cuts[1:])
    }
    for copy in arrivals.values():
        copy.start()
    row = lax.broadcasted_iota(jnp.int32, (rows, rows), 0)
    column = lax.broadcasted_iota(jnp.int32, (rows, rows), 1)
    picked = (row % ROWS) * 8 + row // ROWS == column
    order = jnp.where(picked, 1.0, 0.0).astype(jnp.bfloat16)

    def mixed(step, slot):
        cells = pieces[step, slot].astype(jnp.float32)
        return jnp.concatenate(
            [cells[:, LANES * r : LANES * (r + 1)] for r in range(ROWS)], axis=0
        ).astype(jnp.bfloat16)

    departures = []

    def depart(start, count):
        copy = pltpu.make_async_copy(
            codes.at[:, pl.ds(start, count)],
            out_ref.at[:, pl.ds(start, count)],
            out_sems.at[len(departures)],
        )
        copy.start()
        departures.append(copy)

    for step in range(steps):
        if step in arrivals:
            arrivals[step].wait()
        for slot in range(0, slots, cap):
            both = jnp.concatenate([mixed(step, slot + c) for c in range(cap)], axis=1)
            parts = jnp.dot(order, both, preferred_element_type=jnp.float32)

            def part(index):
                return parts[ROWS * index : ROWS * (index + 1), :]

            squares = part(1) * part(1)
            for index in range(2, 7):
                squares = squares + part(index) * part(index)
            slope = jnp.tanh(part(0))
            total = 1.0 + squares * (1.0 / 6.0)
            rate = total * lax.rsqrt(total) * jnp.exp(0.5 * slope)
            coef = (0.1 * part(7)) * rate * (1.0 - slope * slope)
            coef_code = squeezed(coef, COEF_BASE, COEF_SCALE).astype(jnp.int16)
            rate_code = jnp.round((rate - RATE_MID) * RATE_SCALE)
            rate_code = rate_code.astype(jnp.int32).astype(jnp.int16)
            for c in range(cap):
                lanes = slice(LANES * c, LANES * (c + 1))
                codes[slot // cap, per * step + 2 * c] = rate_code[:, lanes]
                codes[slot // cap, per * step + 2 * c + 1] = coef_code[:, lanes]
        if step + 1 == half_way:
            depart(0, per * half_way)
    depart(per * half_way, out_ref.shape[1] - per * half_way)
    for copy in departures:
        copy.wait()


def encode(stored):
    steps, _, _, owners, cap, comps, cells = stored.shape
    flat = stored.reshape(steps, owners * cap, comps, cells)
    shape = (owners, steps * cap * 2, ROWS, LANES)
    return pl.pallas_call(
        encode_body,
        in_specs=[pl.BlockSpec(memory_space=pl.ANY)],
        out_specs=pl.BlockSpec(memory_space=pl.ANY),
        out_shape=jax.ShapeDtypeStruct(shape, jnp.int16),
        scratch_shapes=[
            pltpu.VMEM(flat.shape, jnp.bfloat16),
            pltpu.VMEM(shape, jnp.int16),
            pltpu.SemaphoreType.DMA((steps,)),
            pltpu.SemaphoreType.DMA((2,)),
        ],
        compiler_params=pltpu.CompilerParams(vmem_limit_bytes=ENCODE_VMEM),
    )(flat)


def taken(info_ref, rec_ref, step, piece, field):
    held = info_ref[16 * step + piece]
    return rec_ref[held // 2, 4 * step + 2 * (held % 2) + field]


def joined(codes, field):
    if field == 1:
        codes = [spread_out(code, COEF_BASE, COEF_SCALE) for code in codes]
    else:
        codes = [code.astype(jnp.int32).astype(jnp.float32) for code in codes]
        codes = [code * (1.0 / RATE_SCALE) + RATE_MID for code in codes]
    return jnp.concatenate(codes, axis=0)


def decoded(info_ref, rec_ref, step, layer, field):
    codes = [taken(info_ref, rec_ref, step, 4 * layer + q, field) for q in range(4)]
    return joined(codes, field)


def sorted_field(codes_ref, step, layer, field):
    codes = [codes_ref[2 * step + field, 4 * layer + q] for q in range(4)]
    return joined(codes, field)


def radial(x):
    lane = lax.broadcasted_iota(jnp.int32, x.shape, 1)
    inner = jnp.where(lane == 0, 0.0, pltpu.roll(x, 1, axis=1))
    outer = jnp.where(lane == x.shape[1] - 1, 0.0, pltpu.roll(x, x.shape[1] - 1, axis=1))
    return inner + outer


def laplace(field, low, high, left=None, right=None):
    layers = len(field)
    azimuths = field[0].shape[0]
    row = lax.broadcasted_iota(jnp.int32, field[0].shape, 0)
    out = []
    for layer in range(layers):
        x = field[layer]
        below = low if layer == 0 else field[layer - 1]
        above = high if layer == layers - 1 else field[layer + 1]
        first = 0.0 if left is None else left[layer : layer + 1, :]
        last = 0.0 if right is None else right[layer : layer + 1, :]
        before = jnp.where(row == 0, first, pltpu.roll(x, 1, axis=0))
        after = jnp.where(row == azimuths - 1, last, pltpu.roll(x, azimuths - 1, axis=0))
        out.append(((below + above) + (before + after)) + radial(x) - 6.0 * x)
    return out


def chain(field, decay, carry):
    layers = len(field)
    out = [None] * layers
    for layer in reversed(range(layers)):
        out[layer] = carry
        carry = decay * carry + (1.0 - decay) * field[layer]
    return out, carry


def powers(length):
    decay = jnp.exp(-1.0 / length)
    cube = decay * decay * decay
    return decay, decay * cube, 4.0 * (1.0 - decay) * cube


def place():
    return {64: lax.axis_index("axial"), 65: lax.axis_size("axial")}


def half_powers(info_ref, length_ref):
    half = length_ref.shape[0] // 2
    return powers(length_ref[pl.ds(half * (info_ref[64] % 2), half), :])


def halves(info_ref, values, scratch, keep_ref, give_ref):
    mine = info_ref[64] % 2
    half = scratch.shape[1] // 2
    for index, value in enumerate(values):
        scratch[index] = value
    for index in range(len(values)):
        keep_ref[index] = scratch[index, pl.ds(half * mine, half), :]
        give_ref[index] = scratch[index, pl.ds(half * (1 - mine), half), :]


def restored(info_ref, mine_ref, got_ref, scratch):
    mine = info_ref[64] % 2
    half = scratch.shape[1] // 2
    count = scratch.shape[0]
    for index in range(count):
        scratch[index, pl.ds(half * mine, half), :] = mine_ref[index]
        scratch[index, pl.ds(half * (1 - mine), half), :] = got_ref[index]
    return [scratch[index] for index in range(count)]


def cores(info_ref, keep_ref, got_ref):
    upper_here = info_ref[64] % 2 == 1
    own = [keep_ref[index] for index in range(min(4, keep_ref.shape[0]))]
    other = [got_ref[index] for index in range(len(own))]
    upper = [jnp.where(upper_here, a, b) for a, b in zip(own, other)]
    lower = [jnp.where(upper_here, b, a) for a, b in zip(own, other)]
    return upper, lower


def share_out(info_ref, upper, lower, mine_ref, other_ref):
    upper_here = info_ref[64] % 2 == 1
    for index, (a, b) in enumerate(zip(upper, lower)):
        mine_ref[index] = jnp.where(upper_here, a, b)
        other_ref[index] = jnp.where(upper_here, b, a)


def applied(carry, here, fall, cross):
    out = [sums + fall * value for value, sums in zip(carry, here)]
    if len(carry) > 1:
        out[1] = out[1] + cross * carry[0]
        out[2] = out[2] + cross * carry[1] + here[3] * carry[0]
    return tuple(out)


def scaled(value):
    top = jnp.max(jnp.max(jnp.abs(value), axis=1, keepdims=True), axis=0, keepdims=True)
    size = jnp.ceil(jnp.log2(jnp.maximum(top, 2.0**-100)))
    code = jnp.round(value * jnp.exp2(-size) * PLANE_TOP)
    return code.astype(jnp.int32), jnp.broadcast_to(size, (1, value.shape[1])).astype(jnp.int32)


def unscaled(code, size):
    return code.astype(jnp.int32).astype(jnp.float32) * (jnp.exp2(size) * (1.0 / PLANE_TOP))


def put_sum(out_ref, at, start, code):
    code = code.astype(jnp.int16)
    for block in range(code.shape[0] // ROWS):
        out_ref[at, start + block] = code[ROWS * block : ROWS * (block + 1), :]


def got_sum(sums_ref, at, start, count):
    code = [sums_ref[at, start + block] for block in range(count)]
    return jnp.concatenate([spread_out(part, SUM_BASE, SUM_SCALE) for part in code], axis=0)


def answered(gain, share, decay):
    climbs, _ = chain(share, decay, jnp.zeros_like(decay))
    return [g * s + c for g, s, c in zip(gain, share, climbs)]


def shares(decay, layers):
    out = [None] * layers
    power = jnp.ones_like(decay)
    for layer in reversed(range(layers)):
        out[layer] = power
        power = decay * power
    return out


def first_body(
    info_ref, rec_ref, lt_ref, lr_ref, low_ref, high_ref, left_ref, right_ref, length_ref,
    new_lt_ref, new_lr_ref, source_ref, far_ref, keep_ref, give_ref, scratch,
):
    layers = lt_ref.shape[0]
    decay, _, _ = powers(length_ref[...])
    nothing = jnp.zeros_like(decay)
    lt = [lt_ref[layer] for layer in range(layers)]
    lr = [lr_ref[layer] for layer in range(layers)]
    low = jnp.where(info_ref[64] == 0, 0.0, low_ref[...])
    high = jnp.where(info_ref[64] == info_ref[65] - 1, 0.0, high_ref[0])
    spread = laplace(lt, low, high, left_ref[0:layers, :], right_ref[0:layers, :])
    new_lt = [
        lt[l] + 0.15 * spread[l] + decoded(info_ref, rec_ref, 3, l, 1) * lr[l]
        for l in range(layers)
    ]
    climbs, begin = chain(lr, decay, nothing)
    base = [
        -0.3 * lt[l] + (1.0 + 0.2 * decoded(info_ref, rec_ref, 3, l, 0)) * lr[l]
        for l in range(layers)
    ]
    lr = [base[l] + climbs[l] for l in range(layers)]
    gate = [decoded(info_ref, rec_ref, 2, l, 1) for l in range(layers)]
    half = decay.shape[0] // 2
    up = (new_lt[-2], new_lt[-1], gate[-1] * base[-1], gate[-1])
    down = (new_lt[0], new_lt[1], gate[0] * base[0], gate[0])
    upper_here = info_ref[64] % 2 == 1
    for index in range(4):
        far_ref[index] = jnp.where(upper_here, up[index], down[index])
        near = jnp.where(upper_here, down[index], up[index])
        give_ref[4 + 2 * index] = near[:half]
        give_ref[5 + 2 * index] = near[half:]
    for l in range(layers):
        give_ref[12, l : l + 1, :] = new_lt[l][0:1, :]
        give_ref[12, layers + l : layers + l + 1, :] = new_lt[l][2 * half - 1 : 2 * half, :]
    beyond_sums = []
    for ref in (left_ref, right_ref):
        side_decay, _, _ = powers(ref[2 * layers : 2 * layers + 1, :])
        side = [ref[layers + l : layers + l + 1, :] for l in range(layers)]
        beyond_sums.append(chain(side, side_decay, jnp.zeros_like(side_decay))[1])
    keep_ref[4] = jnp.zeros_like(keep_ref[4])
    give_ref[12, 8:, :] = jnp.zeros_like(give_ref[12, 8:, :])
    keep_ref[4, 0:1, :] = jnp.where(upper_here, beyond_sums[1], beyond_sums[0])
    give_ref[12, 8:9, :] = jnp.where(upper_here, beyond_sums[0], beyond_sums[1])
    _, now = chain(lr, decay, nothing)
    gain = [1.0 + 0.2 * decoded(info_ref, rec_ref, 2, l, 0) for l in range(layers)]
    after = [a - 0.3 * new_lt[l] for l, a in enumerate(answered(gain, lr, decay))]
    _, later = chain(after, decay, nothing)
    _, weight = chain(answered(gain, shares(decay, layers), decay), decay, nothing)
    halves(info_ref, (begin, now, later, weight), scratch, keep_ref, give_ref)
    for l in range(layers):
        new_lt_ref[l] = new_lt[l]
        new_lr_ref[l] = lr[l]
        source_ref[l] = gate[l] * lr[l]


def side_powers(info_ref, early_left_ref, early_right_ref):
    upper_here = info_ref[64] % 2 == 1
    length = jnp.where(upper_here, early_right_ref[8:9, :], early_left_ref[8:9, :])
    return powers(length)


def pair_chip_body(
    keep_ref, got_ref, early_left_ref, early_right_ref, length_ref, out_ref,
):
    info_ref = place()
    _, fall, cross = half_powers(info_ref, length_ref)
    _, side_fall, _ = side_powers(info_ref, early_left_ref, early_right_ref)
    upper, lower = cores(info_ref, keep_ref, got_ref)
    total = list(applied(upper[:3], lower, fall, cross))
    total.append(fall * (lower[3] + upper[3]) + cross * cross)
    upper_here = info_ref[64] % 2 == 1
    own, other = keep_ref[4, 0:1, :], got_ref[12, 8:9, :]
    side = jnp.where(upper_here, other, own) + side_fall * jnp.where(upper_here, own, other)
    codes, sizes = zip(*[scaled(value) for value in [*total, side]])
    filler = jnp.zeros((ROWS - 1 - len(sizes), side.shape[1]), jnp.int32)
    last = jnp.concatenate([codes[-1], *sizes, filler], axis=0)
    for chip in range(out_ref.shape[0]):
        start = 0
        for code in (*codes[:-1], last):
            put_sum(out_ref, chip, start, code)
            start += code.shape[0] // ROWS


def reach_body(
    info_ref, rec_ref, lt_ref, lr_ref, source_ref, near_ref, far_ref, length_ref,
    new_lt_ref, left_out, right_out, keep_ref, give_ref, fields_ref, scratch,
):
    layers, azimuths, _ = lt_ref.shape
    bottom = info_ref[64] == 0
    top = info_ref[64] == info_ref[65] - 1
    upper_here = info_ref[64] % 2 == 1
    low, high = [], []
    for index in range(3):
        near = jnp.concatenate([near_ref[4 + 2 * index], near_ref[5 + 2 * index]], axis=0)
        far = jnp.where(jnp.logical_or(bottom, top), 0.0, far_ref[index])
        low.append(jnp.where(upper_here, near, far))
        high.append(jnp.where(upper_here, far, near))
    lt = [low[1], *[lt_ref[l] for l in range(layers)], high[0]]
    source = [low[2], *[source_ref[l] for l in range(layers)], high[2]]
    spread = laplace(lt, low[0], high[1])
    new_lt = [lt[l] + 0.15 * spread[l] + source[l] for l in range(layers + 2)]
    new_lt[0] = jnp.where(bottom, 0.0, new_lt[0])
    new_lt[-1] = jnp.where(top, 0.0, new_lt[-1])
    gate = [decoded(info_ref, rec_ref, 2, l, 1) for l in range(layers)]
    sides = ((left_out, 0, 1, 0), (right_out, azimuths - 1, azimuths - 2, layers))
    for out, edge, inside, other in sides:
        for l in range(layers + 2):
            out[l : l + 1, :] = lt[l][edge : edge + 1, :]
        out[layers + 2 : layers + 4, :] = jnp.zeros_like(out[layers + 2 : layers + 4, :])
        for l in range(layers):
            out[8 + l : 9 + l, :] = lt[l + 1][inside : inside + 1, :]
            out[12 + l : 13 + l, :] = source[l + 1][edge : edge + 1, :]
            out[20 + l : 21 + l, :] = gate[l][edge : edge + 1, :]
        out[16:20, :] = near_ref[12, other : other + layers, :]
    for l in range(layers + 2):
        new_lt_ref[l] = new_lt[l]
    new_lt = new_lt[1:-1]
    decay, _, _ = powers(length_ref[...])
    nothing = jnp.zeros_like(decay)
    one = [1.0 + 0.2 * decoded(info_ref, rec_ref, 2, l, 0) for l in range(layers)]
    two = [1.0 + 0.2 * decoded(info_ref, rec_ref, 1, l, 0) for l in range(layers)]
    lr = [lr_ref[layer] for layer in range(layers)]
    lr = [a - 0.3 * lt_ref[l] for l, a in enumerate(answered(one, lr, decay))]
    lr = [a - 0.3 * new_lt[l] for l, a in enumerate(answered(two, lr, decay))]
    _, later = chain(lr, decay, nothing)
    share = shares(decay, layers)
    by_zero = answered(two, answered(one, share, decay), decay)
    by_zero = [by_zero[l] - 0.3 * gate[l] * share[l] for l in range(layers)]
    _, one_weight = chain(answered(two, share, decay), decay, nothing)
    _, zero_weight = chain(by_zero, decay, nothing)
    halves(info_ref, (later, one_weight, zero_weight), scratch, keep_ref, give_ref)
    for step in range(3):
        for field in range(2):
            for piece in range(16):
                fields_ref[2 * step + field, piece] = taken(
                    info_ref, rec_ref, step, piece, field
                )


def beyond(there, here):
    middle = there[1:5]
    total = (there[0:4] + there[2:6]) + (there[8:12] + here[1:5]) + radial(middle)
    return middle + 0.15 * (total - 6.0 * middle) + there[12:16]


def pair_carry_body(
    keep_ref, got_ref, more_ref, more_got_ref, sums_ref, left_ref, right_ref,
    early_left_ref, early_right_ref, length_ref, mine_ref, other_ref, out_ref,
):
    info_ref = place()
    _, fall, cross = half_powers(info_ref, length_ref)
    _, side_fall, _ = side_powers(info_ref, early_left_ref, early_right_ref)
    chips = sums_ref.shape[0]
    per = fall.shape[0] // ROWS
    above = (jnp.zeros_like(fall),) * 3
    side = jnp.zeros_like(side_fall)
    for chip in reversed(range(1, chips)):
        inside = chip > info_ref[64] // 2
        tail = sums_ref[chip, 4 * per].astype(jnp.int32).astype(jnp.float32)
        here = [
            jnp.concatenate(
                [
                    unscaled(sums_ref[chip, per * index + block], tail[1 + index : 2 + index])
                    for block in range(per)
                ],
                axis=0,
            )
            for index in range(4)
        ]
        new = applied(above, here, fall * fall, 2.0 * fall * cross)
        above = tuple(jnp.where(inside, a, b) for a, b in zip(new, above))
        new = tail[0:1] * (jnp.exp2(tail[5:6]) * (1.0 / PLANE_TOP)) + side_fall * side_fall * side
        side = jnp.where(inside, new, side)
    upper, _ = cores(info_ref, keep_ref, got_ref)
    below = applied(above, upper, fall, cross)
    share_out(info_ref, above, below, mine_ref, other_ref)
    upper_here = info_ref[64] % 2 == 1
    below_side = side_fall * side + jnp.where(
        upper_here, keep_ref[4, 0:1, :], got_ref[12, 8:9, :]
    )
    mine_ref[3] = jnp.zeros_like(fall)
    other_ref[3] = jnp.zeros_like(fall)
    mine_ref[3, 0:1, :] = jnp.where(upper_here, side, below_side)
    other_ref[3, 0:1, :] = jnp.where(upper_here, below_side, side)
    upper, lower = cores(info_ref, more_ref, more_got_ref)
    upper = upper[0] + upper[1] * above[1] + upper[2] * above[0] + cross * above[2]
    lower = lower[0] + lower[1] * below[1] + lower[2] * below[0] + cross * below[2]
    end = length_ref.shape[0] - 1
    beside = jnp.where(upper_here, right_ref[...], left_ref[...])
    decay, _, _ = powers(jnp.where(upper_here, length_ref[end:, :], length_ref[0:1, :]))
    row = lax.broadcasted_iota(jnp.int32, fall.shape, 0)
    edge = row == jnp.where(upper_here, fall.shape[0] - 1, 0)
    weight = (-0.3 * 0.15) * (1.0 - decay)
    own, other = jnp.zeros_like(decay), jnp.zeros_like(decay)
    for layer in range(4):
        own = own + weight * beside[1 + layer : 2 + layer, :]
        other = other + weight * beside[16 + layer : 17 + layer, :]
        weight = weight * decay
    upper = upper + jnp.where(edge, jnp.where(upper_here, own, other), 0.0)
    lower = lower + jnp.where(edge, jnp.where(upper_here, other, own), 0.0)
    total = squeezed(lower + fall * upper, SUM_BASE, SUM_SCALE)
    upper = squeezed(upper, SUM_BASE, SUM_SCALE)
    for peer in range(out_ref.shape[0]):
        put_sum(out_ref, peer, 0, jnp.where(info_ref[64] // 2 == peer // 2, upper, total))


def third_body(
    fields_ref, seed_ref, seed_lr_ref, one_ref, lt_ref, lr_ref, own_left_ref,
    own_right_ref, left_ref, right_ref, near_ref, beyond_ref, high_ref, early_left_ref,
    early_right_ref, length_ref, face_ref,
    mine_ref, got_ref, new_lt_ref, new_lr_ref, flux_ref, near_out, far_out, left_out, right_out,
    scratch,
):
    info_ref = place()
    layers, azimuths, radials = lr_ref.shape
    decay, _, _ = powers(length_ref[...])
    zero, one, two = restored(info_ref, mine_ref, got_ref, scratch)
    upper_here = info_ref[64] % 2 == 1
    share = shares(decay, layers)
    lift = [share[l] * zero for l in range(layers)]
    seed_lr = [seed_lr_ref[layer] for layer in range(layers)]
    _, under = chain(seed_lr, decay, zero)
    over = (zero - (1.0 - decay) * high_ref[1]) / decay
    near = jnp.concatenate([near_ref[10], near_ref[11]], axis=0)
    gate_low = jnp.where(upper_here, near, beyond_ref[3])
    gate_high = jnp.where(upper_here, beyond_ref[3], near)
    lifts = [
        jnp.where(info_ref[64] == 0, 0.0, gate_low * under),
        *[sorted_field(fields_ref, 2, l, 1) * lift[l] for l in range(layers)],
        jnp.where(info_ref[64] == info_ref[65] - 1, 0.0, gate_high * over),
    ]
    mine_side, got_side = mine_ref[3, 0:1, :], got_ref[3, 0:1, :]

    def lifted(there, early_ref, side):
        side_decay, _, _ = powers(early_ref[8:9, :])
        side_share = jnp.concatenate(shares(side_decay, layers), axis=0)
        return there[20:24] * side_share * side

    before = [one_ref[layer] for layer in range(layers)]
    left, right = left_ref[...], right_ref[...]
    row = lax.broadcasted_iota(jnp.int32, (azimuths, radials), 0)
    full = []
    for l in range(layers + 2):
        missing = jnp.where(
            row == 0,
            left[l : l + 1, :],
            jnp.where(row == azimuths - 1, right[l : l + 1, :], 0.0),
        )
        full.append(lt_ref[l] + 0.15 * missing + lifts[l])
    lt = full[1:-1]
    lr = [lr_ref[layer] + lift[layer] for layer in range(layers)]
    climbs, _ = chain(lr, decay, one)
    lr = [
        -0.3 * before[l]
        + (1.0 + 0.2 * sorted_field(fields_ref, 2, l, 0)) * lr[l]
        + climbs[l]
        for l in range(layers)
    ]
    spread = laplace(
        lt,
        full[0],
        full[-1],
        beyond(left, own_left_ref[...])
        + lifted(left, early_left_ref, jnp.where(upper_here, got_side, mine_side)),
        beyond(right, own_right_ref[...])
        + lifted(right, early_right_ref, jnp.where(upper_here, mine_side, got_side)),
    )
    new_lt = [
        lt[l] + 0.15 * spread[l] + sorted_field(fields_ref, 1, l, 1) * lr[l]
        for l in range(layers)
    ]
    upper_here = info_ref[64] % 2 == 1
    near_out[...] = jnp.where(upper_here, new_lt[0], new_lt[-1])
    far_out[...] = jnp.where(upper_here, new_lt[-1], new_lt[0])
    for l in range(layers):
        left_out[l : l + 1, :] = new_lt[l][0:1, :]
        right_out[l : l + 1, :] = new_lt[l][azimuths - 1 : azimuths, :]
    climbs, _ = chain(lr, decay, two)
    for l in range(layers):
        new_lt_ref[l] = new_lt[l]
        new_lr_ref[l] = (
            -0.3 * lt[l] + (1.0 + 0.2 * sorted_field(fields_ref, 1, l, 0)) * lr[l] + climbs[l]
        )
    lane = lax.broadcasted_iota(jnp.int32, (azimuths, radials), 1)
    ones = jnp.ones((8, radials), jnp.float32)
    for l in range(layers):
        kept = jnp.where(
            lane == face_ref[l], (seed_ref[l] + before[l]) + (lt[l] + new_lt[l]), 0.0
        )
        line = lax.dot_general(
            ones,
            kept,
            (((1,), (1,)), ((), ())),
            precision=lax.Precision.HIGHEST,
            preferred_element_type=jnp.float32,
        )[0:1, :]
        twice = jnp.concatenate([line, line], axis=1)
        flux_ref[l : l + 1, :] = twice
        left_out[layers + l : layers + l + 1, :] = twice
        right_out[layers + l : layers + l + 1, :] = twice


def last_body(
    weight_ref, fields_ref, lt_ref, lr_ref, near_ref, far_ref, left_ref, right_ref,
    length_ref, sums_ref, flux_ref, new_lt_ref, new_lr_ref, heat_ref,
):
    info_ref = place()
    layers, azimuths, radials = lt_ref.shape
    band = weight_ref.shape[0] // 2
    decay, fall, _ = powers(length_ref[...])
    chips = sums_ref.shape[0] // 2
    here = info_ref[64] // 2

    per = sums_ref.shape[1]

    def total_of(chip):
        return jnp.concatenate(
            [got_sum(sums_ref, 2 * chip + core, 0, per) for core in range(2)], axis=0
        )

    above = jnp.zeros_like(fall)
    for chip in reversed(range(1, chips)):
        above = jnp.where(chip > here, fall * fall * above + total_of(chip), above)
    three = jnp.where(info_ref[64] % 2 == 1, above, fall * above + total_of(here))
    lt = [lt_ref[layer] for layer in range(layers)]
    lr = [lr_ref[layer] for layer in range(layers)]
    end = jnp.logical_or(info_ref[64] == 0, info_ref[64] == info_ref[65] - 1)
    near, far = near_ref[...], jnp.where(end, 0.0, far_ref[...])
    upper_here = info_ref[64] % 2 == 1
    low, high = jnp.where(upper_here, near, far), jnp.where(upper_here, far, near)
    spread = laplace(lt, low, high, left_ref[...], right_ref[...])
    climbs, _ = chain(lr, decay, three)
    for l in range(layers):
        new_lt_ref[l] = lt[l] + 0.15 * spread[l] + sorted_field(fields_ref, 0, l, 1) * lr[l]
        new_lr_ref[l] = (
            -0.3 * lt[l]
            + (1.0 + 0.2 * sorted_field(fields_ref, 0, l, 0)) * lr[l]
            + climbs[l]
        )
    lane = lax.broadcasted_iota(jnp.int32, (layers, radials), 1)
    ring = jnp.where(
        lane < azimuths,
        flux_ref[...],
        jnp.where(
            lane < azimuths + band,
            right_ref[layers : 2 * layers, :],
            left_ref[layers : 2 * layers, :],
        ),
    )
    heat = jnp.zeros_like(ring)
    for offset in range(-band, band + 1):
        heat = heat + weight_ref[offset + band : offset + band + 1, :] * pltpu.roll(ring, (-offset) % radials, axis=1)
    heat_ref[...] = heat[:, :azimuths]


def run(body, scalars, args, shapes, scratch=(), span=1):
    smem = pl.BlockSpec(memory_space=pltpu.SMEM)
    vmem = pl.BlockSpec(memory_space=pltpu.VMEM)
    return pl.pallas_call(
        body,
        in_specs=[smem] * len(scalars) + [vmem] * len(args),
        out_specs=[vmem] * len(shapes),
        out_shape=[
            jax.ShapeDtypeStruct(shape, jnp.int16 if len(shape) == 4 else jnp.float32)
            for shape in shapes
        ],
        scratch_shapes=[pltpu.VMEM(shape, jnp.float32) for shape in scratch],
        compiler_params=pltpu.CompilerParams(vmem_limit_bytes=STEP_VMEM),
        cost_estimate=pl.CostEstimate(
            flops=span * SPAN_FLOPS, bytes_accessed=span * SPAN_BYTES, transcendentals=0
        ),
    )(*scalars, *args)


def turned(value, axis, shift):
    count = lax.axis_size(axis)
    return lax.ppermute(value, axis, [(i, (i + shift) % count) for i in range(count)])


def swapped(value):
    return lax.ppermute(value, "axial", [(i, i ^ 1) for i in range(lax.axis_size("axial"))])


def crossed(value):
    axial = lax.axis_size("axial")
    return lax.ppermute(
        value, "axial", [(i, (i - 1 + 2 * (i % 2)) % axial) for i in range(axial)]
    )


def between_chips(value):
    axial = lax.axis_size("axial")
    groups = [list(range(core, axial, 2)) for core in range(2)]
    return lax.all_to_all(value, "axial", 0, 0, tiled=True, axis_index_groups=groups)


def local(stored, holder, seed_temp, seed_disloc, decay_length, face_radius, kernel):
    layers, azimuths, radials = seed_temp.shape
    axial, me = lax.axis_size("axial"), lax.axis_index("axial")
    wanted = lax.dynamic_index_in_dim(holder, me, 1, keepdims=False).reshape(-1)
    info = jnp.concatenate([wanted, jnp.stack([me, axial]).astype(jnp.int32)])
    weights = jnp.broadcast_to(kernel[:, None], (kernel.shape[0], radials))
    plane = (azimuths, radials)
    side = (layers, radials)
    wide = (2 * layers, radials)
    block = (layers, azimuths, radials)

    def half(count):
        return (count, azimuths // 2, radials)

    def copies(peers, count):
        return (peers, count * azimuths // (2 * ROWS), ROWS, radials)

    pieces = lax.all_to_all(encode(stored), "axial", 0, 0, tiled=True)

    def column(at):
        rows = [seed_temp[:, at], seed_disloc[:, at], decay_length[at : at + 1]]
        return jnp.pad(jnp.concatenate(rows, axis=0), ((0, 16 - 2 * layers - 1), (0, 0)))

    low = turned(seed_temp[layers - 1], "axial", 1)
    high = turned(jnp.stack([seed_temp[0], seed_disloc[0]]), "axial", -1)
    early = (turned(column(azimuths - 1), "azim", 1), turned(column(0), "azim", -1))
    face = face_radius[:, :, None]
    pieces, low, high, face, *early = lax.optimization_barrier(
        (pieces, low, high, face, *early)
    )
    lt1, lr1, source, far, keep, give = run(
        first_body,
        (info,),
        (pieces, seed_temp, seed_disloc, low, high, *early, decay_length),
        [block, block, block, (4, *plane), half(5), half(13)],
        [(4, *plane)],
    )
    got = swapped(give)
    far = crossed(far)
    (total,) = run(
        pair_chip_body,
        (),
        (keep, got, *early, decay_length),
        [(axial // 2, azimuths // ROWS * 2 + 1, ROWS, radials)],
        span=CHIP_SPAN,
    )
    sums = between_chips(total)
    lt2, left, right, more, give, fields = run(
        reach_body,
        (info,),
        (pieces, lt1, lr1, source, got, far, decay_length),
        [
            (layers + 2, *plane), (24, radials), (24, radials), half(3), half(3),
            (6, 4 * layers, ROWS, radials),
        ],
        [(3, *plane)],
        span=REACH_SPAN,
    )
    more_got = swapped(give)
    sides = (turned(right, "azim", 1), turned(left, "azim", -1))
    sums, *sides = lax.optimization_barrier((sums, *sides))
    mine, other, total = run(
        pair_carry_body,
        (),
        (keep, got, more, more_got, sums, *sides, *early, decay_length),
        [half(4), half(4), copies(axial, 1)],
    )
    sums = lax.all_to_all(total, "axial", 0, 0, tiled=True)
    lt3, lr3, flux, near, far, left, right = run(
        third_body,
        (),
        (
            fields, seed_temp, seed_disloc, lt1, lt2, lr1, left, right, *sides, got, far,
            high, *early, decay_length, face, mine, swapped(other),
        ),
        [block, block, side, plane, plane, wide, wide],
        [(3, *plane)],
        span=THIRD_SPAN,
    )
    halo = (
        swapped(near),
        crossed(far),
        turned(right, "azim", 1),
        turned(left, "azim", -1),
    )
    return tuple(
        run(
            last_body,
            (),
            (weights, fields, lt3, lr3, *halo, decay_length, sums, flux),
            [block, block, (layers, azimuths)],
        )
    )


def solution(mesh):
    in_specs = (
        P(None, "axial", "azim", None, None, None, None),
        P(),
        P("axial", "azim", None),
        P("axial", "azim", None),
        P("azim", None),
        P("axial", "azim"),
        P(),
    )
    out_specs = (P("axial", "azim", None), P("axial", "azim", None), P("axial", "azim"))
    return jax.shard_map(local, mesh=mesh, in_specs=in_specs, out_specs=out_specs, check_vma=False)
```
